32 devices in a mesh: seq: 16 (over z, x, core), tp: 2 (over y).
Axes of the slice: x: 2, y: 2, z: 4, core: 2. Of those that a mesh axis runs over, the one named last changes fastest.
Arguments:
- layer_input: bfloat16 [4608, 896], P('seq'), may hold values from -6 to 6
- block_order: int32 [32], replicated, may hold values from 0 to 31, each once
- attn_gain: float32 [896], replicated, may hold values from 0.5 to 1.5
- query_weight: bfloat16 [896, 896], P(None, 'tp'), may hold values from -0.1875 to 0.1875
- query_bias: float32 [896], P('tp'), may hold values from -3 to 3
- key_weight: bfloat16 [896, 128], P(None, 'tp'), may hold values from -0.1875 to 0.1875
- key_bias: float32 [128], P('tp'), may hold values from -3 to 3
- value_weight: bfloat16 [896, 128], P(None, 'tp'), may hold values from -0.1875 to 0.1875
- value_bias: float32 [128], P('tp'), may hold values from -1.2 to 1.2
- out_weight: bfloat16 [896, 896], P('tp'), may hold values from -1.5 to 1.5
- mlp_gain: float32 [896], replicated, may hold values from 0.5 to 1.5
- gate_weight: bfloat16 [896, 4864], P(None, 'tp'), may hold values from -0.1875 to 0.1875
- up_weight: bfloat16 [896, 4864], P(None, 'tp'), may hold values from -0.1875 to 0.1875
- down_weight: bfloat16 [4864, 896], P('tp'), may hold values from -0.078125 to 0.078125
- out_cotangent: bfloat16 [4608, 896], P('seq'), may hold values from -6 to 6
Outputs:
- layer_output: bfloat16 [4608, 896], P('seq')
- input_grad: bfloat16 [4608, 896], P('seq')
- attn_gain_grad: float32 [896], replicated
- query_weight_grad: float32 [896, 896], P(None, 'tp')
- query_bias_grad: float32 [896], P('tp')
- key_weight_grad: float32 [896, 128], P(None, 'tp')
- key_bias_grad: float32 [128], P('tp')
- value_weight_grad: float32 [896, 128], P(None, 'tp')
- value_bias_grad: float32 [128], P('tp')
- out_weight_grad: float32 [896, 896], P('tp')
- mlp_gain_grad: float32 [896], replicated
- gate_weight_grad: float32 [896, 4864], P(None, 'tp')
- up_weight_grad: float32 [896, 4864], P(None, 'tp')
- down_weight_grad: float32 [4864, 896], P('tp')
The draws below stay inside these ranges and needn't reach their ends.
Inputs may be any that keep to these rules, and one draw needn't show every extreme that they name: `block_order`: A permutation: each of the 32 blocks of 144 consecutive positions stands in exactly one slot.
All inputs are finite; a program needn't handle non-finite values.
Results may differ from the reference program's by a relative error of at most 0.03.
Values may be sent and summed in bfloat16 or wider, within the bound.
A program may use at most 192 MiB of HBM per device.

```python
import jax
import jax.numpy as jnp
from jax import lax

D = 896
HEADS = 14
KV_HEADS = 2
HEAD_DIM = 64
FF = 4864
BLOCKS = 32
TOKENS = 4608


def steps_of(own_key, shape, pieces, low, high):
    factor_of, own = 1.0, jax.random.fold_in(own_key, 6)
    for dim, blocks in pieces:
        draws = jnp.exp(jax.random.uniform(jax.random.fold_in(own, dim), (blocks,), jnp.float32, low / len(pieces), high / len(pieces)))
        factor_of = factor_of * jnp.repeat(draws, shape[dim] // blocks).reshape([-1 if axis == dim else 1 for axis in range(len(shape))])
    return factor_of


def normal_values(rng, dims, spread, most, shards=(), kind=jnp.bfloat16):
    loudness = steps_of(rng, dims, shards, -0.22, 0.18) if shards else 1.0
    array = jax.random.normal(rng, dims, jnp.float32) * spread * loudness
    return jnp.minimum(jnp.maximum(array, -most), most).astype(kind)


def setup_inputs(seed: int = 0) -> dict:
    splits = jax.random.split(jax.random.key(seed), 16)
    return {
        "layer_input": normal_values(splits[0], (TOKENS, D), 1.0, 6.0, ((0, 16),)),
        "block_order": jax.random.permutation(splits[1], BLOCKS).astype(jnp.int32),
        "attn_gain": jnp.clip(1.0 + 0.1 * jax.random.normal(splits[2], (D,), jnp.float32), 0.5, 1.5),
        "query_weight": normal_values(splits[3], (D, HEADS * HEAD_DIM), D ** -0.5, 0.1875, ((1, 2),)),
        "query_bias": normal_values(splits[4], (HEADS * HEAD_DIM,), 0.5, 3.0, ((0, 2),), jnp.float32),
        "key_weight": normal_values(splits[5], (D, KV_HEADS * HEAD_DIM), D ** -0.5, 0.1875, ((1, 2),)),
        "key_bias": normal_values(splits[6], (KV_HEADS * HEAD_DIM,), 0.5, 3.0, ((0, 2),), jnp.float32),
        "value_weight": normal_values(splits[7], (D, KV_HEADS * HEAD_DIM), D ** -0.5, 0.1875, ((1, 2),)),
        "value_bias": normal_values(splits[8], (KV_HEADS * HEAD_DIM,), 0.2, 1.2, ((0, 2),), jnp.float32),
        "out_weight": normal_values(splits[9], (HEADS * HEAD_DIM, D), (max(1, HEADS * HEAD_DIM // 64)) ** -0.5, 1.5, ((0, 2),)),
        "mlp_gain": jnp.clip(1.0 + 0.1 * jax.random.normal(splits[10], (D,), jnp.float32), 0.5, 1.5),
        "gate_weight": normal_values(splits[11], (D, FF), D ** -0.5, 0.1875, ((1, 2),)),
        "up_weight": normal_values(splits[12], (D, FF), D ** -0.5, 0.1875, ((1, 2),)),
        "down_weight": normal_values(splits[13], (FF, D), FF ** -0.5, 0.078125, ((0, 2),)),
        "out_cotangent": normal_values(splits[14], (TOKENS, D), 1.0, 6.0, ((0, 16),)),
    }


EPSILON = 1e-06
NEGATIVE = -1e+30
ROPE_BASE = 1000000.0
PRECISION = lax.Precision.HIGHEST

@jax.custom_vjp
def low(v):
    return lax.optimization_barrier(v.astype(jnp.bfloat16)).astype(jnp.float32)

@jax.custom_vjp
def low_back(v):
    return v

def low_keep(v):
    return (low(v), None)

def low_pass(kept, grad):
    return (grad,)

def back_keep(v):
    return (v, None)

def back_low(kept, grad):
    return (low(grad),)
low.defvjp(low_keep, low_pass)
low_back.defvjp(back_keep, back_low)

def pick_block(total, largest):
    chosen = 1
    for candidate in range(1, min(total, largest) + 1):
        if total % candidate == 0:
            chosen = candidate
    return chosen

def rope_tables(positions, head_size):
    half_size = head_size // 2
    exponent = jnp.arange(half_size, dtype=jnp.float32) * (2.0 / head_size)
    frequency = jnp.power(ROPE_BASE, -exponent)
    angle = positions.astype(jnp.float32)[:, None] * frequency[None, :]
    return (jnp.cos(angle)[:, None, :], jnp.sin(angle)[:, None, :])

def rotate(values, cosine, sine):
    half_size = values.shape[-1] // 2
    first = values[..., :half_size]
    second = values[..., half_size:]
    return jnp.concatenate([first * cosine - second * sine, second * cosine + first * sine], axis=-1)

def rms_scale(values, gain):
    factor = lax.rsqrt(lax.optimization_barrier(jnp.mean(values * values, axis=-1, keepdims=True)) + EPSILON)
    return values * factor * gain

def matmul(left, right):
    return jnp.dot(left, right, precision=PRECISION)

def reference(layer_input, block_order, attn_gain, query_weight, query_bias, key_weight, key_bias, value_weight, value_bias, out_weight, mlp_gain, gate_weight, up_weight, down_weight, out_cotangent):
    row_count = layer_input.shape[0]
    block_rows = row_count // BLOCKS
    steps_in = jnp.arange(block_rows, dtype=jnp.int32)
    positions = (block_order.astype(jnp.int32)[:, None] * block_rows + steps_in[None, :]).reshape(-1)
    cosine, sine = rope_tables(positions, HEAD_DIM)
    group_size = HEADS // KV_HEADS
    score_scale = HEAD_DIM ** (-0.5)
    query_block = pick_block(row_count, 256)
    mlp_block = pick_block(row_count, 4096)

    def forward(inputs, gain_first, weight_query, bias_query, weight_key, bias_key, weight_value, bias_value, weight_out, gain_second, weight_gate, weight_up, weight_down):
        normed_attn = low(rms_scale(inputs, gain_first))
        query_rows = low_back(matmul(normed_attn, weight_query) + bias_query).reshape(row_count, HEADS, HEAD_DIM)
        key_rows = low_back(matmul(normed_attn, weight_key) + bias_key).reshape(row_count, KV_HEADS, HEAD_DIM)
        value_rows = low_back(low(matmul(normed_attn, weight_value) + bias_value)).reshape(row_count, KV_HEADS, HEAD_DIM)
        query_rot = low(rotate(query_rows, cosine, sine)).reshape(row_count // query_block, query_block, KV_HEADS, group_size, HEAD_DIM)
        key_rot = low(rotate(key_rows, cosine, sine))
        place_blocks = positions.reshape(-1, query_block)

        def attend(pair):
            query_part, place_part = pair
            scores = jnp.einsum('qcgd,kcd->cgqk', query_part, key_rot, precision=PRECISION) * score_scale
            scores = low_back(scores)
            visible = positions[None, :] <= place_part[:, None]
            probs = low(jax.nn.softmax(jnp.where(visible, scores, NEGATIVE), axis=-1))
            return jnp.einsum('cgqk,kcd->qcgd', probs, value_rows, precision=PRECISION)
        attention = lax.map(jax.checkpoint(attend), (query_rot, place_blocks)).reshape(row_count, HEADS * HEAD_DIM)
        attention_low = low_back(low(attention))
        resid = inputs + low_back(matmul(attention_low, weight_out))
        normed_mlp = low(rms_scale(resid, gain_second))

        def feed(part):
            gate = low_back(matmul(part, weight_gate))
            upward = low_back(matmul(part, weight_up))
            mixed = low(jax.nn.silu(gate) * upward)
            return low_back(matmul(mixed, weight_down))
        branch = lax.map(jax.checkpoint(feed), normed_mlp.reshape(row_count // mlp_block, mlp_block, normed_mlp.shape[1]))
        return resid + branch.reshape(row_count, normed_mlp.shape[1])
    floats = (layer_input.astype(jnp.float32), attn_gain.astype(jnp.float32), query_weight.astype(jnp.float32), query_bias.astype(jnp.float32), key_weight.astype(jnp.float32), key_bias.astype(jnp.float32), value_weight.astype(jnp.float32), value_bias.astype(jnp.float32), out_weight.astype(jnp.float32), mlp_gain.astype(jnp.float32), gate_weight.astype(jnp.float32), up_weight.astype(jnp.float32), down_weight.astype(jnp.float32))
    output, pullback = jax.vjp(forward, *floats)
    grads = pullback(out_cotangent.astype(jnp.float32))
    return (output.astype(jnp.bfloat16), grads[0].astype(jnp.bfloat16), grads[1], grads[2], grads[3], grads[4], grads[5], grads[6], grads[7], grads[8], grads[9], grads[10], grads[11], grads[12])
```

```python
import functools

import jax
import jax.numpy as jnp
from jax import lax
from jax.experimental import pallas as pl
from jax.experimental.pallas import tpu as pltpu
from jax.sharding import PartitionSpec as P

HEAD_DIM = 64
EPSILON = 1e-06
NEGATIVE = -1e30
ROPE_BASE = 1000000.0
LANES = 128
QUAD = 4
GRAIN = 8
MESH = pl.DeviceIdType.MESH
VMEM_LIMIT = 60 * 1024 * 1024
BF16 = jnp.bfloat16
F32 = jnp.float32


def round_up(value, step):
    return -(-value // step) * step


def nn(left, right):
    return lax.dot_general(left, right, (((1,), (0,)), ((), ())), preferred_element_type=F32)


def nt(left, right):
    return lax.dot_general(left, right, (((1,), (1,)), ((), ())), preferred_element_type=F32)


def tn(left, right):
    return lax.dot_general(left, right, (((0,), (0,)), ((), ())), preferred_element_type=F32)


class Place:
    def __init__(self, groups):
        seq = lax.axis_index("seq").astype(jnp.int32)
        tp = lax.axis_index("tp").astype(jnp.int32)
        self.groups = groups
        self.seq = seq
        self.tp = tp
        self.group = seq // QUAD
        self.quad = seq % QUAD
        self.core = seq % 2
        self.side = (seq // 2) % 2
        self.sibling = (seq + 1 - 2 * self.core, tp)
        self.across = (seq + 2 - 4 * self.side, tp)
        self.partner = (seq, 1 - tp)

    def seq_at(self, group, side, core):
        return group * QUAD + side * 2 + core

    def in_group(self, group):
        return (group * QUAD + self.quad, self.tp)


def send(src, dst, send_sem, recv_sem, device):
    pltpu.make_async_remote_copy(
        src_ref=src,
        dst_ref=dst,
        send_sem=send_sem,
        recv_sem=recv_sem,
        device_id=device,
        device_id_type=MESH,
    ).start()


def sent(src, send_sem, device):
    pltpu.make_async_remote_copy(
        src_ref=src,
        dst_ref=src,
        send_sem=send_sem,
        recv_sem=send_sem,
        device_id=device,
        device_id_type=MESH,
    ).wait_send()


def arrived(dst, recv_sem, device):
    pltpu.make_async_remote_copy(
        src_ref=dst,
        dst_ref=dst,
        send_sem=recv_sem,
        recv_sem=recv_sem,
        device_id=device,
        device_id_type=MESH,
    ).wait_recv()


def meet(place, whole_column):
    barrier = pltpu.get_barrier_semaphore()
    for device in (place.sibling, place.across, place.partner):
        pl.semaphore_signal(barrier, inc=1, device_id=device, device_id_type=MESH)
    if whole_column:
        for step in range(1, place.groups):
            other = place.in_group((place.group + step) % place.groups)
            pl.semaphore_signal(barrier, inc=1, device_id=other, device_id_type=MESH)
        pl.semaphore_wait(barrier, 3 + place.groups - 1)
    else:
        pl.semaphore_wait(barrier, 3)


class LayerGather:
    def __init__(self, place, all_ref, half, recv, part, sems):
        self.place = place
        self.all_ref = all_ref
        self.half = half
        self.first = round_up(half // 2, 16)
        self.recv, self.part, self.sems = recv, part, sems

    def index(self, flip_side, flip_core, flip_tp):
        place = self.place
        side = 1 - place.side if flip_side else place.side
        core = 1 - place.core if flip_core else place.core
        tp = 1 - place.tp if flip_tp else place.tp
        return (side * 2 + core) * 2 + tp

    def rows(self, block, start=0, size=None):
        size = self.half if size is None else size
        return self.all_ref.at[pl.ds(pl.multiple_of(block * self.half + start, 16), size)]

    def start(self):
        place = self.place
        own = self.index(0, 0, 0)
        for number, device in enumerate((place.across, place.partner, place.sibling)):
            send(self.rows(own), self.rows(own), self.sems.at[number], self.recv.at[own], device)

    def from_across(self):
        place = self.place
        block = self.index(1, 0, 0)
        arrived(self.rows(block), self.recv.at[block], place.across)
        part = self.rows(block, 0, self.first)
        send(part, part, self.sems.at[3], self.part.at[0], place.partner)
        send(self.rows(block), self.rows(block), self.sems.at[4], self.recv.at[block], place.sibling)

    def from_partner(self):
        place = self.place
        block = self.index(0, 0, 1)
        arrived(self.rows(block), self.recv.at[block], place.partner)
        part = self.rows(block, self.first, self.half - self.first)
        send(part, part, self.sems.at[5], self.part.at[1], place.across)
        send(self.rows(block), self.rows(block), self.sems.at[6], self.recv.at[block], place.sibling)

    def diagonal(self):
        place = self.place
        block = self.index(1, 0, 1)
        arrived(self.rows(block, 0, self.first), self.part.at[0], place.partner)
        arrived(self.rows(block, self.first, self.half - self.first), self.part.at[1], place.across)
        send(self.rows(block), self.rows(block), self.sems.at[7], self.recv.at[block], place.sibling)

    def finish(self):
        place = self.place
        for side in (0, 1):
            for tp in (0, 1):
                block = self.index(side, 1, tp)
                arrived(self.rows(block), self.recv.at[block], place.sibling)
        own = self.index(0, 0, 0)
        for number, device in enumerate((place.across, place.partner, place.sibling)):
            sent(self.rows(own), self.sems.at[number], device)
        sent(self.rows(own, 0, self.first), self.sems.at[3], place.partner)
        sent(self.rows(own), self.sems.at[4], place.sibling)
        sent(self.rows(own, self.first, self.half - self.first), self.sems.at[5], place.across)
        sent(self.rows(own), self.sems.at[6], place.sibling)
        sent(self.rows(own), self.sems.at[7], place.sibling)


def extended_keys(kv, chip, rows, width, slots):
    count = kv.shape[0]
    lane = lax.broadcasted_iota(jnp.int32, (count, width), 1) - HEAD_DIM
    row = lax.broadcasted_iota(jnp.int32, (count, width), 0)
    block = rows // 2
    number = jnp.zeros_like(row)
    for edge in range(block, count, block):
        number = number + (row >= edge).astype(jnp.int32)
    hot = (lane == number + chip * (count // block)) | ((lane >= slots) & (lane < slots + 3))
    extra = jnp.where(hot, 1.0, 0.0).astype(BF16)
    if width == LANES:
        return jnp.where(lane < 0, kv, extra)
    first = jnp.where(lane[:, :LANES] < 0, kv, extra[:, :LANES])
    return jnp.concatenate([first, extra[:, LANES:]], axis=1)


def hide_later(scores, place, rows, first_query):
    count, width = scores.shape
    block = rows // 2
    key = lax.broadcasted_iota(jnp.int32, (count, 1), 0) - place.core * rows
    query = lax.broadcasted_iota(jnp.int32, (1, width), 1) + first_query
    query = query % rows
    end = jnp.where(query < block, block, rows)
    return jnp.where((key > query) & (key < end), NEGATIVE, scores)


def split_rows(values, at, count):
    one = values.astype(BF16).astype(F32)
    two = (values - one).astype(BF16).astype(F32)
    three = values - one - two
    row = lax.broadcasted_iota(jnp.int32, (count, values.shape[1]), 0) - at
    picked = jnp.where(row == 0, one, jnp.where(row == 1, two, jnp.where(row == 2, three, 0.0)))
    return picked.astype(BF16)


def attend_kernel(
    groups,
    slots,
    kv_own,
    qt,
    x_in,
    out_weight,
    gain,
    cot,
    kv_all,
    normed_all,
    cot_all,
    resid_out,
    att_out,
    ot_out,
    lse_out,
    s_buf,
    m_buf,
    l_buf,
    part_buf,
    part_send,
    part_recv,
    kv_recv,
    kv_z,
    kv_x,
    kv_sib,
    n_recv,
    n_part,
    n_sems,
    c_recv,
    c_part,
    c_sems,
    p_sems,
):
    place = Place(groups)
    rows = kv_own.shape[0]
    half = rows // 2
    span = 2 * rows
    width, queries = qt.shape
    block = queries // 2
    chunks = 2 * groups
    heads = out_weight.shape[0] // HEAD_DIM

    kv_all[pl.ds(place.seq * rows, rows), :] = kv_own[...]
    own_half = place.quad * 2 + place.tp
    cot_all[pl.ds(pl.multiple_of(own_half * half, 16), half), :] = cot[
        pl.ds(pl.multiple_of(place.tp * half, 16), half), :
    ]
    meet(place, True)

    def kv_rows(seq):
        return kv_all.at[pl.ds(pl.multiple_of(seq * rows, 16), rows)]

    own = kv_rows(place.seq)
    send(own, own, kv_sib.at[0], kv_recv.at[place.seq], place.sibling)
    for step in range(1, groups):
        other = place.in_group((place.group + step) % groups)
        send(own, own, kv_z.at[step - 1], kv_recv.at[place.seq], other)
    send(own, own, kv_x.at[0], kv_recv.at[place.seq], place.across)

    def chunk_place(number):
        far = number % 2
        group = (place.group + number // 2) % groups
        side = place.side + far * (1 - 2 * place.side)
        return group, side

    def pass_on(number):
        group, side = chunk_place(number)
        seq = place.seq_at(group, side, place.core)
        view = kv_rows(seq)
        arrived(view, kv_recv.at[seq], place.across)
        send(view, view, kv_sib.at[number], kv_recv.at[seq], place.sibling)

        @pl.when(number % 2 == 0)
        def near():
            send(view, view, kv_x.at[number // 2], kv_recv.at[seq], place.across)

    def ready(number):
        group, side = chunk_place(number)
        seq = place.seq_at(group, side, 1 - place.core)
        arrived(kv_rows(seq), kv_recv.at[seq], place.sibling)

    gather_cot = LayerGather(place, cot_all, half, c_recv, c_part, c_sems)
    gather_normed = LayerGather(place, normed_all, half, n_recv, n_part, n_sems)

    def kv_chunk(number):
        group, side = chunk_place(number)
        chip = group * 2 + side
        return chip, kv_all[pl.ds(pl.multiple_of(chip * span, 16), span), :]

    def scores(number, part, slot, own_chip=False):
        chip, kv = kv_chunk(number)
        keys = extended_keys(kv, chip, rows, width, slots)
        value = nn(keys, qt[:, part * block : (part + 1) * block])
        if own_chip:
            value = hide_later(value, place, rows, part * block)
        s_buf[slot] = value

    def absorb(number, part, slot, first=False):
        chip, kv = kv_chunk(number)
        lanes = slice(part * block, (part + 1) * block)
        value = s_buf[slot]
        top = jnp.max(value, axis=0, keepdims=True)
        if not first:
            old = m_buf[:, lanes]
            top = jnp.maximum(old, top)
            shrink = jnp.exp(old - top)
        weights = jnp.exp(value - top)
        total = jnp.sum(weights, axis=0, keepdims=True)
        product = tn(kv[:, HEAD_DIM:], weights.astype(BF16))
        if not first:
            total = total + l_buf[:, lanes] * shrink
            product = product + ot_out[:, lanes] * shrink
        m_buf[:, lanes] = top
        l_buf[:, lanes] = total
        ot_out[:, lanes] = product

    ready(0)
    scores(0, 0, 0, True)
    scores(0, 1, 1, True)
    absorb(0, 0, 0, True)
    pass_on(1)
    pass_on(2)
    ready(1)
    scores(1, 0, 0)
    absorb(0, 1, 1, True)

    def step(number, unused):
        scores(number, 1, 1)
        absorb(number, 0, 0)

        @pl.when(number + 2 < chunks)
        def look_ahead():
            pass_on(number + 2)

        @pl.when(number + 1 < chunks)
        def next_ready():
            ready(number + 1)

        @pl.when(number == 1)
        def cot_start():
            gather_cot.start()

        @pl.when(number == chunks - 3)
        def cot_middle():
            gather_cot.from_across()
            gather_cot.from_partner()

        scores(jnp.minimum(number + 1, chunks - 1), 0, 0)
        absorb(number, 1, 1)
        return unused

    lax.fori_loop(1, chunks, step, 0)

    ot = ot_out[...] / l_buf[...]
    ot_out[...] = ot
    lse_out[...] = m_buf[...] + jnp.log(l_buf[...])
    natural = jnp.transpose(ot).astype(BF16)
    att = jnp.concatenate(
        [natural[head * rows : (head + 1) * rows, :] for head in range(heads)], axis=1
    )
    att_out[...] = att
    part_buf[...] = nn(att, out_weight[...])
    other_rows = pl.ds(pl.multiple_of((1 - place.tp) * half, 16), half)
    my_rows = pl.ds(pl.multiple_of(place.tp * half, 16), half)
    part_send[...] = part_buf[other_rows, :].astype(BF16)
    send(part_send, part_recv, p_sems.at[0], p_sems.at[1], place.partner)
    gather_cot.diagonal()
    mine = part_buf[my_rows, :] + x_in[my_rows, :].astype(F32)
    arrived(part_recv, p_sems.at[1], place.partner)
    resid = mine + part_recv[...].astype(F32)
    resid_out[...] = resid
    factor = lax.rsqrt(jnp.mean(resid * resid, axis=-1, keepdims=True) + EPSILON)
    normed_all[pl.ds(pl.multiple_of(own_half * half, 16), half), :] = (
        resid * factor * gain[...]
    ).astype(BF16)
    gather_normed.start()
    gather_normed.from_across()
    gather_normed.from_partner()
    gather_normed.diagonal()
    gather_normed.finish()
    gather_cot.finish()
    sent(part_send, p_sems.at[0], place.partner)

    def close(number, unused):
        sent(own, kv_sib.at[number], place.sibling)
        return unused

    lax.fori_loop(0, chunks, close, 0)
    for step_out in range(groups):
        sent(own, kv_x.at[step_out], place.across)
    for step_out in range(1, groups):
        sent(own, kv_z.at[step_out - 1], place.in_group((place.group + step_out) % groups))


class ChainSum:
    def __init__(self, place, own, incoming, final, sems):
        self.place = place
        self.own, self.incoming, self.final = own, incoming, final
        self.count = own.shape[0]
        (
            self.up_recv,
            self.up_send,
            self.fin_recv,
            self.fin_send,
            self.x_recv,
            self.x_send,
            self.c_recv,
            self.c_send,
        ) = sems

    def root(self, parity):
        return self.place.groups // 2 - 1 + parity

    def lag_up(self, parity):
        groups, group, root = self.place.groups, self.place.group, self.root(parity)
        most = max(root, groups - 1 - root)
        return jnp.where(
            group < root, group, jnp.where(group > root, groups - 1 - group, most)
        )

    def lag_down(self, parity):
        groups, group, root = self.place.groups, self.place.group, self.root(parity)
        most = max(root, groups - 1 - root)
        return most + jnp.abs(group - root)

    def total_steps(self):
        groups = self.place.groups
        most = groups // 2
        return self.count + 2 * most + 2

    def spread(self, i):
        place = self.place
        view = self.final.at[place.quad, i]
        send(view, view, self.x_send.at[i], self.x_recv.at[i], place.across)
        send(view, view, self.c_send.at[0, i], self.c_recv.at[0, i], place.sibling)

    def up(self, i, parity):
        place, root = self.place, self.root(parity)
        group, last = place.group, place.groups - 1
        mine = self.own.at[i]

        @pl.when((group > 0) & (group <= root))
        def from_left():
            arrived(self.incoming.at[i], self.up_recv.at[0, i], place.in_group(group - 1))
            mine[...] = (mine[...].astype(F32) + self.incoming[i].astype(F32)).astype(BF16)

        @pl.when((group < last) & (group > root))
        def from_right():
            arrived(self.incoming.at[i], self.up_recv.at[1, i], place.in_group(group + 1))
            mine[...] = (mine[...].astype(F32) + self.incoming[i].astype(F32)).astype(BF16)

        @pl.when(group < root)
        def to_right():
            send(
                mine,
                self.incoming.at[i],
                self.up_send.at[i],
                self.up_recv.at[0, i],
                place.in_group(group + 1),
            )

        @pl.when(group > root + 1)
        def to_left():
            send(
                mine,
                self.incoming.at[i],
                self.up_send.at[i],
                self.up_recv.at[1, i],
                place.in_group(group - 1),
            )

        @pl.when(group == root + 1)
        def to_root():
            send(
                mine,
                self.final.at[place.quad, i],
                self.up_send.at[i],
                self.up_recv.at[1, i],
                place.in_group(group - 1),
            )

        @pl.when(group == root)
        def at_root():
            view = self.final.at[place.quad, i]

            @pl.when(group < last)
            def both():
                arrived(view, self.up_recv.at[1, i], place.in_group(group + 1))
                view[...] = (mine[...].astype(F32) + view[...].astype(F32)).astype(BF16)

            @pl.when(group == last)
            def alone():
                view[...] = mine[...]

            @pl.when(group > 0)
            def left():
                send(
                    view,
                    view,
                    self.fin_send.at[0, i],
                    self.fin_recv.at[i],
                    place.in_group(group - 1),
                )

            @pl.when(group < last)
            def right():
                send(
                    view,
                    view,
                    self.fin_send.at[1, i],
                    self.fin_recv.at[i],
                    place.in_group(group + 1),
                )

            self.spread(i)

    def down(self, i, parity):
        place, root = self.place, self.root(parity)
        group, last = place.group, place.groups - 1
        view = self.final.at[place.quad, i]

        @pl.when(group != root)
        def take():
            arrived(view, self.fin_recv.at[i], place.sibling)

            @pl.when((group < root) & (group > 0))
            def left():
                send(
                    view,
                    view,
                    self.fin_send.at[0, i],
                    self.fin_recv.at[i],
                    place.in_group(group - 1),
                )

            @pl.when((group > root) & (group < last))
            def right():
                send(
                    view,
                    view,
                    self.fin_send.at[1, i],
                    self.fin_recv.at[i],
                    place.in_group(group + 1),
                )

            self.spread(i)

    def cross(self, i):
        place = self.place
        view = self.final.at[place.across[0] % QUAD, i]
        arrived(view, self.x_recv.at[i], place.across)
        send(view, view, self.c_send.at[1, i], self.c_recv.at[1, i], place.sibling)

    def step(self, number):
        for parity in (0, 1):
            i = number - self.lag_up(parity)

            @pl.when((i >= 0) & (i < self.count) & (i % 2 == parity))
            def go_up(i=i, parity=parity):
                self.up(i, parity)

        for parity in (0, 1):
            i = number - self.lag_down(parity)

            @pl.when((i >= 0) & (i < self.count) & (i % 2 == parity))
            def go_down(i=i, parity=parity):
                self.down(i, parity)

        for parity in (0, 1):
            i = number - self.lag_down(parity) - 1

            @pl.when((i >= 0) & (i < self.count) & (i % 2 == parity))
            def go_cross(i=i):
                self.cross(i)

    def finish(self):
        place = self.place
        group, last = place.group, place.groups - 1
        sibling_quad = place.sibling[0] % QUAD
        diagonal = 3 - place.quad

        def close(i, unused):
            root = place.groups // 2 - 1 + i % 2
            view = self.own.at[i]
            arrived(self.final.at[sibling_quad, i], self.c_recv.at[0, i], place.sibling)
            arrived(self.final.at[diagonal, i], self.c_recv.at[1, i], place.sibling)

            @pl.when(group != root)
            def up_done():
                sent(view, self.up_send.at[i], place.sibling)

            @pl.when((group <= root) & (group > 0))
            def left_done():
                sent(view, self.fin_send.at[0, i], place.sibling)

            @pl.when((group >= root) & (group < last))
            def right_done():
                sent(view, self.fin_send.at[1, i], place.sibling)

            sent(view, self.x_send.at[i], place.across)
            sent(view, self.c_send.at[0, i], place.sibling)
            sent(view, self.c_send.at[1, i], place.sibling)
            return unused

        lax.fori_loop(0, self.count, close, 0)


def chain_sems(count):
    dma = pltpu.SemaphoreType.DMA
    return [
        dma((2, count)),
        dma((count,)),
        dma((count,)),
        dma((2, count)),
        dma((count,)),
        dma((count,)),
        dma((2, count)),
        dma((2, count)),
    ]


class LayerSum:
    def __init__(self, place, part, half, core_in, left, right, left_in, right_in, last_in, sems):
        self.place, self.part, self.half = place, part, half
        self.core_in, self.left, self.right = core_in, left, right
        self.left_in, self.right_in, self.last_in = left_in, right_in, last_in
        self.sems = sems
        self.cut = left.shape[2]
        self.columns = part.shape[1]

    def rows(self, side, core):
        size = 2 * self.half
        return pl.ds(pl.multiple_of((side * 2 + core) * size, 16), size)

    def start(self):
        place = self.place
        for side in (0, 1):
            view = self.part.at[self.rows(side, 1 - place.core)]
            send(
                view,
                self.core_in.at[side],
                self.sems.at[side],
                self.sems.at[2 + side],
                place.sibling,
            )

    def own_rows(self, tp):
        return pl.ds(pl.multiple_of(tp * self.half, 16), self.half)

    def after_core(self):
        place = self.place
        for side in (0, 1):
            arrived(self.core_in.at[side], self.sems.at[2 + side], place.sibling)
            total = self.part[self.rows(side, place.core), :].astype(F32) + self.core_in[
                side
            ].astype(F32)
            self.left[side] = total[:, : self.cut].astype(BF16)
            self.right[side] = total[:, self.cut :].astype(BF16)

    def cross(self):
        place = self.place
        for side in (0, 1):
            send(
                self.left.at[side, self.own_rows(1 - place.tp)],
                self.left_in.at[side],
                self.sems.at[4 + side],
                self.sems.at[6 + side],
                place.partner,
            )
        send(
            self.right.at[1 - place.side],
            self.right_in,
            self.sems.at[8],
            self.sems.at[9],
            place.across,
        )

    def after_cross(self):
        place = self.place
        mine = self.own_rows(place.tp)
        for side in (0, 1):
            arrived(self.left_in.at[side], self.sems.at[6 + side], place.partner)
            self.left_in[side] = (
                self.left[side, mine, :].astype(F32) + self.left_in[side].astype(F32)
            ).astype(BF16)
        arrived(self.right_in, self.sems.at[9], place.across)
        self.right_in[...] = (
            self.right[place.side].astype(F32) + self.right_in[...].astype(F32)
        ).astype(BF16)
        send(
            self.left_in.at[1 - place.side],
            self.last_in.at[:, : self.cut],
            self.sems.at[10],
            self.sems.at[11],
            place.across,
        )
        send(
            self.right_in.at[self.own_rows(1 - place.tp)],
            self.last_in.at[:, self.cut :],
            self.sems.at[12],
            self.sems.at[13],
            place.partner,
        )

    def result(self):
        place = self.place
        arrived(self.last_in.at[:, : self.cut], self.sems.at[11], place.across)
        arrived(self.last_in.at[:, self.cut :], self.sems.at[13], place.partner)
        mine = jnp.concatenate(
            [self.left_in[place.side], self.right_in[self.own_rows(place.tp), :]], axis=1
        )
        return mine.astype(F32) + self.last_in[...].astype(F32)

    def finish(self):
        place = self.place
        for side in (0, 1):
            sent(self.core_in.at[side], self.sems.at[side], place.sibling)
            sent(self.left_in.at[side], self.sems.at[4 + side], place.partner)
        sent(self.right_in, self.sems.at[8], place.across)
        sent(self.last_in.at[:, : self.cut], self.sems.at[10], place.across)
        sent(self.last_in.at[:, self.cut :], self.sems.at[12], place.partner)


def layer_sum_scratch(half, columns):
    cut = columns // LANES // 2 * LANES
    if cut * 2 < columns:
        cut += LANES
    return [
        pltpu.VMEM((2, 2 * half, columns), BF16),
        pltpu.VMEM((2, 2 * half, cut), BF16),
        pltpu.VMEM((2, 2 * half, columns - cut), BF16),
        pltpu.VMEM((2, half, cut), BF16),
        pltpu.VMEM((2 * half, columns - cut), BF16),
        pltpu.VMEM((half, columns), BF16),
        pltpu.SemaphoreType.DMA((14,)),
    ]


def backward_kernel(
    groups,
    slots,
    grad_part,
    mlp_part,
    wide_in,
    tall_in,
    resid_in,
    cot,
    gain,
    out_weight,
    att,
    ot,
    lse,
    qt_in,
    kv_all,
    layer_out,
    resid_grad,
    dq_out,
    dkv_out,
    wide,
    tall,
    out_grad,
    gain_grad,
    *scratch,
):
    place = Place(groups)
    wide_own, tall_own, wide_up, tall_up = scratch[0:4]
    wide_sems, tall_sems = scratch[4:12], scratch[12:20]
    sum_g, sum_m = scratch[20:27], scratch[27:34]
    branch, qt, dot_t, q_pad, do_pad, dkv = scratch[34:40]
    sib_send, sib_in, x_send, x_in, z_send, z_in = scratch[40:46]
    kv_sems, pair_sems = scratch[46:48]
    rows = att.shape[0]
    half = rows // 2
    span = 2 * rows
    width, queries = qt_in.shape
    block = queries // 2
    chunks = 2 * groups
    heads = out_weight.shape[0] // HEAD_DIM
    my_rows = pl.ds(pl.multiple_of(place.tp * half, 16), half)
    other_rows = pl.ds(pl.multiple_of((1 - place.tp) * half, 16), half)

    grad_sum = LayerSum(place, grad_part, half, *sum_g)
    mlp_sum = LayerSum(place, mlp_part, half, *sum_m)
    tall_sum = ChainSum(place, tall_own, tall_up, tall, tall_sems)
    wide_sum = ChainSum(place, wide_own, wide_up, wide, wide_sems)
    fills = [
        pltpu.make_async_copy(tall_in, tall_own, pair_sems.at[4]),
        pltpu.make_async_copy(wide_in, wide_own, pair_sems.at[5]),
    ]
    for fill in fills:
        fill.start()
    tall_steps = tall_sum.count

    def chain_step(number):
        tall_sum.step(number)
        wide_sum.step(number - tall_steps)

    all_steps = tall_steps + wide_sum.total_steps()

    meet(place, True)
    grad_sum.start()
    for fill in fills:
        fill.wait()
    chain_step(0)
    mlp_sum.start()

    qt[...] = qt_in[...]
    at = HEAD_DIM + slots
    qt[at : at + 16, :] = split_rows(-lse[...], 0, 16)
    natural_q = jnp.transpose(qt_in[0:HEAD_DIM, :].astype(F32)).astype(BF16)
    q_pad[...] = jnp.concatenate([natural_q, jnp.zeros_like(natural_q)], axis=1)

    grad_sum.after_core()
    grad_sum.cross()
    chain_step(1)
    mlp_sum.after_core()
    grad_sum.after_cross()
    mlp_sum.cross()
    chain_step(2)

    resid = resid_in[...]
    factor = lax.rsqrt(jnp.mean(resid * resid, axis=-1, keepdims=True) + EPSILON)
    normed = resid * factor
    grad_normed = grad_sum.result()
    gain_grad[...] = jnp.sum(grad_normed * normed, axis=0, keepdims=True)
    weighted = grad_normed * gain[...]
    inner = jnp.mean(weighted * normed, axis=-1, keepdims=True)
    grad_resid = cot[my_rows, :].astype(F32) + factor * (weighted - normed * inner)
    resid_grad[...] = grad_resid
    branch[my_rows, :] = grad_resid.astype(BF16)
    send(
        branch.at[my_rows],
        branch.at[my_rows],
        pair_sems.at[0],
        pair_sems.at[1],
        place.partner,
    )
    mlp_sum.after_cross()
    chain_step(3)
    chain_step(4)
    arrived(branch.at[other_rows], pair_sems.at[1], place.partner)

    grads = branch[...]
    out_grad[...] = tn(att[...], grads)
    grad_att = nt(grads, out_weight[...]).astype(BF16)
    stacked = jnp.concatenate(
        [grad_att[:, head * HEAD_DIM : (head + 1) * HEAD_DIM] for head in range(heads)]
        + [jnp.zeros((queries - heads * rows, HEAD_DIM), BF16)],
        axis=0,
    )
    do_pad[...] = jnp.concatenate([jnp.zeros_like(stacked), stacked], axis=1)
    turned = jnp.transpose(stacked.astype(F32))
    delta = jnp.sum(turned * ot[...], axis=0, keepdims=True)
    dot_t[0:HEAD_DIM, :] = split_rows(-delta, 0, HEAD_DIM)
    dot_t[HEAD_DIM:, :] = turned.astype(BF16)
    chain_step(5)
    layer_out[my_rows, :] = (resid + mlp_sum.result()).astype(BF16)
    send(
        layer_out.at[my_rows],
        layer_out.at[my_rows],
        pair_sems.at[2],
        pair_sems.at[3],
        place.partner,
    )
    dq_out[...] = jnp.zeros_like(dq_out)

    def chunk_place(number):
        far = 1 - number % 2
        group = (place.group + 1 + number // 2) % groups
        side = place.side + far * (1 - 2 * place.side)
        return group, side

    lane = lax.broadcasted_iota(jnp.int32, (1, LANES), 1)
    ones = jnp.where(lane < 3, 1.0, 0.0).astype(BF16)

    def attend_back(number, slot, own_chip=False):
        group, side = chunk_place(number)
        chip = group * 2 + side
        at_rows = pl.ds(pl.multiple_of(chip * span, 16), span)
        kv = kv_all[at_rows, :]
        keys = extended_keys(kv, chip, rows, width, slots)
        values = jnp.where(lane >= HEAD_DIM, kv, jnp.broadcast_to(ones, kv.shape))
        for part in range(2):
            lanes = slice(part * block, (part + 1) * block)
            score = nn(keys, qt[:, lanes])
            if own_chip:
                score = hide_later(score, place, rows, part * block)
            weights = jnp.exp(score)
            change = nn(values, dot_t[:, lanes])
            low = (weights * change).astype(BF16)
            total = nn(weights.astype(BF16), do_pad[lanes, :]) + nn(low, q_pad[lanes, :])
            if part == 0:
                dkv[slot] = total
            else:
                dkv[slot] += total
            dq_out[:, lanes] += tn(kv[:, :HEAD_DIM], low)

    def hand_over(number, slot):
        other = pl.ds(pl.multiple_of((1 - place.core) * rows, 16), rows)
        sib_send[number] = dkv[slot, other, :].astype(BF16)
        send(
            sib_send.at[number],
            sib_in.at[number],
            kv_sems.at[0, number],
            kv_sems.at[1, number],
            place.sibling,
        )

    def take_over(number, near, own_group=False):
        group, side = chunk_place(number)
        step = number // 2
        arrived(sib_in.at[number], kv_sems.at[1, number], place.sibling)
        mine = pl.ds(pl.multiple_of(place.core * rows, 16), rows)
        total = dkv[1 if near else 0, mine, :] + sib_in[number].astype(F32)
        if not near:
            x_send[step] = total.astype(BF16)
            send(
                x_send.at[step],
                x_in.at[step],
                kv_sems.at[2, step],
                kv_sems.at[3, step],
                place.across,
            )
            return
        arrived(x_in.at[step], kv_sems.at[3, step], place.across)
        total = total + x_in[step].astype(F32)
        if own_group:
            dkv_out[...] = total
            return
        z_send[step] = total.astype(BF16)
        back = groups - 2 - step
        send(
            z_send.at[step],
            z_in.at[back],
            kv_sems.at[4, step],
            kv_sems.at[5, back],
            place.in_group(group),
        )

    def pair(step, unused):
        attend_back(2 * step, 0)
        hand_over(2 * step, 0)
        chain_step(6 + 2 * step)

        @pl.when(step > 0)
        def last_near():
            take_over(2 * step - 1, True)

        attend_back(2 * step + 1, 1)
        hand_over(2 * step + 1, 1)
        take_over(2 * step, False)
        chain_step(7 + 2 * step)
        return unused

    lax.fori_loop(0, groups - 1, pair, 0)
    attend_back(chunks - 2, 0)
    hand_over(chunks - 2, 0)
    chain_step(6 + 2 * (groups - 1))
    if groups > 1:
        take_over(chunks - 3, True)
    attend_back(chunks - 1, 1, True)
    hand_over(chunks - 1, 1)
    take_over(chunks - 2, False)
    chain_step(7 + 2 * (groups - 1))
    take_over(chunks - 1, True, True)
    for step in range(groups - 1):
        arrived(z_in.at[step], kv_sems.at[5, step], place.sibling)
        dkv_out[...] += z_in[step].astype(F32)

    def rest(number, unused):
        chain_step(number)
        return unused

    lax.fori_loop(8 + 2 * (groups - 1), all_steps, rest, 0)

    arrived(layer_out.at[other_rows], pair_sems.at[3], place.partner)
    sent(branch.at[my_rows], pair_sems.at[0], place.partner)
    sent(branch.at[my_rows], pair_sems.at[2], place.partner)
    grad_sum.finish()
    mlp_sum.finish()
    tall_sum.finish()
    wide_sum.finish()
    for number in range(chunks):
        sent(sib_send.at[number], kv_sems.at[0, number], place.sibling)
    for step in range(groups):
        sent(x_send.at[step], kv_sems.at[2, step], place.across)
    for step in range(groups - 1):
        sent(z_send.at[step], kv_sems.at[4, step], place.sibling)


def vmem_specs(count):
    return [pl.BlockSpec(memory_space=pltpu.VMEM)] * count


def params(collective):
    return pltpu.CompilerParams(
        collective_id=collective, has_side_effects=True, vmem_limit_bytes=VMEM_LIMIT
    )


def attend(groups, slots, kv_own, qt, x_in, out_weight, gain, cot):
    rows, features = x_in.shape
    half = rows // 2
    total = groups * QUAD * rows
    width, queries = qt.shape
    dma = pltpu.SemaphoreType.DMA
    shape = jax.ShapeDtypeStruct
    return pl.pallas_call(
        functools.partial(attend_kernel, groups, slots),
        out_shape=[
            shape((total, LANES), BF16),
            shape((QUAD * rows, features), BF16),
            shape((QUAD * rows, features), BF16),
            shape((half, features), F32),
            shape((rows, out_weight.shape[0]), BF16),
            shape((HEAD_DIM, queries), F32),
            shape((1, queries), F32),
        ],
        in_specs=vmem_specs(6),
        out_specs=vmem_specs(7),
        scratch_shapes=[
            pltpu.VMEM((2, 2 * rows, queries // 2), F32),
            pltpu.VMEM((1, queries), F32),
            pltpu.VMEM((1, queries), F32),
            pltpu.VMEM((rows, features), F32),
            pltpu.VMEM((half, features), BF16),
            pltpu.VMEM((half, features), BF16),
            dma((groups * QUAD,)),
            dma((groups,)),
            dma((groups,)),
            dma((2 * groups,)),
            dma((8,)),
            dma((2,)),
            dma((8,)),
            dma((8,)),
            dma((2,)),
            dma((8,)),
            dma((2,)),
        ],
        compiler_params=params(1),
        name="attend",
    )(kv_own, qt, x_in, out_weight, gain, cot)


def backward(groups, slots, grad_part, mlp_part, wide, tall, resid, cot, gain, out_weight, att, ot, lse, qt, kv_all):
    rows, inner = att.shape
    half = rows // 2
    features = grad_part.shape[1]
    total = kv_all.shape[0]
    width, queries = qt.shape
    chunks = 2 * groups
    dma = pltpu.SemaphoreType.DMA
    shape = jax.ShapeDtypeStruct
    pass_shape = (rows, LANES)
    return pl.pallas_call(
        functools.partial(backward_kernel, groups, slots),
        out_shape=[
            shape((rows, features), BF16),
            shape((half, features), F32),
            shape((HEAD_DIM, queries), F32),
            shape((rows, LANES), F32),
            shape((QUAD, *wide.shape), BF16),
            shape((QUAD, *tall.shape), BF16),
            shape((inner, features), F32),
            shape((1, features), F32),
        ],
        in_specs=vmem_specs(2) + [pl.BlockSpec(memory_space=pl.ANY)] * 2 + vmem_specs(9),
        out_specs=vmem_specs(8),
        scratch_shapes=[
            pltpu.VMEM(wide.shape, BF16),
            pltpu.VMEM(tall.shape, BF16),
            pltpu.VMEM(wide.shape, BF16),
            pltpu.VMEM(tall.shape, BF16),
            *chain_sems(wide.shape[0]),
            *chain_sems(tall.shape[0]),
            *layer_sum_scratch(half, features),
            *layer_sum_scratch(half, features),
            pltpu.VMEM((rows, features), BF16),
            pltpu.VMEM((width, queries), BF16),
            pltpu.VMEM((LANES, queries), BF16),
            pltpu.VMEM((queries, LANES), BF16),
            pltpu.VMEM((queries, LANES), BF16),
            pltpu.VMEM((2, 2 * rows, LANES), F32),
            pltpu.VMEM((chunks, *pass_shape), BF16),
            pltpu.VMEM((chunks, *pass_shape), BF16),
            pltpu.VMEM((groups, *pass_shape), BF16),
            pltpu.VMEM((groups, *pass_shape), BF16),
            pltpu.VMEM((groups, *pass_shape), BF16),
            pltpu.VMEM((groups, *pass_shape), BF16),
            dma((6, chunks)),
            dma((6,)),
        ],
        compiler_params=params(2),
        name="backward",
    )(grad_part, mlp_part, wide, tall, resid, cot, gain, out_weight, att, ot, lse, qt, kv_all)


def rope_tables(positions, head_size):
    half_size = head_size // 2
    exponent = jnp.arange(half_size, dtype=F32) * (2.0 / head_size)
    frequency = jnp.power(ROPE_BASE, -exponent)
    angle = positions.astype(F32)[:, None] * frequency[None, :]
    return (jnp.cos(angle)[:, None, :], jnp.sin(angle)[:, None, :])


def rotate(values, cosine, sine):
    half_size = values.shape[-1] // 2
    first = values[..., :half_size]
    second = values[..., half_size:]
    return jnp.concatenate(
        [first * cosine - second * sine, second * cosine + first * sine], axis=-1
    )


def rms_backward(grad_normed, normed, factor, gain):
    gain_grad = jnp.sum(grad_normed * normed, axis=0)
    weighted = grad_normed * gain
    values_grad = factor * (weighted - normed * jnp.mean(weighted * normed, axis=-1, keepdims=True))
    return (gain_grad, values_grad)


def piece_of(weight, axis, piece, quad):
    pads = [(0, 0, 0), (0, 0, 0)]
    pads[axis] = (0, piece * QUAD - weight.shape[axis], 0)
    padded = lax.pad(weight, jnp.zeros((), weight.dtype), pads)
    return lax.dynamic_slice_in_dim(padded, quad * piece, piece, axis)


def per_device(
    groups,
    layer_input,
    block_order,
    attn_gain,
    query_weight,
    query_bias,
    key_weight,
    key_bias,
    value_weight,
    value_bias,
    out_weight,
    mlp_gain,
    gate_weight,
    up_weight,
    down_weight,
    out_cotangent,
):
    rows, features = layer_input.shape
    block_rows = rows // 2
    slots = block_order.shape[0]
    hidden = gate_weight.shape[1]
    heads = query_weight.shape[1] // HEAD_DIM
    piece = round_up(hidden // LANES, QUAD) // QUAD * LANES
    queries = round_up(heads * rows, 2 * LANES)
    width = round_up(HEAD_DIM + slots + 16, LANES)
    scale = HEAD_DIM ** (-0.5)
    seq_index = lax.axis_index("seq")
    quad = seq_index % QUAD
    tp_index = lax.axis_index("tp")
    own_slots = lax.dynamic_slice_in_dim(block_order, 2 * seq_index, 2)
    steps_in = jnp.arange(block_rows, dtype=jnp.int32)
    own_places = (own_slots[:, None] * block_rows + steps_in[None, :]).reshape(-1)
    cosine, sine = rope_tables(own_places, HEAD_DIM)
    inputs = layer_input.astype(F32)
    factor_first = lax.rsqrt(jnp.mean(inputs * inputs, axis=-1, keepdims=True) + EPSILON)
    normed_first = inputs * factor_first
    normed_attn = (normed_first * attn_gain).astype(BF16)
    query_rows = (
        jnp.dot(normed_attn, query_weight, preferred_element_type=F32) + query_bias
    ).reshape(rows, heads, HEAD_DIM)
    key_rows = (jnp.dot(normed_attn, key_weight, preferred_element_type=F32) + key_bias).reshape(
        rows, 1, HEAD_DIM
    )
    value_rows = (
        jnp.dot(normed_attn, value_weight, preferred_element_type=F32) + value_bias
    ).astype(BF16)
    query_rot = rotate(query_rows, cosine, sine).astype(BF16)
    key_rot = rotate(key_rows, cosine, sine).astype(BF16).reshape(rows, HEAD_DIM)
    kv_own = jnp.concatenate([key_rot, value_rows], axis=1)
    query_t = jnp.transpose(query_rot * jnp.asarray(scale, BF16), (2, 1, 0)).reshape(
        HEAD_DIM, heads * rows
    )
    later = block_order[:, None] > jnp.repeat(own_slots, block_rows)[None, :]
    bias = jnp.tile(jnp.where(later, NEGATIVE, 0.0).astype(BF16), (1, heads))
    qt = jnp.concatenate(
        [query_t, bias, jnp.zeros((width - HEAD_DIM - slots, heads * rows), BF16)], axis=0
    )
    qt = jnp.pad(qt, ((0, 0), (0, queries - heads * rows)))
    gain_row = mlp_gain[None, :]

    kv_all, normed_all, cot_all, resid, att, ot, lse = attend(
        groups, slots, kv_own, qt, layer_input, out_weight, gain_row, out_cotangent
    )

    gate_piece = piece_of(gate_weight, 1, piece, quad)
    up_piece = piece_of(up_weight, 1, piece, quad)
    down_piece = piece_of(down_weight, 0, piece, quad)
    gate = jnp.dot(normed_all, gate_piece, preferred_element_type=F32)
    upward = jnp.dot(normed_all, up_piece, preferred_element_type=F32)
    sigmoid_gate = jax.nn.sigmoid(gate)
    silu_gate = gate * sigmoid_gate
    mixed = (silu_gate * upward).astype(BF16)
    mlp_part = jnp.dot(mixed, down_piece, preferred_element_type=F32).astype(BF16)
    down_grad = jnp.einsum("rf,rd->fd", mixed, cot_all, preferred_element_type=F32).astype(BF16)
    grad_mixed = jnp.einsum("rd,fd->rf", cot_all, down_piece, preferred_element_type=F32)
    grad_gate = (grad_mixed * upward * sigmoid_gate * (1.0 + gate * (1.0 - sigmoid_gate))).astype(
        BF16
    )
    grad_upward = (grad_mixed * silu_gate).astype(BF16)
    gate_grad = jnp.einsum("rd,rf->df", normed_all, grad_gate, preferred_element_type=F32)
    up_grad = jnp.einsum("rd,rf->df", normed_all, grad_upward, preferred_element_type=F32)
    grad_part = (
        jnp.einsum("rf,df->rd", grad_gate, gate_piece, preferred_element_type=F32)
        + jnp.einsum("rf,df->rd", grad_upward, up_piece, preferred_element_type=F32)
    ).astype(BF16)
    wide = jnp.concatenate([gate_grad.astype(BF16), up_grad.astype(BF16)], axis=0).reshape(
        2 * GRAIN, features // GRAIN, piece
    )
    tall = down_grad.reshape(GRAIN, piece // GRAIN, features)

    layer_output, grad_resid_half, dq, dkv, wide_sum, tall_sum, out_grad, mlp_gain_half = backward(
        groups, slots, grad_part, mlp_part, wide, tall, resid, out_cotangent, gain_row, out_weight,
        att, ot, lse, qt, kv_all,
    )

    keep = hidden - (QUAD - 1) * piece
    wide_sum = wide_sum.reshape(QUAD, 2, features, piece)
    tall_sum = tall_sum.reshape(QUAD, piece, features)

    def side_by_side(number):
        parts = [wide_sum[i, number] for i in range(QUAD - 1)] + [
            wide_sum[QUAD - 1, number][:, :keep]
        ]
        return jnp.concatenate(parts, axis=1).astype(F32)

    gate_sum, up_sum = side_by_side(0), side_by_side(1)
    down_sum = tall_sum.reshape(QUAD * piece, features)[:hidden].astype(F32)

    grad_query_rot = jnp.transpose(
        dq[:, : heads * rows].reshape(HEAD_DIM, heads, rows), (2, 1, 0)
    ) * scale
    grad_query = rotate(grad_query_rot, cosine, -sine).reshape(rows, -1).astype(BF16)
    grad_key = (
        rotate(dkv[:, :HEAD_DIM].reshape(rows, 1, HEAD_DIM), cosine, -sine)
        .reshape(rows, HEAD_DIM)
        .astype(BF16)
    )
    grad_value = dkv[:, HEAD_DIM:].astype(BF16)
    query_grad = jnp.einsum("rd,rh->dh", normed_attn, grad_query, preferred_element_type=F32)
    key_grad = jnp.einsum("rd,rh->dh", normed_attn, grad_key, preferred_element_type=F32)
    value_grad = jnp.einsum("rd,rh->dh", normed_attn, grad_value, preferred_element_type=F32)
    query_bias_grad = jnp.sum(grad_query.astype(F32), axis=0)
    key_bias_grad = jnp.sum(grad_key.astype(F32), axis=0)
    value_bias_grad = jnp.sum(grad_value.astype(F32), axis=0)
    grad_normed_attn = (
        jnp.einsum("rh,dh->rd", grad_query, query_weight, preferred_element_type=F32)
        + jnp.einsum("rh,dh->rd", grad_key, key_weight, preferred_element_type=F32)
        + jnp.einsum("rh,dh->rd", grad_value, value_weight, preferred_element_type=F32)
    )
    grad_normed_attn = lax.psum(grad_normed_attn.astype(BF16), "tp").astype(F32)
    attn_gain_grad, grad_input_part = rms_backward(
        grad_normed_attn, normed_first, factor_first, attn_gain
    )
    grad_resid = lax.all_gather(grad_resid_half, "tp", axis=0, tiled=True)
    input_grad = (grad_resid + grad_input_part).astype(BF16)
    mlp_gain_grad = lax.psum(mlp_gain_half[0], ("seq", "tp"))
    small = jnp.concatenate([attn_gain_grad, query_bias_grad, key_bias_grad, value_bias_grad])
    small = lax.psum(small, "seq")
    attn_gain_grad = small[:features]
    query_bias_grad = small[features : features + heads * HEAD_DIM]
    key_bias_grad = small[features + heads * HEAD_DIM : features + (heads + 1) * HEAD_DIM]
    value_bias_grad = small[features + (heads + 1) * HEAD_DIM :]
    query_grad, key_grad, value_grad, out_grad = (
        value.astype(F32)
        for value in lax.psum(
            tuple(v.astype(BF16) for v in (query_grad, key_grad, value_grad, out_grad)), "seq"
        )
    )
    return (
        layer_output,
        input_grad,
        attn_gain_grad,
        query_grad,
        query_bias_grad,
        key_grad,
        key_bias_grad,
        value_grad,
        value_bias_grad,
        out_grad,
        mlp_gain_grad,
        gate_sum,
        up_sum,
        down_sum,
    )


def solution(mesh):
    groups = mesh.shape["seq"] // QUAD
    by_rows, columns, rows, vector, whole = (
        P("seq", None),
        P(None, "tp"),
        P("tp", None),
        P("tp"),
        P(),
    )
    return jax.shard_map(
        functools.partial(per_device, groups),
        mesh=mesh,
        in_specs=(
            by_rows, whole, whole, columns, vector, columns, vector, columns, vector, rows,
            whole, columns, columns, rows, by_rows,
        ),
        out_specs=(
            by_rows, by_rows, whole, columns, vector, columns, vector, columns, vector, rows,
            whole, columns, columns, rows,
        ),
        check_vma=False,
    )
```

```python
import functools

import jax
import jax.numpy as jnp
from jax import lax
from jax.experimental import pallas as pl
from jax.experimental.pallas import tpu as pltpu
from jax.sharding import PartitionSpec as P

HEAD_DIM = 64
EPSILON = 1e-06
NEGATIVE = -1e30
ROPE_BASE = 1000000.0
LANES = 128
QUAD = 4
WIDE_ROWS = 64
TALL_ROWS = 64
SHARE = (4, 3, 3, 4, 1, 1, 2, 3, 2, 2, 4, 1, 2, 1, 2)
PACE = 4
MESH = pl.DeviceIdType.MESH
VMEM_LIMIT = 60 * 1024 * 1024
BF16 = jnp.bfloat16
F32 = jnp.float32


def round_up(value, step):
    return -(-value // step) * step


def nn(left, right):
    return lax.dot_general(left, right, (((1,), (0,)), ((), ())), preferred_element_type=F32)


def nt(left, right):
    return lax.dot_general(left, right, (((1,), (1,)), ((), ())), preferred_element_type=F32)


def tn(left, right):
    return lax.dot_general(left, right, (((0,), (0,)), ((), ())), preferred_element_type=F32)


class Place:
    def __init__(self, groups):
        seq = lax.axis_index("seq").astype(jnp.int32)
        tp = lax.axis_index("tp").astype(jnp.int32)
        self.groups = groups
        self.seq = seq
        self.tp = tp
        self.group = seq // QUAD
        self.quad = seq % QUAD
        self.core = seq % 2
        self.side = (seq // 2) % 2
        self.sibling = (seq + 1 - 2 * self.core, tp)
        self.across = (seq + 2 - 4 * self.side, tp)
        self.partner = (seq, 1 - tp)

    def seq_at(self, group, side, core):
        return group * QUAD + side * 2 + core

    def in_group(self, group):
        return (group * QUAD + self.quad, self.tp)


def send(src, dst, send_sem, recv_sem, device):
    pltpu.make_async_remote_copy(
        src_ref=src,
        dst_ref=dst,
        send_sem=send_sem,
        recv_sem=recv_sem,
        device_id=device,
        device_id_type=MESH,
    ).start()


def sent(src, send_sem, device):
    pltpu.make_async_remote_copy(
        src_ref=src,
        dst_ref=src,
        send_sem=send_sem,
        recv_sem=send_sem,
        device_id=device,
        device_id_type=MESH,
    ).wait_send()


def arrived(dst, recv_sem, device):
    pltpu.make_async_remote_copy(
        src_ref=dst,
        dst_ref=dst,
        send_sem=recv_sem,
        recv_sem=recv_sem,
        device_id=device,
        device_id_type=MESH,
    ).wait_recv()


def meet(place, whole_column):
    barrier = pltpu.get_barrier_semaphore()
    for device in (place.sibling, place.across, place.partner):
        pl.semaphore_signal(barrier, inc=1, device_id=device, device_id_type=MESH)
    if whole_column:
        for step in range(1, place.groups):
            other = place.in_group((place.group + step) % place.groups)
            pl.semaphore_signal(barrier, inc=1, device_id=other, device_id_type=MESH)
        pl.semaphore_wait(barrier, 3 + place.groups - 1)
    else:
        pl.semaphore_wait(barrier, 3)


class LayerGather:
    def __init__(self, place, all_ref, half, recv, part, sems):
        self.place = place
        self.all_ref = all_ref
        self.half = half
        self.first = round_up(half // 2, 16)
        self.recv, self.part, self.sems = recv, part, sems

    def index(self, flip_side, flip_core, flip_tp):
        place = self.place
        side = 1 - place.side if flip_side else place.side
        core = 1 - place.core if flip_core else place.core
        tp = 1 - place.tp if flip_tp else place.tp
        return (side * 2 + core) * 2 + tp

    def rows(self, block, start=0, size=None):
        size = self.half if size is None else size
        return self.all_ref.at[pl.ds(pl.multiple_of(block * self.half + start, 16), size)]

    def start(self):
        place = self.place
        own = self.index(0, 0, 0)
        for number, device in enumerate((place.across, place.partner, place.sibling)):
            send(self.rows(own), self.rows(own), self.sems.at[number], self.recv.at[own], device)

    def from_across(self):
        place = self.place
        block = self.index(1, 0, 0)
        arrived(self.rows(block), self.recv.at[block], place.across)
        part = self.rows(block, 0, self.first)
        send(part, part, self.sems.at[3], self.part.at[0], place.partner)
        send(self.rows(block), self.rows(block), self.sems.at[4], self.recv.at[block], place.sibling)

    def from_partner(self):
        place = self.place
        block = self.index(0, 0, 1)
        arrived(self.rows(block), self.recv.at[block], place.partner)
        part = self.rows(block, self.first, self.half - self.first)
        send(part, part, self.sems.at[5], self.part.at[1], place.across)
        send(self.rows(block), self.rows(block), self.sems.at[6], self.recv.at[block], place.sibling)

    def diagonal(self):
        place = self.place
        block = self.index(1, 0, 1)
        arrived(self.rows(block, 0, self.first), self.part.at[0], place.partner)
        arrived(self.rows(block, self.first, self.half - self.first), self.part.at[1], place.across)
        send(self.rows(block), self.rows(block), self.sems.at[7], self.recv.at[block], place.sibling)

    def finish(self):
        place = self.place
        for side in (0, 1):
            for tp in (0, 1):
                block = self.index(side, 1, tp)
                arrived(self.rows(block), self.recv.at[block], place.sibling)
        own = self.index(0, 0, 0)
        for number, device in enumerate((place.across, place.partner, place.sibling)):
            sent(self.rows(own), self.sems.at[number], device)
        sent(self.rows(own, 0, self.first), self.sems.at[3], place.partner)
        sent(self.rows(own), self.sems.at[4], place.sibling)
        sent(self.rows(own, self.first, self.half - self.first), self.sems.at[5], place.across)
        sent(self.rows(own), self.sems.at[6], place.sibling)
        sent(self.rows(own), self.sems.at[7], place.sibling)


def extended_keys(kv, chip, rows, width, slots):
    count = kv.shape[0]
    lane = lax.broadcasted_iota(jnp.int32, (count, width), 1) - HEAD_DIM
    row = lax.broadcasted_iota(jnp.int32, (count, width), 0)
    block = rows // 2
    number = jnp.zeros_like(row)
    for edge in range(block, count, block):
        number = number + (row >= edge).astype(jnp.int32)
    hot = (lane == number + chip * (count // block)) | ((lane >= slots) & (lane < slots + 3))
    extra = jnp.where(hot, 1.0, 0.0).astype(BF16)
    if width == LANES:
        return jnp.where(lane < 0, kv, extra)
    first = jnp.where(lane[:, :LANES] < 0, kv, extra[:, :LANES])
    return jnp.concatenate([first, extra[:, LANES:]], axis=1)


def hide_later(scores, place, rows, first_query):
    count, width = scores.shape
    block = rows // 2
    key = lax.broadcasted_iota(jnp.int32, (count, 1), 0) - place.core * rows
    query = lax.broadcasted_iota(jnp.int32, (1, width), 1) + first_query
    query = query % rows
    end = jnp.where(query < block, block, rows)
    return jnp.where((key > query) & (key < end), NEGATIVE, scores)


def split_rows(values, at, count):
    one = values.astype(BF16).astype(F32)
    two = (values - one).astype(BF16).astype(F32)
    three = values - one - two
    row = lax.broadcasted_iota(jnp.int32, (count, values.shape[1]), 0) - at
    picked = jnp.where(row == 0, one, jnp.where(row == 1, two, jnp.where(row == 2, three, 0.0)))
    return picked.astype(BF16)


def attend_kernel(
    groups,
    slots,
    kv_own,
    qt,
    x_in,
    out_weight,
    gain,
    cot,
    kv_all,
    normed_all,
    cot_all,
    resid_out,
    att_out,
    ot_out,
    lse_out,
    s_buf,
    m_buf,
    l_buf,
    part_buf,
    part_send,
    part_recv,
    kv_recv,
    kv_z,
    kv_x,
    kv_sib,
    n_recv,
    n_part,
    n_sems,
    c_recv,
    c_part,
    c_sems,
    p_sems,
):
    place = Place(groups)
    rows = kv_own.shape[0]
    half = rows // 2
    span = 2 * rows
    width, queries = qt.shape
    block = queries // 2
    chunks = 2 * groups
    heads = out_weight.shape[0] // HEAD_DIM

    kv_all[pl.ds(place.seq * rows, rows), :] = kv_own[...]
    own_half = place.quad * 2 + place.tp
    cot_all[pl.ds(pl.multiple_of(own_half * half, 16), half), :] = cot[
        pl.ds(pl.multiple_of(place.tp * half, 16), half), :
    ]
    meet(place, True)

    def kv_rows(seq):
        return kv_all.at[pl.ds(pl.multiple_of(seq * rows, 16), rows)]

    own = kv_rows(place.seq)
    send(own, own, kv_sib.at[0], kv_recv.at[place.seq], place.sibling)
    for step in range(1, groups):
        other = place.in_group((place.group + step) % groups)
        send(own, own, kv_z.at[step - 1], kv_recv.at[place.seq], other)
    send(own, own, kv_x.at[0], kv_recv.at[place.seq], place.across)

    def chunk_place(number):
        far = number % 2
        group = (place.group + number // 2) % groups
        side = place.side + far * (1 - 2 * place.side)
        return group, side

    def pass_on(number):
        group, side = chunk_place(number)
        seq = place.seq_at(group, side, place.core)
        view = kv_rows(seq)
        arrived(view, kv_recv.at[seq], place.across)
        send(view, view, kv_sib.at[number], kv_recv.at[seq], place.sibling)

        @pl.when(number % 2 == 0)
        def near():
            send(view, view, kv_x.at[number // 2], kv_recv.at[seq], place.across)

    def ready(number):
        group, side = chunk_place(number)
        seq = place.seq_at(group, side, 1 - place.core)
        arrived(kv_rows(seq), kv_recv.at[seq], place.sibling)

    gather_cot = LayerGather(place, cot_all, half, c_recv, c_part, c_sems)
    gather_normed = LayerGather(place, normed_all, half, n_recv, n_part, n_sems)

    def kv_chunk(number):
        group, side = chunk_place(number)
        chip = group * 2 + side
        return chip, kv_all[pl.ds(pl.multiple_of(chip * span, 16), span), :]

    def scores(number, part, slot, own_chip=False):
        chip, kv = kv_chunk(number)
        keys = extended_keys(kv, chip, rows, width, slots)
        value = nn(keys, qt[:, part * block : (part + 1) * block])
        if own_chip:
            value = hide_later(value, place, rows, part * block)
        s_buf[slot] = value

    def absorb(number, part, slot, first=False):
        chip, kv = kv_chunk(number)
        lanes = slice(part * block, (part + 1) * block)
        value = s_buf[slot]
        top = jnp.max(value, axis=0, keepdims=True)
        if not first:
            old = m_buf[:, lanes]
            top = jnp.maximum(old, top)
            shrink = jnp.exp(old - top)
        weights = jnp.exp(value - top)
        total = jnp.sum(weights, axis=0, keepdims=True)
        product = tn(kv[:, HEAD_DIM:], weights.astype(BF16))
        if not first:
            total = total + l_buf[:, lanes] * shrink
            product = product + ot_out[:, lanes] * shrink
        m_buf[:, lanes] = top
        l_buf[:, lanes] = total
        ot_out[:, lanes] = product

    ready(0)
    scores(0, 0, 0, True)
    scores(0, 1, 1, True)
    absorb(0, 0, 0, True)
    pass_on(1)
    pass_on(2)
    ready(1)
    scores(1, 0, 0)
    absorb(0, 1, 1, True)

    def step(number, unused):
        scores(number, 1, 1)
        absorb(number, 0, 0)

        @pl.when(number + 2 < chunks)
        def look_ahead():
            pass_on(number + 2)

        @pl.when(number + 1 < chunks)
        def next_ready():
            ready(number + 1)

        @pl.when(number == 1)
        def cot_start():
            gather_cot.start()

        @pl.when(number == chunks - 3)
        def cot_middle():
            gather_cot.from_across()
            gather_cot.from_partner()

        scores(jnp.minimum(number + 1, chunks - 1), 0, 0)
        absorb(number, 1, 1)
        return unused

    lax.fori_loop(1, chunks, step, 0)

    ot = ot_out[...] / l_buf[...]
    ot_out[...] = ot
    lse_out[...] = m_buf[...] + jnp.log(l_buf[...])
    natural = jnp.transpose(ot).astype(BF16)
    att = jnp.concatenate(
        [natural[head * rows : (head + 1) * rows, :] for head in range(heads)], axis=1
    )
    att_out[...] = att
    part_buf[...] = nn(att, out_weight[...])
    other_rows = pl.ds(pl.multiple_of((1 - place.tp) * half, 16), half)
    my_rows = pl.ds(pl.multiple_of(place.tp * half, 16), half)
    part_send[...] = part_buf[other_rows, :].astype(BF16)
    send(part_send, part_recv, p_sems.at[0], p_sems.at[1], place.partner)
    gather_cot.diagonal()
    mine = part_buf[my_rows, :] + x_in[my_rows, :].astype(F32)
    arrived(part_recv, p_sems.at[1], place.partner)
    resid = mine + part_recv[...].astype(F32)
    resid_out[...] = resid
    factor = lax.rsqrt(jnp.mean(resid * resid, axis=-1, keepdims=True) + EPSILON)
    normed_all[pl.ds(pl.multiple_of(own_half * half, 16), half), :] = (
        resid * factor * gain[...]
    ).astype(BF16)
    gather_normed.start()
    gather_normed.from_across()
    gather_normed.from_partner()
    gather_normed.diagonal()
    gather_normed.finish()
    gather_cot.finish()
    sent(part_send, p_sems.at[0], place.partner)

    def close(number, unused):
        sent(own, kv_sib.at[number], place.sibling)
        return unused

    lax.fori_loop(0, chunks, close, 0)
    for step_out in range(groups):
        sent(own, kv_x.at[step_out], place.across)
    for step_out in range(1, groups):
        sent(own, kv_z.at[step_out - 1], place.in_group((place.group + step_out) % groups))


class ChainSum:
    def __init__(self, place, own, incoming, final, sems):
        self.place = place
        self.own, self.incoming, self.final = own, incoming, final
        self.count = own.shape[0]
        (
            self.up_recv,
            self.up_send,
            self.fin_recv,
            self.fin_send,
            self.x_recv,
            self.x_send,
            self.c_recv,
            self.c_send,
            self.keep,
        ) = sems

    def root(self, parity):
        return self.place.groups // 2 - 1 + parity

    def lag_up(self, parity):
        groups, group, root = self.place.groups, self.place.group, self.root(parity)
        most = max(root, groups - 1 - root)
        return PACE * jnp.where(
            group < root, group, jnp.where(group > root, groups - 1 - group, most)
        )

    def lag_down(self, parity):
        groups, group, root = self.place.groups, self.place.group, self.root(parity)
        most = max(root, groups - 1 - root)
        return PACE * (most + jnp.abs(group - root))

    def total_steps(self):
        groups = self.place.groups
        most = groups // 2
        return self.count + PACE * (2 * most + 1)

    def spread(self, i, view):
        place = self.place
        final = self.final.at[place.quad, i]
        send(view, final, self.x_send.at[i], self.x_recv.at[i], place.across)
        send(view, final, self.c_send.at[0, i], self.c_recv.at[0, i], place.sibling)

    def up(self, i, parity):
        place, root = self.place, self.root(parity)
        group, last = place.group, place.groups - 1
        mine = self.own.at[i]

        def add(way):
            neighbour = place.in_group(group - 1 + 2 * way)
            arrived(self.incoming.at[way, i], self.up_recv.at[way, i], neighbour)
            mine[...] = (mine[...].astype(F32) + self.incoming[way, i].astype(F32)).astype(BF16)

        def onward(way, dst, send_sem, recv_sem):
            send(mine, dst, send_sem, recv_sem, place.in_group(group + 1 - 2 * way))

        @pl.when((group > 0) & (group <= root))
        def from_left():
            add(0)

        @pl.when((group < last) & (group >= root))
        def from_right():
            add(1)

        @pl.when(group < root)
        def to_right():
            onward(0, self.incoming.at[0, i], self.up_send.at[i], self.up_recv.at[0, i])

        @pl.when(group > root)
        def to_left():
            onward(1, self.incoming.at[1, i], self.up_send.at[i], self.up_recv.at[1, i])

        @pl.when(group == root)
        def at_root():
            final = self.final.at[place.quad, i]

            @pl.when(group > 0)
            def left():
                onward(1, final, self.fin_send.at[0, i], self.fin_recv.at[i])

            @pl.when(group < last)
            def right():
                onward(0, final, self.fin_send.at[1, i], self.fin_recv.at[i])

            self.spread(i, mine)
            pltpu.make_async_copy(mine, final, self.keep.at[i]).start()

    def down(self, i, parity):
        place, root = self.place, self.root(parity)
        group, last = place.group, place.groups - 1
        view = self.final.at[place.quad, i]

        @pl.when(group != root)
        def take():
            arrived(view, self.fin_recv.at[i], place.sibling)

            @pl.when((group < root) & (group > 0))
            def left():
                send(
                    view,
                    view,
                    self.fin_send.at[0, i],
                    self.fin_recv.at[i],
                    place.in_group(group - 1),
                )

            @pl.when((group > root) & (group < last))
            def right():
                send(
                    view,
                    view,
                    self.fin_send.at[1, i],
                    self.fin_recv.at[i],
                    place.in_group(group + 1),
                )

            self.spread(i, view)

    def cross(self, i):
        place = self.place
        view = self.final.at[place.across[0] % QUAD, i]
        arrived(view, self.x_recv.at[i], place.across)
        send(view, view, self.c_send.at[1, i], self.c_recv.at[1, i], place.sibling)

    def step(self, number):
        for parity in (0, 1):
            i = number - self.lag_up(parity)

            @pl.when((i >= 0) & (i < self.count) & (i % 2 == parity))
            def go_up(i=i, parity=parity):
                self.up(i, parity)

        for parity in (0, 1):
            i = number - self.lag_down(parity)

            @pl.when((i >= 0) & (i < self.count) & (i % 2 == parity))
            def go_down(i=i, parity=parity):
                self.down(i, parity)

        for parity in (0, 1):
            i = number - self.lag_down(parity) - PACE

            @pl.when((i >= 0) & (i < self.count) & (i % 2 == parity))
            def go_cross(i=i):
                self.cross(i)

    def finish(self):
        place = self.place
        group, last = place.group, place.groups - 1
        sibling_quad = place.sibling[0] % QUAD
        diagonal = 3 - place.quad

        def close(i, unused):
            root = place.groups // 2 - 1 + i % 2
            view = self.own.at[i]
            arrived(self.final.at[sibling_quad, i], self.c_recv.at[0, i], place.sibling)
            arrived(self.final.at[diagonal, i], self.c_recv.at[1, i], place.sibling)

            @pl.when(group != root)
            def up_done():
                sent(view, self.up_send.at[i], place.sibling)

            @pl.when(group == root)
            def kept():
                final = self.final.at[place.quad, i]
                pltpu.make_async_copy(view, final, self.keep.at[i]).wait()

            @pl.when((group <= root) & (group > 0))
            def left_done():
                sent(view, self.fin_send.at[0, i], place.sibling)

            @pl.when((group >= root) & (group < last))
            def right_done():
                sent(view, self.fin_send.at[1, i], place.sibling)

            sent(view, self.x_send.at[i], place.across)
            sent(view, self.c_send.at[0, i], place.sibling)
            sent(view, self.c_send.at[1, i], place.sibling)
            return unused

        lax.fori_loop(0, self.count, close, 0)


def chain_sems(count):
    dma = pltpu.SemaphoreType.DMA
    return [
        dma((2, count)),
        dma((count,)),
        dma((count,)),
        dma((2, count)),
        dma((count,)),
        dma((count,)),
        dma((2, count)),
        dma((2, count)),
        dma((count,)),
    ]


class LayerSum:
    def __init__(self, place, part, half, core_in, left, right, left_in, right_in, last_in, sems):
        self.place, self.part, self.half = place, part, half
        self.core_in, self.left, self.right = core_in, left, right
        self.left_in, self.right_in, self.last_in = left_in, right_in, last_in
        self.sems = sems
        self.cut = left.shape[2]
        self.columns = part.shape[1]

    def rows(self, side, core):
        size = 2 * self.half
        return pl.ds(pl.multiple_of((side * 2 + core) * size, 16), size)

    def start(self):
        place = self.place
        for side in (0, 1):
            view = self.part.at[self.rows(side, 1 - place.core)]
            send(
                view,
                self.core_in.at[side],
                self.sems.at[side],
                self.sems.at[2 + side],
                place.sibling,
            )

    def own_rows(self, tp):
        return pl.ds(pl.multiple_of(tp * self.half, 16), self.half)

    def after_core(self):
        place = self.place
        for side in (0, 1):
            arrived(self.core_in.at[side], self.sems.at[2 + side], place.sibling)
            total = self.part[self.rows(side, place.core), :].astype(F32) + self.core_in[
                side
            ].astype(F32)
            self.left[side] = total[:, : self.cut].astype(BF16)
            self.right[side] = total[:, self.cut :].astype(BF16)

    def cross(self):
        place = self.place
        for side in (0, 1):
            send(
                self.left.at[side, self.own_rows(1 - place.tp)],
                self.left_in.at[side],
                self.sems.at[4 + side],
                self.sems.at[6 + side],
                place.partner,
            )
        send(
            self.right.at[1 - place.side],
            self.right_in,
            self.sems.at[8],
            self.sems.at[9],
            place.across,
        )

    def after_cross(self):
        place = self.place
        mine = self.own_rows(place.tp)
        for side in (0, 1):
            arrived(self.left_in.at[side], self.sems.at[6 + side], place.partner)
            self.left_in[side] = (
                self.left[side, mine, :].astype(F32) + self.left_in[side].astype(F32)
            ).astype(BF16)
        arrived(self.right_in, self.sems.at[9], place.across)
        self.right_in[...] = (
            self.right[place.side].astype(F32) + self.right_in[...].astype(F32)
        ).astype(BF16)
        send(
            self.left_in.at[1 - place.side],
            self.last_in.at[:, : self.cut],
            self.sems.at[10],
            self.sems.at[11],
            place.across,
        )
        send(
            self.right_in.at[self.own_rows(1 - place.tp)],
            self.last_in.at[:, self.cut :],
            self.sems.at[12],
            self.sems.at[13],
            place.partner,
        )

    def result(self):
        place = self.place
        arrived(self.last_in.at[:, : self.cut], self.sems.at[11], place.across)
        arrived(self.last_in.at[:, self.cut :], self.sems.at[13], place.partner)
        mine = jnp.concatenate(
            [self.left_in[place.side], self.right_in[self.own_rows(place.tp), :]], axis=1
        )
        return mine.astype(F32) + self.last_in[...].astype(F32)

    def finish(self):
        place = self.place
        for side in (0, 1):
            sent(self.core_in.at[side], self.sems.at[side], place.sibling)
            sent(self.left_in.at[side], self.sems.at[4 + side], place.partner)
        sent(self.right_in, self.sems.at[8], place.across)
        sent(self.last_in.at[:, : self.cut], self.sems.at[10], place.across)
        sent(self.last_in.at[:, self.cut :], self.sems.at[12], place.partner)


class QuadSum:
    def __init__(self, place, part, own, core_in, x_send, x_in, sems):
        self.place, self.part, self.own = place, part, own
        self.core_in, self.x_send, self.x_in, self.sems = core_in, x_send, x_in, sems

    def start(self):
        place = self.place
        for side in (0, 1):
            send(
                self.part.at[side * 2 + 1 - place.core],
                self.core_in.at[side],
                self.sems.at[side],
                self.sems.at[2 + side],
                place.sibling,
            )

    def total(self, side):
        return self.part[side * 2 + self.place.core].astype(F32) + self.core_in[side].astype(F32)

    def middle(self):
        place = self.place
        for side in (0, 1):
            arrived(self.core_in.at[side], self.sems.at[2 + side], place.sibling)
        self.x_send[...] = self.total(1 - place.side).astype(BF16)
        send(self.x_send, self.x_in, self.sems.at[4], self.sems.at[5], place.across)

    def end(self):
        place = self.place
        arrived(self.x_in, self.sems.at[5], place.across)
        mine = (self.total(place.side) + self.x_in[...].astype(F32)).astype(BF16)
        count, step = self.own.shape[0], self.own.shape[1]
        for i in range(count):
            piece = mine[i * step : (i + 1) * step, :]
            if piece.shape[0]:
                self.own[i, : piece.shape[0], :] = piece
            if piece.shape[0] < step:
                left = step - piece.shape[0]
                self.own[i, piece.shape[0] :, :] = jnp.zeros((left, piece.shape[1]), BF16)

    def finish(self):
        place = self.place
        for side in (0, 1):
            sent(self.core_in.at[side], self.sems.at[side], place.sibling)
        sent(self.x_send, self.sems.at[4], place.across)


class ColumnSum:
    def __init__(self, place, own, incoming, final, sems):
        self.place, self.own, self.incoming, self.final = place, own, incoming, final
        self.rs_send, self.rs_recv, self.ag_send, self.ag_recv = (sems.at[i] for i in range(4))
        self.x_send, self.x_recv, self.c_send, self.c_recv = (sems.at[i] for i in range(4, 8))
        self.d_send, self.d_recv = (sems.at[i] for i in range(8, 10))

    def others(self):
        place = self.place
        for step in range(1, place.groups):
            yield step, (place.group + step) % place.groups

    def start(self):
        place = self.place
        for step, other in self.others():
            back = place.groups - step
            send(
                self.own.at[other],
                self.incoming.at[back],
                self.rs_send.at[step],
                self.rs_recv.at[back],
                place.in_group(other),
            )

    def spread(self, part, view):
        place = self.place
        final = self.final.at[place.quad, part]
        send(view, final, self.x_send.at[part], self.x_recv.at[part], place.across)
        send(view, final, self.c_send.at[part], self.c_recv.at[part], place.sibling)

    def middle(self):
        place = self.place
        mine = self.own.at[place.group]
        total = mine[...].astype(F32)
        for step, other in self.others():
            arrived(self.incoming.at[step], self.rs_recv.at[step], place.sibling)
            total = total + self.incoming[step].astype(F32)
        mine[...] = total.astype(BF16)
        final = self.final.at[place.quad, place.group]
        for step, other in self.others():
            send(
                mine,
                final,
                self.ag_send.at[step],
                self.ag_recv.at[place.group],
                place.in_group(other),
            )
        self.spread(place.group, mine)
        pltpu.make_async_copy(mine, final, self.ag_send.at[0]).start()

    def end(self):
        place = self.place
        for step, other in self.others():
            view = self.final.at[place.quad, other]
            arrived(view, self.ag_recv.at[other], place.sibling)
            self.spread(other, view)

    def cross(self):
        place = self.place
        quad = place.across[0] % QUAD
        for step in range(place.groups):
            part = (place.group + step) % place.groups
            view = self.final.at[quad, part]
            arrived(view, self.x_recv.at[part], place.across)
            send(view, view, self.d_send.at[part], self.d_recv.at[part], place.sibling)

    def finish(self):
        place = self.place
        view = self.own.at[0]
        for part in range(place.groups):
            arrived(view, self.c_recv.at[part], place.sibling)
            arrived(view, self.d_recv.at[part], place.sibling)
            sent(view, self.x_send.at[part], place.across)
            sent(view, self.c_send.at[part], place.sibling)
            sent(view, self.d_send.at[part], place.sibling)
        for step, other in self.others():
            sent(view, self.rs_send.at[step], place.sibling)
            sent(view, self.ag_send.at[step], place.sibling)
        final = self.final.at[place.quad, place.group]
        pltpu.make_async_copy(self.own.at[place.group], final, self.ag_send.at[0]).wait()


def column_parts(groups, rows, columns):
    return (groups, round_up(-(-rows // groups), 16), columns)


def column_sum_scratch(groups, rows, columns):
    parts = column_parts(groups, rows, columns)
    return [
        *quad_sum_scratch(rows, columns),
        pltpu.VMEM(parts, BF16),
        pltpu.VMEM(parts, BF16),
        pltpu.SemaphoreType.DMA((10, groups)),
    ]


def quad_sum_scratch(rows, columns):
    return [
        pltpu.VMEM((QUAD, rows, columns), BF16),
        pltpu.VMEM((2, rows, columns), BF16),
        pltpu.VMEM((rows, columns), BF16),
        pltpu.VMEM((rows, columns), BF16),
        pltpu.SemaphoreType.DMA((6,)),
    ]


def layer_sum_scratch(half, columns):
    cut = columns // LANES // 2 * LANES
    if cut * 2 < columns:
        cut += LANES
    return [
        pltpu.VMEM((2, 2 * half, columns), BF16),
        pltpu.VMEM((2, 2 * half, cut), BF16),
        pltpu.VMEM((2, 2 * half, columns - cut), BF16),
        pltpu.VMEM((2, half, cut), BF16),
        pltpu.VMEM((2 * half, columns - cut), BF16),
        pltpu.VMEM((half, columns), BF16),
        pltpu.SemaphoreType.DMA((14,)),
    ]


def backward_kernel(
    groups,
    slots,
    grad_part,
    mlp_part,
    wide_in,
    tall_in,
    resid_in,
    cot,
    gain,
    out_weight,
    att,
    ot,
    lse,
    qt_in,
    kv_all,
    x_in,
    attn_gain,
    weights_in,
    cosine,
    sine,
    layer_out,
    input_grad,
    wide,
    tall,
    outs,
    ins_q,
    ins_kv,
    gains,
    biases,
    *scratch,
):
    place = Place(groups)
    wide_own, tall_own, wide_up, tall_up = scratch[0:4]
    wide_sems, tall_sems = scratch[4:13], scratch[13:22]
    sum_g, sum_m = scratch[22:29], scratch[29:36]
    branch, qt, dot_t, q_pad, do_pad, dkv = scratch[36:42]
    sib_send, sib_in, side_send, side_in, z_send, z_in = scratch[42:48]
    kv_sems, pair_sems = scratch[48:50]
    dq_out, dkv_out, resid_grad = scratch[50:53]
    turn_send, turn_in, gain_in, bias_in, gain_z, bias_z, vector_sems = scratch[53:60]
    sum_o, sum_q, sum_kv = scratch[60:68], scratch[68:76], scratch[76:84]
    rows = att.shape[0]
    half = rows // 2
    span = 2 * rows
    width, queries = qt_in.shape
    block = queries // 2
    chunks = 2 * groups
    heads = out_weight.shape[0] // HEAD_DIM
    my_rows = pl.ds(pl.multiple_of(place.tp * half, 16), half)
    other_rows = pl.ds(pl.multiple_of((1 - place.tp) * half, 16), half)

    grad_sum = LayerSum(place, grad_part, half, *sum_g)
    mlp_sum = LayerSum(place, mlp_part, half, *sum_m)
    tall_sum = ChainSum(place, tall_own, tall_up, tall, tall_sems)
    wide_sum = ChainSum(place, wide_own, wide_up, wide, wide_sems)
    fills = [
        pltpu.make_async_copy(tall_in, tall_own, pair_sems.at[4]),
        pltpu.make_async_copy(wide_in, wide_own, pair_sems.at[5]),
    ]
    for fill in fills:
        fill.start()

    def quad_and_column(final, refs):
        quad = QuadSum(place, refs[0], refs[5], *refs[1:5])
        return quad, ColumnSum(place, refs[5], refs[6], final, refs[7])

    outs_quad, outs_sum = quad_and_column(outs, sum_o)
    q_quad, q_sum = quad_and_column(ins_q, sum_q)
    kv_quad, kv_sum = quad_and_column(ins_kv, sum_kv)
    tall_steps = tall_sum.count

    def chain_step(number):
        tall_sum.step(number)
        wide_sum.step(number - tall_steps)

    def chain_steps(first, count):
        def one(number, unused):
            chain_step(number)
            return unused

        lax.fori_loop(first, first + count, one, 0)
        return first + count

    all_steps = tall_steps + wide_sum.total_steps()

    meet(place, True)
    grad_sum.start()
    for fill in fills:
        fill.wait()
    done = chain_steps(0, SHARE[0])

    qt[...] = qt_in[...]
    at = HEAD_DIM + slots
    qt[at : at + 16, :] = split_rows(-lse[...], 0, 16)
    natural_q = jnp.transpose(qt_in[0:HEAD_DIM, :].astype(F32)).astype(BF16)
    q_pad[...] = jnp.concatenate([natural_q, jnp.zeros_like(natural_q)], axis=1)

    grad_sum.after_core()
    grad_sum.cross()
    mlp_sum.start()
    done = chain_steps(done, SHARE[1])
    grad_sum.after_cross()
    done = chain_steps(done, SHARE[2])

    resid = resid_in[...]
    factor = lax.rsqrt(jnp.mean(resid * resid, axis=-1, keepdims=True) + EPSILON)
    normed = resid * factor
    grad_normed = grad_sum.result()
    features = resid.shape[1]
    gains[:, features:] = jnp.sum(grad_normed * normed, axis=0, keepdims=True)
    weighted = grad_normed * gain[...]
    inner = jnp.mean(weighted * normed, axis=-1, keepdims=True)
    grad_resid = cot[my_rows, :].astype(F32) + factor * (weighted - normed * inner)
    resid_grad[...] = grad_resid
    branch[my_rows, :] = grad_resid.astype(BF16)
    send(
        branch.at[my_rows],
        branch.at[my_rows],
        pair_sems.at[0],
        pair_sems.at[1],
        place.partner,
    )
    mlp_sum.after_core()
    mlp_sum.cross()
    done = chain_steps(done, SHARE[3])
    arrived(branch.at[other_rows], pair_sems.at[1], place.partner)

    grads = branch[...]
    outs_part = sum_o[0]
    outs_part[...] = tn(att[...], grads).astype(BF16).reshape(outs_part.shape)
    outs_quad.start()
    grad_att = nt(grads, out_weight[...]).astype(BF16)
    stacked = jnp.concatenate(
        [grad_att[:, head * HEAD_DIM : (head + 1) * HEAD_DIM] for head in range(heads)]
        + [jnp.zeros((queries - heads * rows, HEAD_DIM), BF16)],
        axis=0,
    )
    do_pad[...] = jnp.concatenate([jnp.zeros_like(stacked), stacked], axis=1)
    turned = jnp.transpose(stacked.astype(F32))
    delta = jnp.sum(turned * ot[...], axis=0, keepdims=True)
    dot_t[0:HEAD_DIM, :] = split_rows(-delta, 0, HEAD_DIM)
    dot_t[HEAD_DIM:, :] = turned.astype(BF16)
    done = chain_steps(done, SHARE[4])
    outs_quad.middle()

    def write_layer():
        layer_out[my_rows, :] = (resid_in[...] + mlp_sum.result()).astype(BF16)
        send(
            layer_out.at[my_rows],
            layer_out.at[my_rows],
            pair_sems.at[2],
            pair_sems.at[3],
            place.partner,
        )

    dq_out[...] = jnp.zeros_like(dq_out)

    def chunk_place(number):
        far = 1 - number % 2
        group = (place.group + 1 + number // 2) % groups
        side = place.side + far * (1 - 2 * place.side)
        return group, side

    lane = lax.broadcasted_iota(jnp.int32, (1, LANES), 1)
    ones = jnp.where(lane < 3, 1.0, 0.0).astype(BF16)

    def attend_back(number, slot, own_chip=False):
        group, side = chunk_place(number)
        chip = group * 2 + side
        at_rows = pl.ds(pl.multiple_of(chip * span, 16), span)
        kv = kv_all[at_rows, :]
        keys = extended_keys(kv, chip, rows, width, slots)
        values = jnp.where(lane >= HEAD_DIM, kv, jnp.broadcast_to(ones, kv.shape))
        for part in range(2):
            lanes = slice(part * block, (part + 1) * block)
            score = nn(keys, qt[:, lanes])
            if own_chip:
                score = hide_later(score, place, rows, part * block)
            weights = jnp.exp(score)
            change = nn(values, dot_t[:, lanes])
            low = (weights * change).astype(BF16)
            total = nn(weights.astype(BF16), do_pad[lanes, :]) + nn(low, q_pad[lanes, :])
            if part == 0:
                dkv[slot] = total
            else:
                dkv[slot] += total
            dq_out[:, lanes] += tn(kv[:, :HEAD_DIM], low)

    def hand_over(number, slot):
        other = pl.ds(pl.multiple_of((1 - place.core) * rows, 16), rows)
        sib_send[number] = dkv[slot, other, :].astype(BF16)
        send(
            sib_send.at[number],
            sib_in.at[number],
            kv_sems.at[0, number],
            kv_sems.at[1, number],
            place.sibling,
        )

    def take_over(number, near, own_group=False):
        group, side = chunk_place(number)
        step = number // 2
        arrived(sib_in.at[number], kv_sems.at[1, number], place.sibling)
        mine = pl.ds(pl.multiple_of(place.core * rows, 16), rows)
        total = dkv[1 if near else 0, mine, :] + sib_in[number].astype(F32)
        if not near:
            side_send[step] = total.astype(BF16)
            send(
                side_send.at[step],
                side_in.at[step],
                kv_sems.at[2, step],
                kv_sems.at[3, step],
                place.across,
            )
            return
        arrived(side_in.at[step], kv_sems.at[3, step], place.across)
        total = total + side_in[step].astype(F32)
        if own_group:
            dkv_out[...] = total
            return
        z_send[step] = total.astype(BF16)
        back = groups - 2 - step
        send(
            z_send.at[step],
            z_in.at[back],
            kv_sems.at[4, step],
            kv_sems.at[5, back],
            place.in_group(group),
        )

    each = 2

    def pair(step, unused):
        attend_back(2 * step, 0)
        hand_over(2 * step, 0)
        chain_steps(done + 2 * each * step, each)

        @pl.when(step > 0)
        def last_near():
            take_over(2 * step - 1, True)

        attend_back(2 * step + 1, 1)
        hand_over(2 * step + 1, 1)
        take_over(2 * step, False)
        chain_steps(done + 2 * each * step + each, each)

        @pl.when(step == 0)
        def outs_ready():
            mlp_sum.after_cross()
            outs_quad.end()
            outs_sum.start()

        @pl.when(step == 1)
        def layer_ready():
            write_layer()
            outs_sum.middle()

        return unused

    lax.fori_loop(0, groups - 1, pair, 0)
    outs_sum.end()
    done += 2 * each * (groups - 1)
    attend_back(chunks - 2, 0)
    hand_over(chunks - 2, 0)
    done = chain_steps(done, each)
    if groups > 1:
        take_over(chunks - 3, True)
    attend_back(chunks - 1, 1, True)
    hand_over(chunks - 1, 1)
    take_over(chunks - 2, False)
    done = chain_steps(done, SHARE[5])

    quarter = HEAD_DIM // 2
    raw = dq_out[...] * HEAD_DIM**-0.5
    one, two = raw[:quarter, :], raw[quarter:, :]
    cos, sin = cosine[...], sine[...]
    turned = jnp.concatenate([one * cos + two * sin, two * cos - one * sin], axis=0)
    natural = jnp.transpose(turned).astype(BF16)
    grad_query = jnp.concatenate(
        [natural[head * rows : (head + 1) * rows, :] for head in range(heads)], axis=1
    )
    x_all = x_in[...].astype(F32)
    factor_all = lax.rsqrt(jnp.mean(x_all * x_all, axis=-1, keepdims=True) + EPSILON)
    normed_attn = (x_all * factor_all * attn_gain[...]).astype(BF16)
    wide_q = grad_query.shape[1]
    q_part = sum_q[0]
    q_part[...] = tn(normed_attn, grad_query).astype(BF16).reshape(q_part.shape)
    q_quad.start()
    turn_send[...] = nt(grad_query, weights_in[:, :wide_q])
    biases[...] = jnp.zeros_like(biases)
    biases[:, :wide_q] = jnp.sum(grad_query.astype(F32), axis=0, keepdims=True)
    done = chain_steps(done, SHARE[11])
    take_over(chunks - 1, True, True)
    q_quad.middle()
    outs_sum.cross()
    done = chain_steps(done, SHARE[6])
    for step in range(groups - 1):
        arrived(z_in.at[step], kv_sems.at[5, step], place.sibling)
        dkv_out[...] += z_in[step].astype(F32)
    turned = jnp.transpose(dkv_out[...])
    one, two = turned[:quarter, :], turned[quarter:HEAD_DIM, :]
    cos, sin = cosine[:, :rows], sine[:, :rows]
    turned = jnp.concatenate(
        [one * cos + two * sin, two * cos - one * sin, turned[HEAD_DIM:, :]], axis=0
    )
    grad_kv = jnp.transpose(turned).astype(BF16)
    kv_part = sum_kv[0]
    kv_part[...] = tn(normed_attn, grad_kv).astype(BF16).reshape(kv_part.shape)
    kv_quad.start()
    turn_send[...] += nt(grad_kv, weights_in[:, wide_q:])
    turn_in[0] = turn_send[other_rows, :].astype(BF16)
    send(turn_in.at[0], turn_in.at[1], vector_sems.at[0], vector_sems.at[1], place.partner)
    biases[:, wide_q : wide_q + LANES] = jnp.sum(grad_kv.astype(F32), axis=0, keepdims=True)
    done = chain_steps(done, SHARE[12])
    kv_quad.middle()
    q_quad.end()
    q_sum.start()
    done = chain_steps(done, SHARE[7])
    kv_quad.end()
    kv_sum.start()
    x_half = x_in[my_rows, :].astype(F32)
    factor = lax.rsqrt(jnp.mean(x_half * x_half, axis=-1, keepdims=True) + EPSILON)
    normed = x_half * factor
    done = chain_steps(done, SHARE[13])
    arrived(turn_in.at[1], vector_sems.at[1], place.partner)
    grad_normed = turn_send[my_rows, :] + turn_in[1].astype(F32)
    gains[:, :features] = jnp.sum(grad_normed * normed, axis=0, keepdims=True)
    weighted = grad_normed * attn_gain[...]
    mean = jnp.mean(weighted * normed, axis=-1, keepdims=True)
    input_grad[my_rows, :] = (
        resid_grad[...] + factor * (weighted - normed * mean)
    ).astype(BF16)

    def vectors(hop, device, with_biases):
        send(gains, gain_in.at[hop], vector_sems.at[4 + 4 * hop], vector_sems.at[5 + 4 * hop], device)
        if with_biases:
            send(
                biases,
                bias_in.at[hop],
                vector_sems.at[6 + 4 * hop],
                vector_sems.at[7 + 4 * hop],
                device,
            )

    def vectors_done(hop, device, with_biases):
        arrived(gain_in.at[hop], vector_sems.at[5 + 4 * hop], device)
        sent(gains, vector_sems.at[4 + 4 * hop], device)
        gains[...] += gain_in[hop]
        if with_biases:
            arrived(bias_in.at[hop], vector_sems.at[7 + 4 * hop], device)
            sent(biases, vector_sems.at[6 + 4 * hop], device)
            biases[...] += bias_in[hop]

    hops = ((place.partner, False), (place.sibling, True), (place.across, True))
    vectors(0, *hops[0])
    send(
        input_grad.at[my_rows],
        input_grad.at[my_rows],
        vector_sems.at[2],
        vector_sems.at[3],
        place.partner,
    )
    done = chain_steps(done, SHARE[14])
    q_sum.middle()
    vectors_done(0, *hops[0])
    vectors(1, *hops[1])
    kv_sum.middle()
    done = chain_steps(done, SHARE[8])
    vectors_done(1, *hops[1])
    vectors(2, *hops[2])
    done = chain_steps(done, SHARE[9])
    vectors_done(2, *hops[2])
    gain_z[place.group] = gains[...]
    bias_z[place.group] = biases[...]
    base = 16
    for step in range(1, groups):
        other = place.in_group((place.group + step) % groups)
        for number, ref in enumerate((gain_z, bias_z)):
            send(
                ref.at[place.group],
                ref.at[place.group],
                vector_sems.at[base + 4 * step + 2 * number],
                vector_sems.at[base + 4 * (groups - step) + 2 * number + 1],
                other,
            )
    q_sum.end()
    kv_sum.end()
    done = chain_steps(done, SHARE[10])
    q_sum.cross()
    kv_sum.cross()
    for step in range(1, groups):
        other = (place.group + groups - step) % groups
        for number, ref in enumerate((gain_z, bias_z)):
            arrived(
                ref.at[other],
                vector_sems.at[base + 4 * (groups - step) + 2 * number + 1],
                place.sibling,
            )
            sent(
                ref.at[place.group],
                vector_sems.at[base + 4 * step + 2 * number],
                place.sibling,
            )
    gains[...] = jnp.sum(gain_z[...], axis=0)
    biases[...] = jnp.sum(bias_z[...], axis=0)

    def last(number, unused):
        chain_step(number)
        return unused

    lax.fori_loop(done, all_steps, last, 0)

    arrived(input_grad.at[other_rows], vector_sems.at[3], place.partner)
    sent(input_grad.at[my_rows], vector_sems.at[2], place.partner)
    sent(turn_in.at[0], vector_sems.at[0], place.partner)
    for part in (outs_quad, q_quad, kv_quad, outs_sum, q_sum, kv_sum):
        part.finish()
    arrived(layer_out.at[other_rows], pair_sems.at[3], place.partner)
    sent(branch.at[my_rows], pair_sems.at[0], place.partner)
    sent(branch.at[my_rows], pair_sems.at[2], place.partner)
    grad_sum.finish()
    mlp_sum.finish()
    tall_sum.finish()
    wide_sum.finish()
    for number in range(chunks):
        sent(sib_send.at[number], kv_sems.at[0, number], place.sibling)
    for step in range(groups):
        sent(side_send.at[step], kv_sems.at[2, step], place.across)
    for step in range(groups - 1):
        sent(z_send.at[step], kv_sems.at[4, step], place.sibling)


def vmem_specs(count):
    return [pl.BlockSpec(memory_space=pltpu.VMEM)] * count


def params(collective):
    return pltpu.CompilerParams(
        collective_id=collective, has_side_effects=True, vmem_limit_bytes=VMEM_LIMIT
    )


def attend(groups, slots, kv_own, qt, x_in, out_weight, gain, cot):
    rows, features = x_in.shape
    half = rows // 2
    total = groups * QUAD * rows
    width, queries = qt.shape
    dma = pltpu.SemaphoreType.DMA
    shape = jax.ShapeDtypeStruct
    return pl.pallas_call(
        functools.partial(attend_kernel, groups, slots),
        out_shape=[
            shape((total, LANES), BF16),
            shape((QUAD * rows, features), BF16),
            shape((QUAD * rows, features), BF16),
            shape((half, features), F32),
            shape((rows, out_weight.shape[0]), BF16),
            shape((HEAD_DIM, queries), F32),
            shape((1, queries), F32),
        ],
        in_specs=vmem_specs(6),
        out_specs=vmem_specs(7),
        scratch_shapes=[
            pltpu.VMEM((2, 2 * rows, queries // 2), F32),
            pltpu.VMEM((1, queries), F32),
            pltpu.VMEM((1, queries), F32),
            pltpu.VMEM((rows, features), F32),
            pltpu.VMEM((half, features), BF16),
            pltpu.VMEM((half, features), BF16),
            dma((groups * QUAD,)),
            dma((groups,)),
            dma((groups,)),
            dma((2 * groups,)),
            dma((8,)),
            dma((2,)),
            dma((8,)),
            dma((8,)),
            dma((2,)),
            dma((8,)),
            dma((2,)),
        ],
        compiler_params=params(1),
        name="attend",
    )(kv_own, qt, x_in, out_weight, gain, cot)


def backward(groups, slots, operands):
    (grad_part, mlp_part, wide, tall, resid, cot, gain, out_weight, att, ot, lse, qt, kv_all) = (
        operands[:13]
    )
    weights_in = operands[15]
    rows, inner = att.shape
    half = rows // 2
    features = grad_part.shape[1]
    width, queries = qt.shape
    chunks = 2 * groups
    both = round_up(weights_in.shape[1], LANES)
    dma = pltpu.SemaphoreType.DMA
    shape = jax.ShapeDtypeStruct
    pass_shape = (rows, LANES)
    outs = (inner // QUAD, features)
    ins_q = (features // QUAD, inner)
    ins_kv = (features // QUAD, weights_in.shape[1] - inner)
    return pl.pallas_call(
        functools.partial(backward_kernel, groups, slots),
        out_shape=[
            shape((rows, features), BF16),
            shape((rows, features), BF16),
            shape((QUAD, *wide.shape), BF16),
            shape((QUAD, *tall.shape), BF16),
            *(shape((QUAD, *column_parts(groups, *dims)), BF16) for dims in (outs, ins_q, ins_kv)),
            shape((1, 2 * features), F32),
            shape((1, both), F32),
        ],
        in_specs=vmem_specs(2) + [pl.BlockSpec(memory_space=pl.ANY)] * 2 + vmem_specs(14),
        out_specs=vmem_specs(2) + [pl.BlockSpec(memory_space=pl.ANY)] * 5 + vmem_specs(2),
        scratch_shapes=[
            pltpu.VMEM(wide.shape, BF16),
            pltpu.VMEM(tall.shape, BF16),
            pltpu.VMEM((2, *wide.shape), BF16),
            pltpu.VMEM((2, *tall.shape), BF16),
            *chain_sems(wide.shape[0]),
            *chain_sems(tall.shape[0]),
            *layer_sum_scratch(half, features),
            *layer_sum_scratch(half, features),
            pltpu.VMEM((rows, features), BF16),
            pltpu.VMEM((width, queries), BF16),
            pltpu.VMEM((LANES, queries), BF16),
            pltpu.VMEM((queries, LANES), BF16),
            pltpu.VMEM((queries, LANES), BF16),
            pltpu.VMEM((2, 2 * rows, LANES), F32),
            pltpu.VMEM((chunks, *pass_shape), BF16),
            pltpu.VMEM((chunks, *pass_shape), BF16),
            pltpu.VMEM((groups, *pass_shape), BF16),
            pltpu.VMEM((groups, *pass_shape), BF16),
            pltpu.VMEM((groups, *pass_shape), BF16),
            pltpu.VMEM((groups, *pass_shape), BF16),
            dma((6, chunks)),
            dma((6,)),
            pltpu.VMEM((HEAD_DIM, queries), F32),
            pltpu.VMEM((rows, LANES), F32),
            pltpu.VMEM((half, features), F32),
            pltpu.VMEM((rows, features), F32),
            pltpu.VMEM((2, half, features), BF16),
            pltpu.VMEM((3, 1, 2 * features), F32),
            pltpu.VMEM((3, 1, both), F32),
            pltpu.VMEM((groups, 1, 2 * features), F32),
            pltpu.VMEM((groups, 1, both), F32),
            dma((16 + 4 * groups + 4,)),
            *column_sum_scratch(groups, *outs),
            *column_sum_scratch(groups, *ins_q),
            *column_sum_scratch(groups, *ins_kv),
        ],
        compiler_params=params(2),
        name="backward",
    )(*operands)


def rope_tables(positions, head_size):
    half_size = head_size // 2
    exponent = jnp.arange(half_size, dtype=F32) * (2.0 / head_size)
    frequency = jnp.power(ROPE_BASE, -exponent)
    angle = positions.astype(F32)[:, None] * frequency[None, :]
    return (jnp.cos(angle)[:, None, :], jnp.sin(angle)[:, None, :])


def rotate(values, cosine, sine):
    half_size = values.shape[-1] // 2
    first = values[..., :half_size]
    second = values[..., half_size:]
    return jnp.concatenate(
        [first * cosine - second * sine, second * cosine + first * sine], axis=-1
    )


def piece_of(weight, axis, piece, quad):
    pads = [(0, 0, 0), (0, 0, 0)]
    pads[axis] = (0, piece * QUAD - weight.shape[axis], 0)
    padded = lax.pad(weight, jnp.zeros((), weight.dtype), pads)
    return lax.dynamic_slice_in_dim(padded, quad * piece, piece, axis)


def per_device(
    groups,
    layer_input,
    block_order,
    attn_gain,
    query_weight,
    query_bias,
    key_weight,
    key_bias,
    value_weight,
    value_bias,
    out_weight,
    mlp_gain,
    gate_weight,
    up_weight,
    down_weight,
    out_cotangent,
):
    rows, features = layer_input.shape
    block_rows = rows // 2
    slots = block_order.shape[0]
    hidden = gate_weight.shape[1]
    heads = query_weight.shape[1] // HEAD_DIM
    piece = round_up(hidden // LANES, QUAD) // QUAD * LANES
    queries = round_up(heads * rows, 2 * LANES)
    width = round_up(HEAD_DIM + slots + 16, LANES)
    scale = HEAD_DIM ** (-0.5)
    seq_index = lax.axis_index("seq")
    quad = seq_index % QUAD
    tp_index = lax.axis_index("tp")
    own_slots = lax.dynamic_slice_in_dim(block_order, 2 * seq_index, 2)
    steps_in = jnp.arange(block_rows, dtype=jnp.int32)
    own_places = (own_slots[:, None] * block_rows + steps_in[None, :]).reshape(-1)
    cosine, sine = rope_tables(own_places, HEAD_DIM)
    inputs = layer_input.astype(F32)
    factor_first = lax.rsqrt(jnp.mean(inputs * inputs, axis=-1, keepdims=True) + EPSILON)
    normed_first = inputs * factor_first
    normed_attn = (normed_first * attn_gain).astype(BF16)
    query_rows = (
        jnp.dot(normed_attn, query_weight, preferred_element_type=F32) + query_bias
    ).reshape(rows, heads, HEAD_DIM)
    key_rows = (jnp.dot(normed_attn, key_weight, preferred_element_type=F32) + key_bias).reshape(
        rows, 1, HEAD_DIM
    )
    value_rows = (
        jnp.dot(normed_attn, value_weight, preferred_element_type=F32) + value_bias
    ).astype(BF16)
    query_rot = rotate(query_rows, cosine, sine).astype(BF16)
    key_rot = rotate(key_rows, cosine, sine).astype(BF16).reshape(rows, HEAD_DIM)
    kv_own = jnp.concatenate([key_rot, value_rows], axis=1)
    query_t = jnp.transpose(query_rot * jnp.asarray(scale, BF16), (2, 1, 0)).reshape(
        HEAD_DIM, heads * rows
    )
    later = block_order[:, None] > jnp.repeat(own_slots, block_rows)[None, :]
    bias = jnp.tile(jnp.where(later, NEGATIVE, 0.0).astype(BF16), (1, heads))
    qt = jnp.concatenate(
        [query_t, bias, jnp.zeros((width - HEAD_DIM - slots, heads * rows), BF16)], axis=0
    )
    qt = jnp.pad(qt, ((0, 0), (0, queries - heads * rows)))
    gain_row = mlp_gain[None, :]

    kv_all, normed_all, cot_all, resid, att, ot, lse = attend(
        groups, slots, kv_own, qt, layer_input, out_weight, gain_row, out_cotangent
    )

    gate_piece = piece_of(gate_weight, 1, piece, quad)
    up_piece = piece_of(up_weight, 1, piece, quad)
    down_piece = piece_of(down_weight, 0, piece, quad)
    gate = jnp.dot(normed_all, gate_piece, preferred_element_type=F32)
    upward = jnp.dot(normed_all, up_piece, preferred_element_type=F32)
    sigmoid_gate = jax.nn.sigmoid(gate)
    silu_gate = gate * sigmoid_gate
    mixed = (silu_gate * upward).astype(BF16)
    mlp_part = jnp.dot(mixed, down_piece, preferred_element_type=F32).astype(BF16)
    down_grad = jnp.einsum("rf,rd->fd", mixed, cot_all, preferred_element_type=F32).astype(BF16)
    grad_mixed = jnp.einsum("rd,fd->rf", cot_all, down_piece, preferred_element_type=F32)
    grad_gate = (grad_mixed * upward * sigmoid_gate * (1.0 + gate * (1.0 - sigmoid_gate))).astype(
        BF16
    )
    grad_upward = (grad_mixed * silu_gate).astype(BF16)
    gate_grad = jnp.einsum("rd,rf->df", normed_all, grad_gate, preferred_element_type=F32)
    up_grad = jnp.einsum("rd,rf->df", normed_all, grad_upward, preferred_element_type=F32)
    grad_part = (
        jnp.einsum("rf,df->rd", grad_gate, gate_piece, preferred_element_type=F32)
        + jnp.einsum("rf,df->rd", grad_upward, up_piece, preferred_element_type=F32)
    ).astype(BF16)
    wide = jnp.concatenate([gate_grad.astype(BF16), up_grad.astype(BF16)], axis=0).reshape(
        2 * features // WIDE_ROWS, WIDE_ROWS, piece
    )
    tall = down_grad.reshape(piece // TALL_ROWS, TALL_ROWS, features)
    weights_in = jnp.concatenate([query_weight, key_weight, value_weight], axis=1)
    tables = tuple(
        jnp.pad(
            jnp.tile(jnp.transpose(table[:, 0, :]), (1, heads)),
            ((0, 0), (0, queries - heads * rows)),
        )
        for table in (cosine, sine)
    )
    layer_output, input_grad, wide_sum, tall_sum, outs, ins_q, ins_kv, gains, biases = backward(
        groups,
        slots,
        (
            grad_part, mlp_part, wide, tall, resid, out_cotangent, gain_row, out_weight,
            att, ot, lse, qt, kv_all, layer_input, attn_gain[None, :], weights_in, *tables,
        ),
    )

    keep = hidden - (QUAD - 1) * piece
    wide_sum = wide_sum.reshape(QUAD, 2, features, piece)
    tall_sum = tall_sum.reshape(QUAD, piece, features)

    def side_by_side(number):
        parts = [wide_sum[i, number] for i in range(QUAD - 1)] + [
            wide_sum[QUAD - 1, number][:, :keep]
        ]
        return jnp.concatenate(parts, axis=1).astype(F32)

    gate_sum, up_sum = side_by_side(0), side_by_side(1)
    down_sum = tall_sum.reshape(QUAD * piece, features)[:hidden].astype(F32)

    query_width = heads * HEAD_DIM

    def quarters(parts, row_count):
        parts = parts.reshape(QUAD, -1, parts.shape[-1])[:, : row_count // QUAD]
        return parts.reshape(row_count, -1).astype(F32)

    out_grad = quarters(outs, query_width)
    query_grad = quarters(ins_q, features)
    key_value = quarters(ins_kv, features)
    key_grad, value_grad = key_value[:, :HEAD_DIM], key_value[:, HEAD_DIM:]
    attn_gain_grad, mlp_gain_grad = gains[0, :features], gains[0, features:]
    query_bias_grad = biases[0, :query_width]
    key_bias_grad = biases[0, query_width : query_width + HEAD_DIM]
    value_bias_grad = biases[0, query_width + HEAD_DIM : query_width + 2 * HEAD_DIM]
    return (
        layer_output,
        input_grad,
        attn_gain_grad,
        query_grad,
        query_bias_grad,
        key_grad,
        key_bias_grad,
        value_grad,
        value_bias_grad,
        out_grad,
        mlp_gain_grad,
        gate_sum,
        up_sum,
        down_sum,
    )


def solution(mesh):
    groups = mesh.shape["seq"] // QUAD
    by_rows, columns, rows, vector, whole = (
        P("seq", None),
        P(None, "tp"),
        P("tp", None),
        P("tp"),
        P(),
    )
    return jax.shard_map(
        functools.partial(per_device, groups),
        mesh=mesh,
        in_specs=(
            by_rows, whole, whole, columns, vector, columns, vector, columns, vector, rows,
            whole, columns, columns, rows, by_rows,
        ),
        out_specs=(
            by_rows, by_rows, whole, columns, vector, columns, vector, columns, vector, rows,
            whole, columns, columns, rows,
        ),
        check_vma=False,
    )
```

```python
import functools

import jax
import jax.numpy as jnp
from jax import lax
from jax.experimental import pallas as pl
from jax.experimental.pallas import tpu as pltpu
from jax.sharding import PartitionSpec as P

HEAD_DIM = 64
EPSILON = 1e-06
NEGATIVE = -1e30
ROPE_BASE = 1000000.0
LANES = 128
QUAD = 4
WIDE_ROWS = 64
TALL_ROWS = 64
SHARE = (4, 3, 3, 4, 1, 1, 2, 3, 2, 2, 4, 1, 2, 1, 2)
PACE = 4
MESH = pl.DeviceIdType.MESH
VMEM_LIMIT = 62 * 1024 * 1024
BF16 = jnp.bfloat16
F32 = jnp.float32


def round_up(value, step):
    return -(-value // step) * step


def nn(left, right):
    return lax.dot_general(left, right, (((1,), (0,)), ((), ())), preferred_element_type=F32)


def nt(left, right):
    return lax.dot_general(left, right, (((1,), (1,)), ((), ())), preferred_element_type=F32)


def tn(left, right):
    return lax.dot_general(left, right, (((0,), (0,)), ((), ())), preferred_element_type=F32)


class Place:
    def __init__(self, groups):
        seq = lax.axis_index("seq").astype(jnp.int32)
        tp = lax.axis_index("tp").astype(jnp.int32)
        self.groups = groups
        self.seq = seq
        self.tp = tp
        self.group = seq // QUAD
        self.quad = seq % QUAD
        self.core = seq % 2
        self.side = (seq // 2) % 2
        self.sibling = (seq + 1 - 2 * self.core, tp)
        self.across = (seq + 2 - 4 * self.side, tp)
        self.partner = (seq, 1 - tp)

    def seq_at(self, group, side, core):
        return group * QUAD + side * 2 + core

    def in_group(self, group):
        return (group * QUAD + self.quad, self.tp)


def send(src, dst, send_sem, recv_sem, device):
    pltpu.make_async_remote_copy(
        src_ref=src,
        dst_ref=dst,
        send_sem=send_sem,
        recv_sem=recv_sem,
        device_id=device,
        device_id_type=MESH,
    ).start()


def sent(src, send_sem, device):
    pltpu.make_async_remote_copy(
        src_ref=src,
        dst_ref=src,
        send_sem=send_sem,
        recv_sem=send_sem,
        device_id=device,
        device_id_type=MESH,
    ).wait_send()


def arrived(dst, recv_sem, device):
    pltpu.make_async_remote_copy(
        src_ref=dst,
        dst_ref=dst,
        send_sem=recv_sem,
        recv_sem=recv_sem,
        device_id=device,
        device_id_type=MESH,
    ).wait_recv()


def meet(place, whole_column):
    barrier = pltpu.get_barrier_semaphore()
    for device in (place.sibling, place.across, place.partner):
        pl.semaphore_signal(barrier, inc=1, device_id=device, device_id_type=MESH)
    if whole_column:
        for step in range(1, place.groups):
            other = place.in_group((place.group + step) % place.groups)
            pl.semaphore_signal(barrier, inc=1, device_id=other, device_id_type=MESH)
        pl.semaphore_wait(barrier, 3 + place.groups - 1)
    else:
        pl.semaphore_wait(barrier, 3)


class LayerGather:
    def __init__(self, place, all_ref, half, recv, part, sems):
        self.place = place
        self.all_ref = all_ref
        self.half = half
        self.first = round_up(half // 2, 16)
        self.recv, self.part, self.sems = recv, part, sems

    def index(self, flip_side, flip_core, flip_tp):
        place = self.place
        side = 1 - place.side if flip_side else place.side
        core = 1 - place.core if flip_core else place.core
        tp = 1 - place.tp if flip_tp else place.tp
        return (side * 2 + core) * 2 + tp

    def rows(self, block, start=0, size=None):
        size = self.half if size is None else size
        return self.all_ref.at[pl.ds(pl.multiple_of(block * self.half + start, 16), size)]

    def start(self):
        place = self.place
        own = self.index(0, 0, 0)
        for number, device in enumerate((place.across, place.partner, place.sibling)):
            send(self.rows(own), self.rows(own), self.sems.at[number], self.recv.at[own], device)

    def from_across(self):
        place = self.place
        block = self.index(1, 0, 0)
        arrived(self.rows(block), self.recv.at[block], place.across)
        part = self.rows(block, 0, self.first)
        send(part, part, self.sems.at[3], self.part.at[0], place.partner)
        send(self.rows(block), self.rows(block), self.sems.at[4], self.recv.at[block], place.sibling)

    def from_partner(self):
        place = self.place
        block = self.index(0, 0, 1)
        arrived(self.rows(block), self.recv.at[block], place.partner)
        part = self.rows(block, self.first, self.half - self.first)
        send(part, part, self.sems.at[5], self.part.at[1], place.across)
        send(self.rows(block), self.rows(block), self.sems.at[6], self.recv.at[block], place.sibling)

    def diagonal(self):
        place = self.place
        block = self.index(1, 0, 1)
        arrived(self.rows(block, 0, self.first), self.part.at[0], place.partner)
        arrived(self.rows(block, self.first, self.half - self.first), self.part.at[1], place.across)
        send(self.rows(block), self.rows(block), self.sems.at[7], self.recv.at[block], place.sibling)

    def from_sibling(self, flip_side, flip_tp):
        block = self.index(flip_side, 1, flip_tp)
        arrived(self.rows(block), self.recv.at[block], self.place.sibling)

    def finish(self, waited=False):
        place = self.place
        if not waited:
            for side in (0, 1):
                for tp in (0, 1):
                    self.from_sibling(side, tp)
        own = self.index(0, 0, 0)
        for number, device in enumerate((place.across, place.partner, place.sibling)):
            sent(self.rows(own), self.sems.at[number], device)
        sent(self.rows(own, 0, self.first), self.sems.at[3], place.partner)
        sent(self.rows(own), self.sems.at[4], place.sibling)
        sent(self.rows(own, self.first, self.half - self.first), self.sems.at[5], place.across)
        sent(self.rows(own), self.sems.at[6], place.sibling)
        sent(self.rows(own), self.sems.at[7], place.sibling)


def extended_keys(kv, chip, rows, width, slots):
    count = kv.shape[0]
    lane = lax.broadcasted_iota(jnp.int32, (count, width), 1) - HEAD_DIM
    row = lax.broadcasted_iota(jnp.int32, (count, width), 0)
    block = rows // 2
    number = jnp.zeros_like(row)
    for edge in range(block, count, block):
        number = number + (row >= edge).astype(jnp.int32)
    hot = (lane == number + chip * (count // block)) | ((lane >= slots) & (lane < slots + 3))
    extra = jnp.where(hot, 1.0, 0.0).astype(BF16)
    if width == LANES:
        return jnp.where(lane < 0, kv, extra)
    first = jnp.where(lane[:, :LANES] < 0, kv, extra[:, :LANES])
    return jnp.concatenate([first, extra[:, LANES:]], axis=1)


def hide_later(scores, place, rows, first_query):
    count, width = scores.shape
    block = rows // 2
    key = lax.broadcasted_iota(jnp.int32, (count, 1), 0) - place.core * rows
    query = lax.broadcasted_iota(jnp.int32, (1, width), 1) + first_query
    query = query % rows
    end = jnp.where(query < block, block, rows)
    return jnp.where((key > query) & (key < end), NEGATIVE, scores)


def split_rows(values, at, count):
    one = values.astype(BF16).astype(F32)
    two = (values - one).astype(BF16).astype(F32)
    three = values - one - two
    row = lax.broadcasted_iota(jnp.int32, (count, values.shape[1]), 0) - at
    picked = jnp.where(row == 0, one, jnp.where(row == 1, two, jnp.where(row == 2, three, 0.0)))
    return picked.astype(BF16)


def attend_kernel(
    groups,
    slots,
    kv_own,
    qt,
    x_in,
    out_weight,
    cot,
    kv_all,
    cot_all,
    resid_out,
    att_out,
    ot_out,
    lse_out,
    s_buf,
    m_buf,
    l_buf,
    part_buf,
    part_send,
    part_recv,
    kv_recv,
    kv_z,
    kv_x,
    kv_sib,
    c_recv,
    c_part,
    c_sems,
    p_sems,
):
    place = Place(groups)
    rows = kv_own.shape[0]
    half = rows // 2
    span = 2 * rows
    width, queries = qt.shape
    block = queries // 2
    chunks = 2 * groups
    heads = out_weight.shape[0] // HEAD_DIM

    kv_all[pl.ds(place.seq * rows, rows), :] = kv_own[...]
    own_half = place.quad * 2 + place.tp
    cot_all[pl.ds(pl.multiple_of(own_half * half, 16), half), :] = cot[
        pl.ds(pl.multiple_of(place.tp * half, 16), half), :
    ]
    meet(place, True)

    def kv_rows(seq):
        return kv_all.at[pl.ds(pl.multiple_of(seq * rows, 16), rows)]

    own = kv_rows(place.seq)
    send(own, own, kv_sib.at[0], kv_recv.at[place.seq], place.sibling)
    for step in range(1, groups):
        other = place.in_group((place.group + step) % groups)
        send(own, own, kv_z.at[step - 1], kv_recv.at[place.seq], other)
    send(own, own, kv_x.at[0], kv_recv.at[place.seq], place.across)

    def chunk_place(number):
        far = number % 2
        group = (place.group + number // 2) % groups
        side = place.side + far * (1 - 2 * place.side)
        return group, side

    def pass_on(number):
        group, side = chunk_place(number)
        seq = place.seq_at(group, side, place.core)
        view = kv_rows(seq)
        arrived(view, kv_recv.at[seq], place.across)
        send(view, view, kv_sib.at[number], kv_recv.at[seq], place.sibling)

        @pl.when(number % 2 == 0)
        def near():
            send(view, view, kv_x.at[number // 2], kv_recv.at[seq], place.across)

    def ready(number):
        group, side = chunk_place(number)
        seq = place.seq_at(group, side, 1 - place.core)
        arrived(kv_rows(seq), kv_recv.at[seq], place.sibling)

    gather_cot = LayerGather(place, cot_all, half, c_recv, c_part, c_sems)

    def kv_chunk(number):
        group, side = chunk_place(number)
        chip = group * 2 + side
        return chip, kv_all[pl.ds(pl.multiple_of(chip * span, 16), span), :]

    def scores(number, part, slot, own_chip=False):
        chip, kv = kv_chunk(number)
        keys = extended_keys(kv, chip, rows, width, slots)
        value = nn(keys, qt[:, part * block : (part + 1) * block])
        if own_chip:
            value = hide_later(value, place, rows, part * block)
        s_buf[slot] = value

    def absorb(number, part, slot, first=False):
        chip, kv = kv_chunk(number)
        lanes = slice(part * block, (part + 1) * block)
        value = s_buf[slot]
        top = jnp.max(value, axis=0, keepdims=True)
        if not first:
            old = m_buf[:, lanes]
            top = jnp.maximum(old, top)
            shrink = jnp.exp(old - top)
        weights = jnp.exp(value - top)
        total = jnp.sum(weights, axis=0, keepdims=True)
        product = tn(kv[:, HEAD_DIM:], weights.astype(BF16))
        if not first:
            total = total + l_buf[:, lanes] * shrink
            product = product + ot_out[:, lanes] * shrink
        m_buf[:, lanes] = top
        l_buf[:, lanes] = total
        ot_out[:, lanes] = product

    ready(0)
    scores(0, 0, 0, True)
    scores(0, 1, 1, True)
    absorb(0, 0, 0, True)
    pass_on(1)
    pass_on(2)
    ready(1)
    scores(1, 0, 0)
    absorb(0, 1, 1, True)

    def step(number, unused):
        scores(number, 1, 1)
        absorb(number, 0, 0)

        @pl.when(number + 2 < chunks)
        def look_ahead():
            pass_on(number + 2)

        @pl.when(number + 1 < chunks)
        def next_ready():
            ready(number + 1)

        @pl.when(number == 1)
        def cot_start():
            gather_cot.start()

        @pl.when(number == chunks - 3)
        def cot_middle():
            gather_cot.from_across()
            gather_cot.from_partner()

        scores(jnp.minimum(number + 1, chunks - 1), 0, 0)
        absorb(number, 1, 1)
        return unused

    lax.fori_loop(1, chunks, step, 0)

    ot = ot_out[...] / l_buf[...]
    ot_out[...] = ot
    lse_out[...] = m_buf[...] + jnp.log(l_buf[...])
    natural = jnp.transpose(ot).astype(BF16)
    att = jnp.concatenate(
        [natural[head * rows : (head + 1) * rows, :] for head in range(heads)], axis=1
    )
    att_out[...] = att
    part_buf[...] = nn(att, out_weight[...])
    other_rows = pl.ds(pl.multiple_of((1 - place.tp) * half, 16), half)
    my_rows = pl.ds(pl.multiple_of(place.tp * half, 16), half)
    part_send[...] = part_buf[other_rows, :].astype(BF16)
    send(part_send, part_recv, p_sems.at[0], p_sems.at[1], place.partner)
    gather_cot.diagonal()
    mine = part_buf[my_rows, :] + x_in[my_rows, :].astype(F32)
    arrived(part_recv, p_sems.at[1], place.partner)
    resid = mine + part_recv[...].astype(F32)
    resid_out[...] = resid
    gather_cot.finish()
    sent(part_send, p_sems.at[0], place.partner)

    def close(number, unused):
        sent(own, kv_sib.at[number], place.sibling)
        return unused

    lax.fori_loop(0, chunks, close, 0)
    for step_out in range(groups):
        sent(own, kv_x.at[step_out], place.across)
    for step_out in range(1, groups):
        sent(own, kv_z.at[step_out - 1], place.in_group((place.group + step_out) % groups))


class ChainSum:
    def __init__(self, place, own, incoming, at_root, final, sems):
        self.place = place
        self.own, self.incoming, self.at_root, self.final = own, incoming, at_root, final
        self.count = own.shape[0]
        (
            self.up_recv,
            self.up_send,
            self.fin_recv,
            self.fin_send,
            self.x_recv,
            self.x_send,
            self.c_recv,
            self.c_send,
            self.keep,
        ) = sems

    def root(self, parity):
        return self.place.groups // 2 - 1 + parity

    def lag_up(self, parity):
        groups, group, root = self.place.groups, self.place.group, self.root(parity)
        most = max(root, groups - 1 - root)
        return PACE * jnp.where(
            group < root, group, jnp.where(group > root, groups - 1 - group, most)
        )

    def lag_down(self, parity):
        groups, group, root = self.place.groups, self.place.group, self.root(parity)
        most = max(root, groups - 1 - root)
        return PACE * (most + jnp.abs(group - root))

    def total_steps(self):
        groups = self.place.groups
        most = groups // 2
        return self.count + PACE * (2 * most + 1)

    def spread(self, i, view):
        place = self.place
        final = self.final.at[place.quad, i]
        send(view, final, self.x_send.at[i], self.x_recv.at[i], place.across)
        send(view, final, self.c_send.at[0, i], self.c_recv.at[0, i], place.sibling)

    def up(self, i, parity):
        place, root = self.place, self.root(parity)
        group, last = place.group, place.groups - 1
        mine = self.own.at[i]

        here, second = self.incoming.at[i], self.at_root.at[i // 2]

        def add(way, ref):
            arrived(ref, self.up_recv.at[way, i], place.in_group(group - 1 + 2 * way))
            mine[...] = (mine[...].astype(F32) + ref[...].astype(F32)).astype(BF16)

        def onward(way, dst, send_sem, recv_sem):
            send(mine, dst, send_sem, recv_sem, place.in_group(group + 1 - 2 * way))

        @pl.when((group > 0) & (group <= root))
        def from_left():
            add(0, here)

        @pl.when((group < last) & (group > root))
        def from_right():
            add(1, here)

        @pl.when((group < last) & (group == root))
        def from_right_to_root():
            add(1, second)

        @pl.when(group < root)
        def to_right():
            onward(0, here, self.up_send.at[i], self.up_recv.at[0, i])

        @pl.when(group > root + 1)
        def to_left():
            onward(1, here, self.up_send.at[i], self.up_recv.at[1, i])

        @pl.when(group == root + 1)
        def to_root():
            onward(1, second, self.up_send.at[i], self.up_recv.at[1, i])

        @pl.when(group == root)
        def finished():
            final = self.final.at[place.quad, i]

            @pl.when(group > 0)
            def left():
                onward(1, final, self.fin_send.at[0, i], self.fin_recv.at[i])

            @pl.when(group < last)
            def right():
                onward(0, final, self.fin_send.at[1, i], self.fin_recv.at[i])

            self.spread(i, mine)
            pltpu.make_async_copy(mine, final, self.keep.at[i]).start()

    def down(self, i, parity):
        place, root = self.place, self.root(parity)
        group, last = place.group, place.groups - 1
        view = self.final.at[place.quad, i]

        @pl.when(group != root)
        def take():
            arrived(view, self.fin_recv.at[i], place.sibling)

            @pl.when((group < root) & (group > 0))
            def left():
                send(
                    view,
                    view,
                    self.fin_send.at[0, i],
                    self.fin_recv.at[i],
                    place.in_group(group - 1),
                )

            @pl.when((group > root) & (group < last))
            def right():
                send(
                    view,
                    view,
                    self.fin_send.at[1, i],
                    self.fin_recv.at[i],
                    place.in_group(group + 1),
                )

            self.spread(i, view)

    def cross(self, i):
        place = self.place
        view = self.final.at[place.across[0] % QUAD, i]
        arrived(view, self.x_recv.at[i], place.across)
        send(view, view, self.c_send.at[1, i], self.c_recv.at[1, i], place.sibling)

    def step(self, number):
        for parity in (0, 1):
            i = number - self.lag_up(parity)

            @pl.when((i >= 0) & (i < self.count) & (i % 2 == parity))
            def go_up(i=i, parity=parity):
                self.up(i, parity)

        for parity in (0, 1):
            i = number - self.lag_down(parity)

            @pl.when((i >= 0) & (i < self.count) & (i % 2 == parity))
            def go_down(i=i, parity=parity):
                self.down(i, parity)

        for parity in (0, 1):
            i = number - self.lag_down(parity) - PACE

            @pl.when((i >= 0) & (i < self.count) & (i % 2 == parity))
            def go_cross(i=i):
                self.cross(i)

    def finish(self):
        place = self.place
        group, last = place.group, place.groups - 1
        sibling_quad = place.sibling[0] % QUAD
        diagonal = 3 - place.quad

        def close(i, unused):
            root = place.groups // 2 - 1 + i % 2
            view = self.own.at[i]
            arrived(self.final.at[sibling_quad, i], self.c_recv.at[0, i], place.sibling)
            arrived(self.final.at[diagonal, i], self.c_recv.at[1, i], place.sibling)

            @pl.when(group != root)
            def up_done():
                sent(view, self.up_send.at[i], place.sibling)

            @pl.when(group == root)
            def kept():
                final = self.final.at[place.quad, i]
                pltpu.make_async_copy(view, final, self.keep.at[i]).wait()

            @pl.when((group <= root) & (group > 0))
            def left_done():
                sent(view, self.fin_send.at[0, i], place.sibling)

            @pl.when((group >= root) & (group < last))
            def right_done():
                sent(view, self.fin_send.at[1, i], place.sibling)

            sent(view, self.x_send.at[i], place.across)
            sent(view, self.c_send.at[0, i], place.sibling)
            sent(view, self.c_send.at[1, i], place.sibling)
            return unused

        lax.fori_loop(0, self.count, close, 0)


def chain_sems(count):
    dma = pltpu.SemaphoreType.DMA
    return [
        dma((2, count)),
        dma((count,)),
        dma((count,)),
        dma((2, count)),
        dma((count,)),
        dma((count,)),
        dma((2, count)),
        dma((2, count)),
        dma((count,)),
    ]


class LayerSum:
    def __init__(self, place, part, half, core_in, left, right, left_in, right_in, last_in, sems):
        self.place, self.part, self.half = place, part, half
        self.core_in, self.left, self.right = core_in, left, right
        self.left_in, self.right_in, self.last_in = left_in, right_in, last_in
        self.sems = sems
        self.cut = left.shape[2]
        self.columns = part.shape[1]

    def rows(self, side, core):
        size = 2 * self.half
        return pl.ds(pl.multiple_of((side * 2 + core) * size, 16), size)

    def start(self):
        place = self.place
        for side in (0, 1):
            view = self.part.at[self.rows(side, 1 - place.core)]
            send(
                view,
                self.core_in.at[side],
                self.sems.at[side],
                self.sems.at[2 + side],
                place.sibling,
            )

    def own_rows(self, tp):
        return pl.ds(pl.multiple_of(tp * self.half, 16), self.half)

    def after_core(self):
        place = self.place
        for side in (0, 1):
            arrived(self.core_in.at[side], self.sems.at[2 + side], place.sibling)
            total = self.part[self.rows(side, place.core), :].astype(F32) + self.core_in[
                side
            ].astype(F32)
            self.left[side] = total[:, : self.cut].astype(BF16)
            self.right[side] = total[:, self.cut :].astype(BF16)

    def cross(self):
        place = self.place
        for side in (0, 1):
            send(
                self.left.at[side, self.own_rows(1 - place.tp)],
                self.left_in.at[side],
                self.sems.at[4 + side],
                self.sems.at[6 + side],
                place.partner,
            )
        send(
            self.right.at[1 - place.side],
            self.right_in,
            self.sems.at[8],
            self.sems.at[9],
            place.across,
        )

    def after_cross(self):
        place = self.place
        mine = self.own_rows(place.tp)
        for side in (0, 1):
            arrived(self.left_in.at[side], self.sems.at[6 + side], place.partner)
            self.left_in[side] = (
                self.left[side, mine, :].astype(F32) + self.left_in[side].astype(F32)
            ).astype(BF16)
        arrived(self.right_in, self.sems.at[9], place.across)
        self.right_in[...] = (
            self.right[place.side].astype(F32) + self.right_in[...].astype(F32)
        ).astype(BF16)
        send(
            self.left_in.at[1 - place.side],
            self.last_in.at[:, : self.cut],
            self.sems.at[10],
            self.sems.at[11],
            place.across,
        )
        send(
            self.right_in.at[self.own_rows(1 - place.tp)],
            self.last_in.at[:, self.cut :],
            self.sems.at[12],
            self.sems.at[13],
            place.partner,
        )

    def result(self):
        place = self.place
        arrived(self.last_in.at[:, : self.cut], self.sems.at[11], place.across)
        arrived(self.last_in.at[:, self.cut :], self.sems.at[13], place.partner)
        mine = jnp.concatenate(
            [self.left_in[place.side], self.right_in[self.own_rows(place.tp), :]], axis=1
        )
        return mine.astype(F32) + self.last_in[...].astype(F32)

    def finish(self):
        place = self.place
        for side in (0, 1):
            sent(self.core_in.at[side], self.sems.at[side], place.sibling)
            sent(self.left_in.at[side], self.sems.at[4 + side], place.partner)
        sent(self.right_in, self.sems.at[8], place.across)
        sent(self.last_in.at[:, : self.cut], self.sems.at[10], place.across)
        sent(self.last_in.at[:, self.cut :], self.sems.at[12], place.partner)


class QuadSum:
    def __init__(self, place, part, own, core_in, x_send, x_in, sems):
        self.place, self.part, self.own = place, part, own
        self.core_in, self.x_send, self.x_in, self.sems = core_in, x_send, x_in, sems

    def start(self):
        place = self.place
        for side in (0, 1):
            send(
                self.part.at[side * 2 + 1 - place.core],
                self.core_in.at[side],
                self.sems.at[side],
                self.sems.at[2 + side],
                place.sibling,
            )

    def total(self, side):
        return self.part[side * 2 + self.place.core].astype(F32) + self.core_in[side].astype(F32)

    def middle(self):
        place = self.place
        for side in (0, 1):
            arrived(self.core_in.at[side], self.sems.at[2 + side], place.sibling)
        self.x_send[...] = self.total(1 - place.side).astype(BF16)
        send(self.x_send, self.x_in, self.sems.at[4], self.sems.at[5], place.across)

    def end(self):
        place = self.place
        arrived(self.x_in, self.sems.at[5], place.across)
        mine = (self.total(place.side) + self.x_in[...].astype(F32)).astype(BF16)
        count, step = self.own.shape[0], self.own.shape[1]
        for i in range(count):
            piece = mine[i * step : (i + 1) * step, :]
            if piece.shape[0]:
                self.own[i, : piece.shape[0], :] = piece
            if piece.shape[0] < step:
                left = step - piece.shape[0]
                self.own[i, piece.shape[0] :, :] = jnp.zeros((left, piece.shape[1]), BF16)

    def finish(self):
        place = self.place
        for side in (0, 1):
            sent(self.core_in.at[side], self.sems.at[side], place.sibling)
        sent(self.x_send, self.sems.at[4], place.across)


class ColumnSum:
    def __init__(self, place, own, incoming, final, sems):
        self.place, self.own, self.incoming, self.final = place, own, incoming, final
        self.rs_send, self.rs_recv, self.ag_send, self.ag_recv = (sems.at[i] for i in range(4))
        self.x_send, self.x_recv, self.c_send, self.c_recv = (sems.at[i] for i in range(4, 8))
        self.d_send, self.d_recv = (sems.at[i] for i in range(8, 10))

    def others(self):
        place = self.place
        for step in range(1, place.groups):
            yield step, (place.group + step) % place.groups

    def start(self):
        place = self.place
        for step, other in self.others():
            back = place.groups - step
            send(
                self.own.at[other],
                self.incoming.at[back],
                self.rs_send.at[step],
                self.rs_recv.at[back],
                place.in_group(other),
            )

    def spread(self, part, view):
        place = self.place
        final = self.final.at[place.quad, part]
        send(view, final, self.x_send.at[part], self.x_recv.at[part], place.across)
        send(view, final, self.c_send.at[part], self.c_recv.at[part], place.sibling)

    def middle(self):
        place = self.place
        mine = self.own.at[place.group]
        total = mine[...].astype(F32)
        for step, other in self.others():
            arrived(self.incoming.at[step], self.rs_recv.at[step], place.sibling)
            total = total + self.incoming[step].astype(F32)
        mine[...] = total.astype(BF16)
        final = self.final.at[place.quad, place.group]
        for step, other in self.others():
            send(
                mine,
                final,
                self.ag_send.at[step],
                self.ag_recv.at[place.group],
                place.in_group(other),
            )
        self.spread(place.group, mine)
        pltpu.make_async_copy(mine, final, self.ag_send.at[0]).start()

    def end(self):
        place = self.place
        for step, other in self.others():
            view = self.final.at[place.quad, other]
            arrived(view, self.ag_recv.at[other], place.sibling)
            self.spread(other, view)

    def cross(self):
        place = self.place
        quad = place.across[0] % QUAD
        for step in range(place.groups):
            part = (place.group + step) % place.groups
            view = self.final.at[quad, part]
            arrived(view, self.x_recv.at[part], place.across)
            send(view, view, self.d_send.at[part], self.d_recv.at[part], place.sibling)

    def finish(self):
        place = self.place
        view = self.own.at[0]
        for part in range(place.groups):
            arrived(view, self.c_recv.at[part], place.sibling)
            arrived(view, self.d_recv.at[part], place.sibling)
            sent(view, self.x_send.at[part], place.across)
            sent(view, self.c_send.at[part], place.sibling)
            sent(view, self.d_send.at[part], place.sibling)
        for step, other in self.others():
            sent(view, self.rs_send.at[step], place.sibling)
            sent(view, self.ag_send.at[step], place.sibling)
        final = self.final.at[place.quad, place.group]
        pltpu.make_async_copy(self.own.at[place.group], final, self.ag_send.at[0]).wait()


def column_parts(groups, rows, columns):
    return (groups, round_up(-(-rows // groups), 16), columns)


def column_sum_scratch(groups, rows, columns):
    parts = column_parts(groups, rows, columns)
    return [
        *quad_sum_scratch(rows, columns),
        pltpu.VMEM(parts, BF16),
        pltpu.VMEM(parts, BF16),
        pltpu.SemaphoreType.DMA((10, groups)),
    ]


def quad_sum_scratch(rows, columns):
    return [
        pltpu.VMEM((QUAD, rows, columns), BF16),
        pltpu.VMEM((2, rows, columns), BF16),
        pltpu.VMEM((rows, columns), BF16),
        pltpu.VMEM((rows, columns), BF16),
        pltpu.SemaphoreType.DMA((6,)),
    ]


def layer_sum_scratch(half, columns):
    cut = columns // LANES // 2 * LANES
    if cut * 2 < columns:
        cut += LANES
    return [
        pltpu.VMEM((2, 2 * half, columns), BF16),
        pltpu.VMEM((2, 2 * half, cut), BF16),
        pltpu.VMEM((2, 2 * half, columns - cut), BF16),
        pltpu.VMEM((2, half, cut), BF16),
        pltpu.VMEM((2 * half, columns - cut), BF16),
        pltpu.VMEM((half, columns), BF16),
        pltpu.SemaphoreType.DMA((14,)),
    ]


def backward_kernel(
    groups,
    slots,
    gate_weight,
    up_weight,
    down_weight,
    cot_all,
    resid_in,
    cot,
    gain,
    out_weight,
    att,
    ot,
    lse,
    qt_in,
    kv_all,
    x_in,
    attn_gain,
    weights_in,
    cosine,
    sine,
    layer_out,
    input_grad,
    wide,
    tall,
    outs,
    ins_q,
    ins_kv,
    gains,
    biases,
    *scratch,
):
    place = Place(groups)
    wide_own, tall_own, wide_up, tall_up = scratch[0:4]
    wide_root, tall_root = scratch[4:6]
    scratch = scratch[2:]
    wide_sems, tall_sems = scratch[4:13], scratch[13:22]
    sum_g, sum_m = scratch[22:29], scratch[29:36]
    branch, qt, dot_t, q_pad, do_pad, dkv = scratch[36:42]
    sib_send, sib_in, side_send, side_in, z_send, z_in = scratch[42:48]
    kv_sems, pair_sems = scratch[48:50]
    dq_out, dkv_out, resid_grad = scratch[50:53]
    turn_send, turn_in, gain_in, bias_in, gain_z, bias_z, vector_sems = scratch[53:60]
    sum_o, sum_q, sum_kv = scratch[60:68], scratch[68:76], scratch[76:84]
    rows = att.shape[0]
    half = rows // 2
    span = 2 * rows
    width, queries = qt_in.shape
    parts = 2 if groups <= 4 else 4
    block = queries // parts
    chunks = 2 * groups
    heads = out_weight.shape[0] // HEAD_DIM
    my_rows = pl.ds(pl.multiple_of(place.tp * half, 16), half)
    other_rows = pl.ds(pl.multiple_of((1 - place.tp) * half, 16), half)

    tall_sum = ChainSum(place, tall_own, tall_up, tall_root, tall, tall_sems)
    wide_sum = ChainSum(place, wide_own, wide_up, wide_root, wide, wide_sems)
    gate_piece, up_piece, down_piece, normed_all, mixed, grad_gu, grad_part, mlp_part = scratch[84:92]
    gather_sems = scratch[92:95]
    features = resid_in.shape[1]
    piece = gate_piece.shape[1]
    keep = gate_weight.shape[1] - (QUAD - 1) * piece

    def load_weights(size, quad):
        columns = pl.ds(pl.multiple_of(quad * piece, LANES), size)
        pairs = (
            (gate_weight.at[:, columns], gate_piece.at[:, pl.ds(0, size)]),
            (up_weight.at[:, columns], up_piece.at[:, pl.ds(0, size)]),
            (down_weight.at[columns], down_piece.at[pl.ds(0, size)]),
        )
        return [
            pltpu.make_async_copy(src, dst, pair_sems.at[4 + number])
            for number, (src, dst) in enumerate(pairs)
        ]

    last_quad = QUAD - 1

    @pl.when(place.quad < last_quad)
    def whole_piece():
        for copy in load_weights(piece, place.quad):
            copy.start()

    @pl.when(place.quad == last_quad)
    def last_piece():
        for copy in load_weights(keep, last_quad):
            copy.start()
        if keep < piece:
            gate_piece[:, keep:] = jnp.zeros((features, piece - keep), BF16)
            up_piece[:, keep:] = jnp.zeros((features, piece - keep), BF16)
            down_piece[keep:, :] = jnp.zeros((piece - keep, features), BF16)

    grad_sum = LayerSum(place, grad_part, half, *sum_g)
    mlp_sum = LayerSum(place, mlp_part, half, *sum_m)

    def quad_and_column(final, refs):
        quad = QuadSum(place, refs[0], refs[5], *refs[1:5])
        return quad, ColumnSum(place, refs[5], refs[6], final, refs[7])

    outs_quad, outs_sum = quad_and_column(outs, sum_o)
    q_quad, q_sum = quad_and_column(ins_q, sum_q)
    kv_quad, kv_sum = quad_and_column(ins_kv, sum_kv)
    tall_steps = tall_sum.count

    def chain_step(number):
        tall_sum.step(number)
        wide_sum.step(number - tall_steps)

    def chain_steps(first, count):
        def one(number, unused):
            chain_step(number)
            return unused

        lax.fori_loop(first, first + count, one, 0)
        return first + count

    all_steps = tall_steps + wide_sum.total_steps()

    gather = LayerGather(place, normed_all, half, *gather_sems)
    resid = resid_in[...]
    factor = lax.rsqrt(jnp.mean(resid * resid, axis=-1, keepdims=True) + EPSILON)
    own_block = place.quad * 2 + place.tp
    normed_all[pl.ds(pl.multiple_of(own_block * half, 16), half), :] = (
        resid * factor * gain[...]
    ).astype(BF16)
    meet(place, True)
    gather.start()

    @pl.when(place.quad < last_quad)
    def whole_loaded():
        for copy in load_weights(piece, place.quad):
            copy.wait()

    @pl.when(place.quad == last_quad)
    def last_loaded():
        for copy in load_weights(keep, last_quad):
            copy.wait()

    def feed(number, unused):
        @pl.when(number == 1)
        def second():
            gather.from_sibling(0, 0)

        @pl.when(number == 2)
        def third():
            gather.from_partner()
            gather.from_across()

        @pl.when(number == 4)
        def fifth():
            gather.from_sibling(0, 1)

        @pl.when(number == 5)
        def sixth():
            gather.from_sibling(1, 0)
            gather.diagonal()

        @pl.when(number == 7)
        def eighth():
            gather.from_sibling(1, 1)

        def flip(value, numbers):
            turned = functools.reduce(lambda x, y: x | y, [number == i for i in numbers])
            return jnp.where(turned, 1 - value, value)

        side = flip(place.side, (3, 5, 6, 7))
        core = flip(place.core, (1, 4, 5, 7))
        tp = flip(place.tp, (2, 4, 6, 7))
        at_rows = pl.ds(pl.multiple_of(((side * 2 + core) * 2 + tp) * half, 16), half)
        here = normed_all[at_rows, :]
        gate = nn(here, gate_piece[...])
        upward = nn(here, up_piece[...])
        grad_mixed = nt(cot_all[at_rows, :], down_piece[...])
        sigmoid = jax.nn.sigmoid(gate)
        silu = gate * sigmoid
        mix = (silu * upward).astype(BF16)
        grad_gate = (grad_mixed * upward * sigmoid * (1.0 + gate * (1.0 - sigmoid))).astype(BF16)
        grad_upward = (grad_mixed * silu).astype(BF16)
        mixed[at_rows, :] = mix
        grad_gu[at_rows, :piece] = grad_gate
        grad_gu[at_rows, piece:] = grad_upward
        grad_part[at_rows, :] = (
            nt(grad_gate, gate_piece[...]) + nt(grad_upward, up_piece[...])
        ).astype(BF16)
        mlp_part[at_rows, :] = nn(mix, down_piece[...]).astype(BF16)
        return unused

    lax.fori_loop(0, 8, feed, 0)
    grad_sum.start()
    tall_own[...] = tn(mixed[...], cot_all[...]).astype(BF16).reshape(tall_own.shape)
    done = chain_steps(0, SHARE[0])
    grad_sum.after_core()
    grad_sum.cross()
    both = tn(normed_all[...], grad_gu[...])
    count = wide_own.shape[0] // 2
    for number in range(2):
        wide_own[number * count : (number + 1) * count] = (
            both[:, number * piece : (number + 1) * piece]
            .astype(BF16)
            .reshape(count, *wide_own.shape[1:])
        )
    gather.finish(True)

    qt[...] = qt_in[...]
    at = HEAD_DIM + slots
    qt[at : at + 16, :] = split_rows(-lse[...], 0, 16)
    natural_q = jnp.transpose(qt_in[0:HEAD_DIM, :].astype(F32)).astype(BF16)
    q_pad[...] = jnp.concatenate([natural_q, jnp.zeros_like(natural_q)], axis=1)

    mlp_sum.start()
    done = chain_steps(done, SHARE[1])
    grad_sum.after_cross()
    done = chain_steps(done, SHARE[2])

    normed = resid * factor
    grad_normed = grad_sum.result()
    gains[:, features:] = jnp.sum(grad_normed * normed, axis=0, keepdims=True)
    weighted = grad_normed * gain[...]
    inner = jnp.mean(weighted * normed, axis=-1, keepdims=True)
    grad_resid = cot[my_rows, :].astype(F32) + factor * (weighted - normed * inner)
    resid_grad[...] = grad_resid
    branch[my_rows, :] = grad_resid.astype(BF16)
    send(
        branch.at[my_rows],
        branch.at[my_rows],
        pair_sems.at[0],
        pair_sems.at[1],
        place.partner,
    )
    mlp_sum.after_core()
    mlp_sum.cross()
    done = chain_steps(done, SHARE[3])
    arrived(branch.at[other_rows], pair_sems.at[1], place.partner)

    grads = branch[...]
    outs_part = sum_o[0]
    outs_part[...] = tn(att[...], grads).astype(BF16).reshape(outs_part.shape)
    outs_quad.start()
    grad_att = nt(grads, out_weight[...]).astype(BF16)
    stacked = jnp.concatenate(
        [grad_att[:, head * HEAD_DIM : (head + 1) * HEAD_DIM] for head in range(heads)]
        + [jnp.zeros((queries - heads * rows, HEAD_DIM), BF16)],
        axis=0,
    )
    do_pad[...] = jnp.concatenate([jnp.zeros_like(stacked), stacked], axis=1)
    turned = jnp.transpose(stacked.astype(F32))
    delta = jnp.sum(turned * ot[...], axis=0, keepdims=True)
    dot_t[0:HEAD_DIM, :] = split_rows(-delta, 0, HEAD_DIM)
    dot_t[HEAD_DIM:, :] = turned.astype(BF16)
    done = chain_steps(done, SHARE[4])
    outs_quad.middle()

    def write_layer():
        layer_out[my_rows, :] = (resid_in[...] + mlp_sum.result()).astype(BF16)
        send(
            layer_out.at[my_rows],
            layer_out.at[my_rows],
            pair_sems.at[2],
            pair_sems.at[3],
            place.partner,
        )

    dq_out[...] = jnp.zeros_like(dq_out)

    def chunk_place(number):
        far = 1 - number % 2
        group = (place.group + 1 + number // 2) % groups
        side = place.side + far * (1 - 2 * place.side)
        return group, side

    lane = lax.broadcasted_iota(jnp.int32, (1, LANES), 1)
    ones = jnp.where(lane < 3, 1.0, 0.0).astype(BF16)

    def attend_back(number, slot, own_chip=False):
        group, side = chunk_place(number)
        chip = group * 2 + side
        at_rows = pl.ds(pl.multiple_of(chip * span, 16), span)
        kv = kv_all[at_rows, :]
        keys = extended_keys(kv, chip, rows, width, slots)
        values = jnp.where(lane >= HEAD_DIM, kv, jnp.broadcast_to(ones, kv.shape))
        for part in range(parts):
            lanes = slice(part * block, (part + 1) * block)
            score = nn(keys, qt[:, lanes])
            if own_chip:
                score = hide_later(score, place, rows, part * block)
            weights = jnp.exp(score)
            change = nn(values, dot_t[:, lanes])
            low = (weights * change).astype(BF16)
            total = nn(weights.astype(BF16), do_pad[lanes, :]) + nn(low, q_pad[lanes, :])
            if part == 0:
                dkv[slot] = total
            else:
                dkv[slot] += total
            dq_out[:, lanes] += tn(kv[:, :HEAD_DIM], low)

    def hand_over(number, slot):
        other = pl.ds(pl.multiple_of((1 - place.core) * rows, 16), rows)

        @pl.when(number >= 2)
        def free_again():
            sent(sib_send.at[slot], kv_sems.at[0, number - 2], place.sibling)

        sib_send[slot] = dkv[slot, other, :].astype(BF16)
        send(
            sib_send.at[slot],
            sib_in.at[number],
            kv_sems.at[0, number],
            kv_sems.at[1, number],
            place.sibling,
        )

    def take_over(number, near, own_group=False):
        group, side = chunk_place(number)
        step = number // 2
        arrived(sib_in.at[number], kv_sems.at[1, number], place.sibling)
        mine = pl.ds(pl.multiple_of(place.core * rows, 16), rows)
        total = dkv[1 if near else 0, mine, :] + sib_in[number].astype(F32)
        if not near:
            ring = step % 2

            @pl.when(step >= 2)
            def side_free():
                sent(side_send.at[0], kv_sems.at[2, step - 2], place.across)

            side_send[ring] = total.astype(BF16)
            send(
                side_send.at[ring],
                side_in.at[step],
                kv_sems.at[2, step],
                kv_sems.at[3, step],
                place.across,
            )
            return
        arrived(side_in.at[step], kv_sems.at[3, step], place.across)
        total = total + side_in[step].astype(F32)
        if own_group:
            dkv_out[...] = total
            return
        ring = step % 2

        @pl.when(step >= 2)
        def column_free():
            sent(z_send.at[0], kv_sems.at[4, step - 2], place.sibling)

        z_send[ring] = total.astype(BF16)
        back = groups - 2 - step
        send(
            z_send.at[ring],
            z_in.at[back],
            kv_sems.at[4, step],
            kv_sems.at[5, back],
            place.in_group(group),
        )

    each = 2

    def pair(step, unused):
        attend_back(2 * step, 0)
        hand_over(2 * step, 0)
        chain_steps(done + 2 * each * step, each)

        @pl.when(step > 0)
        def last_near():
            take_over(2 * step - 1, True)

        attend_back(2 * step + 1, 1)
        hand_over(2 * step + 1, 1)
        take_over(2 * step, False)
        chain_steps(done + 2 * each * step + each, each)

        @pl.when(step == 0)
        def outs_ready():
            mlp_sum.after_cross()
            outs_quad.end()
            outs_sum.start()

        @pl.when(step == 1)
        def layer_ready():
            write_layer()
            outs_sum.middle()

        return unused

    lax.fori_loop(0, groups - 1, pair, 0)
    outs_sum.end()
    done += 2 * each * (groups - 1)
    attend_back(chunks - 2, 0)
    hand_over(chunks - 2, 0)
    done = chain_steps(done, each)
    if groups > 1:
        take_over(chunks - 3, True)
    attend_back(chunks - 1, 1, True)
    hand_over(chunks - 1, 1)
    take_over(chunks - 2, False)
    done = chain_steps(done, SHARE[5])

    quarter = HEAD_DIM // 2
    raw = dq_out[...] * HEAD_DIM**-0.5
    one, two = raw[:quarter, :], raw[quarter:, :]
    cos, sin = cosine[...], sine[...]
    turned = jnp.concatenate([one * cos + two * sin, two * cos - one * sin], axis=0)
    natural = jnp.transpose(turned).astype(BF16)
    grad_query = jnp.concatenate(
        [natural[head * rows : (head + 1) * rows, :] for head in range(heads)], axis=1
    )
    x_all = x_in[...].astype(F32)
    factor_all = lax.rsqrt(jnp.mean(x_all * x_all, axis=-1, keepdims=True) + EPSILON)
    normed_attn = (x_all * factor_all * attn_gain[...]).astype(BF16)
    wide_q = grad_query.shape[1]
    q_part = sum_q[0]
    q_part[...] = tn(normed_attn, grad_query).astype(BF16).reshape(q_part.shape)
    q_quad.start()
    turn_send[...] = nt(grad_query, weights_in[:, :wide_q])
    biases[...] = jnp.zeros_like(biases)
    biases[:, :wide_q] = jnp.sum(grad_query.astype(F32), axis=0, keepdims=True)
    done = chain_steps(done, SHARE[11])
    take_over(chunks - 1, True, True)
    q_quad.middle()
    outs_sum.cross()
    done = chain_steps(done, SHARE[6])
    for step in range(groups - 1):
        arrived(z_in.at[step], kv_sems.at[5, step], place.sibling)
        dkv_out[...] += z_in[step].astype(F32)
    turned = jnp.transpose(dkv_out[...])
    one, two = turned[:quarter, :], turned[quarter:HEAD_DIM, :]
    cos, sin = cosine[:, :rows], sine[:, :rows]
    turned = jnp.concatenate(
        [one * cos + two * sin, two * cos - one * sin, turned[HEAD_DIM:, :]], axis=0
    )
    grad_kv = jnp.transpose(turned).astype(BF16)
    kv_part = sum_kv[0]
    kv_part[...] = tn(normed_attn, grad_kv).astype(BF16).reshape(kv_part.shape)
    kv_quad.start()
    turn_send[...] += nt(grad_kv, weights_in[:, wide_q:])
    turn_in[0] = turn_send[other_rows, :].astype(BF16)
    send(turn_in.at[0], turn_in.at[1], vector_sems.at[0], vector_sems.at[1], place.partner)
    biases[:, wide_q : wide_q + LANES] = jnp.sum(grad_kv.astype(F32), axis=0, keepdims=True)
    done = chain_steps(done, SHARE[12])
    kv_quad.middle()
    q_quad.end()
    q_sum.start()
    done = chain_steps(done, SHARE[7])
    kv_quad.end()
    kv_sum.start()
    x_half = x_in[my_rows, :].astype(F32)
    factor = lax.rsqrt(jnp.mean(x_half * x_half, axis=-1, keepdims=True) + EPSILON)
    normed = x_half * factor
    done = chain_steps(done, SHARE[13])
    arrived(turn_in.at[1], vector_sems.at[1], place.partner)
    grad_normed = turn_send[my_rows, :] + turn_in[1].astype(F32)
    gains[:, :features] = jnp.sum(grad_normed * normed, axis=0, keepdims=True)
    weighted = grad_normed * attn_gain[...]
    mean = jnp.mean(weighted * normed, axis=-1, keepdims=True)
    input_grad[my_rows, :] = (
        resid_grad[...] + factor * (weighted - normed * mean)
    ).astype(BF16)

    def vectors(hop, device, with_biases):
        send(gains, gain_in.at[hop], vector_sems.at[4 + 4 * hop], vector_sems.at[5 + 4 * hop], device)
        if with_biases:
            send(
                biases,
                bias_in.at[hop],
                vector_sems.at[6 + 4 * hop],
                vector_sems.at[7 + 4 * hop],
                device,
            )

    def vectors_done(hop, device, with_biases):
        arrived(gain_in.at[hop], vector_sems.at[5 + 4 * hop], device)
        sent(gains, vector_sems.at[4 + 4 * hop], device)
        gains[...] += gain_in[hop]
        if with_biases:
            arrived(bias_in.at[hop], vector_sems.at[7 + 4 * hop], device)
            sent(biases, vector_sems.at[6 + 4 * hop], device)
            biases[...] += bias_in[hop]

    hops = ((place.partner, False), (place.sibling, True), (place.across, True))
    vectors(0, *hops[0])
    send(
        input_grad.at[my_rows],
        input_grad.at[my_rows],
        vector_sems.at[2],
        vector_sems.at[3],
        place.partner,
    )
    done = chain_steps(done, SHARE[14])
    q_sum.middle()
    vectors_done(0, *hops[0])
    vectors(1, *hops[1])
    kv_sum.middle()
    done = chain_steps(done, SHARE[8])
    vectors_done(1, *hops[1])
    vectors(2, *hops[2])
    done = chain_steps(done, SHARE[9])
    vectors_done(2, *hops[2])
    gain_z[place.group] = gains[...]
    bias_z[place.group] = biases[...]
    base = 16
    for step in range(1, groups):
        other = place.in_group((place.group + step) % groups)
        for number, ref in enumerate((gain_z, bias_z)):
            send(
                ref.at[place.group],
                ref.at[place.group],
                vector_sems.at[base + 4 * step + 2 * number],
                vector_sems.at[base + 4 * (groups - step) + 2 * number + 1],
                other,
            )
    q_sum.end()
    kv_sum.end()
    done = chain_steps(done, SHARE[10])
    q_sum.cross()
    kv_sum.cross()
    for step in range(1, groups):
        other = (place.group + groups - step) % groups
        for number, ref in enumerate((gain_z, bias_z)):
            arrived(
                ref.at[other],
                vector_sems.at[base + 4 * (groups - step) + 2 * number + 1],
                place.sibling,
            )
            sent(
                ref.at[place.group],
                vector_sems.at[base + 4 * step + 2 * number],
                place.sibling,
            )
    gains[...] = jnp.sum(gain_z[...], axis=0)
    biases[...] = jnp.sum(bias_z[...], axis=0)

    def last(number, unused):
        chain_step(number)
        return unused

    lax.fori_loop(done, all_steps, last, 0)

    arrived(input_grad.at[other_rows], vector_sems.at[3], place.partner)
    sent(input_grad.at[my_rows], vector_sems.at[2], place.partner)
    sent(turn_in.at[0], vector_sems.at[0], place.partner)
    for part in (outs_quad, q_quad, kv_quad, outs_sum, q_sum, kv_sum):
        part.finish()
    arrived(layer_out.at[other_rows], pair_sems.at[3], place.partner)
    sent(branch.at[my_rows], pair_sems.at[0], place.partner)
    sent(branch.at[my_rows], pair_sems.at[2], place.partner)
    grad_sum.finish()
    mlp_sum.finish()
    tall_sum.finish()
    wide_sum.finish()
    for number in range(chunks - 2, chunks):
        sent(sib_send.at[0], kv_sems.at[0, number], place.sibling)
    for step in range(groups - 2, groups):
        sent(side_send.at[0], kv_sems.at[2, step], place.across)
    for step in range(groups - 3, groups - 1):
        sent(z_send.at[0], kv_sems.at[4, step], place.sibling)


def vmem_specs(count):
    return [pl.BlockSpec(memory_space=pltpu.VMEM)] * count


def params(collective):
    return pltpu.CompilerParams(
        collective_id=collective, has_side_effects=True, vmem_limit_bytes=VMEM_LIMIT
    )


def attend(groups, slots, kv_own, qt, x_in, out_weight, cot):
    rows, features = x_in.shape
    half = rows // 2
    total = groups * QUAD * rows
    width, queries = qt.shape
    dma = pltpu.SemaphoreType.DMA
    shape = jax.ShapeDtypeStruct
    return pl.pallas_call(
        functools.partial(attend_kernel, groups, slots),
        out_shape=[
            shape((total, LANES), BF16),
            shape((QUAD * rows, features), BF16),
            shape((half, features), F32),
            shape((rows, out_weight.shape[0]), BF16),
            shape((HEAD_DIM, queries), F32),
            shape((1, queries), F32),
        ],
        in_specs=vmem_specs(5),
        out_specs=vmem_specs(6),
        scratch_shapes=[
            pltpu.VMEM((2, 2 * rows, queries // 2), F32),
            pltpu.VMEM((1, queries), F32),
            pltpu.VMEM((1, queries), F32),
            pltpu.VMEM((rows, features), F32),
            pltpu.VMEM((half, features), BF16),
            pltpu.VMEM((half, features), BF16),
            dma((groups * QUAD,)),
            dma((groups,)),
            dma((groups,)),
            dma((2 * groups,)),
            dma((8,)),
            dma((2,)),
            dma((8,)),
            dma((2,)),
        ],
        compiler_params=params(1),
        name="attend",
    )(kv_own, qt, x_in, out_weight, cot)


def backward(groups, slots, operands):
    (gate_weight, _, _, cot_all, resid, cot, gain, out_weight, att, ot, lse, qt, kv_all) = operands[
        :13
    ]
    weights_in = operands[15]
    rows, inner = att.shape
    half = rows // 2
    features, hidden = gate_weight.shape
    piece = piece_width(hidden)
    layer_rows = QUAD * rows
    width, queries = qt.shape
    chunks = 2 * groups
    both = round_up(weights_in.shape[1], LANES)
    dma = pltpu.SemaphoreType.DMA
    shape = jax.ShapeDtypeStruct
    pass_shape = (rows, LANES)
    wide = jax.ShapeDtypeStruct((2 * features // WIDE_ROWS, WIDE_ROWS, piece), BF16)
    tall = jax.ShapeDtypeStruct((piece // TALL_ROWS, TALL_ROWS, features), BF16)
    outs = (inner // QUAD, features)
    ins_q = (features // QUAD, inner)
    ins_kv = (features // QUAD, weights_in.shape[1] - inner)
    return pl.pallas_call(
        functools.partial(backward_kernel, groups, slots),
        out_shape=[
            shape((rows, features), BF16),
            shape((rows, features), BF16),
            shape((QUAD, *wide.shape), BF16),
            shape((QUAD, *tall.shape), BF16),
            *(shape((QUAD, *column_parts(groups, *dims)), BF16) for dims in (outs, ins_q, ins_kv)),
            shape((1, 2 * features), F32),
            shape((1, both), F32),
        ],
        in_specs=[pl.BlockSpec(memory_space=pl.ANY)] * 3 + vmem_specs(15),
        out_specs=vmem_specs(2) + [pl.BlockSpec(memory_space=pl.ANY)] * 5 + vmem_specs(2),
        scratch_shapes=[
            pltpu.VMEM(wide.shape, BF16),
            pltpu.VMEM(tall.shape, BF16),
            pltpu.VMEM(wide.shape, BF16),
            pltpu.VMEM(tall.shape, BF16),
            pltpu.VMEM((round_up(wide.shape[0], 2) // 2, *wide.shape[1:]), BF16),
            pltpu.VMEM((round_up(tall.shape[0], 2) // 2, *tall.shape[1:]), BF16),
            *chain_sems(wide.shape[0]),
            *chain_sems(tall.shape[0]),
            *layer_sum_scratch(half, features),
            *layer_sum_scratch(half, features),
            pltpu.VMEM((rows, features), BF16),
            pltpu.VMEM((width, queries), BF16),
            pltpu.VMEM((LANES, queries), BF16),
            pltpu.VMEM((queries, LANES), BF16),
            pltpu.VMEM((queries, LANES), BF16),
            pltpu.VMEM((2, 2 * rows, LANES), F32),
            pltpu.VMEM((2, *pass_shape), BF16),
            pltpu.VMEM((chunks, *pass_shape), BF16),
            pltpu.VMEM((2, *pass_shape), BF16),
            pltpu.VMEM((groups, *pass_shape), BF16),
            pltpu.VMEM((2, *pass_shape), BF16),
            pltpu.VMEM((groups, *pass_shape), BF16),
            dma((6, chunks)),
            dma((7,)),
            pltpu.VMEM((HEAD_DIM, queries), F32),
            pltpu.VMEM((rows, LANES), F32),
            pltpu.VMEM((half, features), F32),
            pltpu.VMEM((rows, features), F32),
            pltpu.VMEM((2, half, features), BF16),
            pltpu.VMEM((3, 1, 2 * features), F32),
            pltpu.VMEM((3, 1, both), F32),
            pltpu.VMEM((groups, 1, 2 * features), F32),
            pltpu.VMEM((groups, 1, both), F32),
            dma((16 + 4 * groups + 4,)),
            *column_sum_scratch(groups, *outs),
            *column_sum_scratch(groups, *ins_q),
            *column_sum_scratch(groups, *ins_kv),
            pltpu.VMEM((features, piece), BF16),
            pltpu.VMEM((features, piece), BF16),
            pltpu.VMEM((piece, features), BF16),
            pltpu.VMEM((layer_rows, features), BF16),
            pltpu.VMEM((layer_rows, piece), BF16),
            pltpu.VMEM((layer_rows, 2 * piece), BF16),
            pltpu.VMEM((layer_rows, features), BF16),
            pltpu.VMEM((layer_rows, features), BF16),
            dma((8,)),
            dma((2,)),
            dma((8,)),
        ],
        compiler_params=params(2),
        name="backward",
    )(*operands)


def rope_tables(positions, head_size):
    half_size = head_size // 2
    exponent = jnp.arange(half_size, dtype=F32) * (2.0 / head_size)
    frequency = jnp.power(ROPE_BASE, -exponent)
    angle = positions.astype(F32)[:, None] * frequency[None, :]
    return (jnp.cos(angle)[:, None, :], jnp.sin(angle)[:, None, :])


def rotate(values, cosine, sine):
    half_size = values.shape[-1] // 2
    first = values[..., :half_size]
    second = values[..., half_size:]
    return jnp.concatenate(
        [first * cosine - second * sine, second * cosine + first * sine], axis=-1
    )


def piece_width(hidden):
    return round_up(hidden // LANES, QUAD) // QUAD * LANES


def per_device(
    groups,
    layer_input,
    block_order,
    attn_gain,
    query_weight,
    query_bias,
    key_weight,
    key_bias,
    value_weight,
    value_bias,
    out_weight,
    mlp_gain,
    gate_weight,
    up_weight,
    down_weight,
    out_cotangent,
):
    rows, features = layer_input.shape
    block_rows = rows // 2
    slots = block_order.shape[0]
    hidden = gate_weight.shape[1]
    heads = query_weight.shape[1] // HEAD_DIM
    piece = piece_width(hidden)
    queries = round_up(heads * rows, 4 * LANES)
    width = round_up(HEAD_DIM + slots + 16, LANES)
    scale = HEAD_DIM ** (-0.5)
    seq_index = lax.axis_index("seq")
    own_slots = lax.dynamic_slice_in_dim(block_order, 2 * seq_index, 2)
    steps_in = jnp.arange(block_rows, dtype=jnp.int32)
    own_places = (own_slots[:, None] * block_rows + steps_in[None, :]).reshape(-1)
    cosine, sine = rope_tables(own_places, HEAD_DIM)
    inputs = layer_input.astype(F32)
    factor_first = lax.rsqrt(jnp.mean(inputs * inputs, axis=-1, keepdims=True) + EPSILON)
    normed_first = inputs * factor_first
    normed_attn = (normed_first * attn_gain).astype(BF16)
    query_rows = (
        jnp.dot(normed_attn, query_weight, preferred_element_type=F32) + query_bias
    ).reshape(rows, heads, HEAD_DIM)
    key_rows = (jnp.dot(normed_attn, key_weight, preferred_element_type=F32) + key_bias).reshape(
        rows, 1, HEAD_DIM
    )
    value_rows = (
        jnp.dot(normed_attn, value_weight, preferred_element_type=F32) + value_bias
    ).astype(BF16)
    query_rot = rotate(query_rows, cosine, sine).astype(BF16)
    key_rot = rotate(key_rows, cosine, sine).astype(BF16).reshape(rows, HEAD_DIM)
    kv_own = jnp.concatenate([key_rot, value_rows], axis=1)
    query_t = jnp.transpose(query_rot * jnp.asarray(scale, BF16), (2, 1, 0)).reshape(
        HEAD_DIM, heads * rows
    )
    later = block_order[:, None] > jnp.repeat(own_slots, block_rows)[None, :]
    bias = jnp.tile(jnp.where(later, NEGATIVE, 0.0).astype(BF16), (1, heads))
    qt = jnp.concatenate(
        [query_t, bias, jnp.zeros((width - HEAD_DIM - slots, heads * rows), BF16)], axis=0
    )
    qt = jnp.pad(qt, ((0, 0), (0, queries - heads * rows)))
    gain_row = mlp_gain[None, :]

    kv_all, cot_all, resid, att, ot, lse = attend(
        groups, slots, kv_own, qt, layer_input, out_weight, out_cotangent
    )

    weights_in = jnp.concatenate([query_weight, key_weight, value_weight], axis=1)
    tables = tuple(
        jnp.pad(
            jnp.tile(jnp.transpose(table[:, 0, :]), (1, heads)),
            ((0, 0), (0, queries - heads * rows)),
        )
        for table in (cosine, sine)
    )
    layer_output, input_grad, wide_sum, tall_sum, outs, ins_q, ins_kv, gains, biases = backward(
        groups,
        slots,
        (
            gate_weight, up_weight, down_weight, cot_all, resid, out_cotangent, gain_row, out_weight,
            att, ot, lse, qt, kv_all, layer_input, attn_gain[None, :], weights_in, *tables,
        ),
    )

    keep = hidden - (QUAD - 1) * piece
    wide_sum = wide_sum.reshape(QUAD, 2, features, piece)
    tall_sum = tall_sum.reshape(QUAD, piece, features)

    def side_by_side(number):
        parts = [wide_sum[i, number] for i in range(QUAD - 1)] + [
            wide_sum[QUAD - 1, number][:, :keep]
        ]
        return jnp.concatenate(parts, axis=1).astype(F32)

    gate_sum, up_sum = side_by_side(0), side_by_side(1)
    down_sum = tall_sum.reshape(QUAD * piece, features)[:hidden].astype(F32)

    query_width = heads * HEAD_DIM

    def quarters(parts, row_count):
        parts = parts.reshape(QUAD, -1, parts.shape[-1])[:, : row_count // QUAD]
        return parts.reshape(row_count, -1).astype(F32)

    out_grad = quarters(outs, query_width)
    query_grad = quarters(ins_q, features)
    key_value = quarters(ins_kv, features)
    key_grad, value_grad = key_value[:, :HEAD_DIM], key_value[:, HEAD_DIM:]
    attn_gain_grad, mlp_gain_grad = gains[0, :features], gains[0, features:]
    query_bias_grad = biases[0, :query_width]
    key_bias_grad = biases[0, query_width : query_width + HEAD_DIM]
    value_bias_grad = biases[0, query_width + HEAD_DIM : query_width + 2 * HEAD_DIM]
    return (
        layer_output,
        input_grad,
        attn_gain_grad,
        query_grad,
        query_bias_grad,
        key_grad,
        key_bias_grad,
        value_grad,
        value_bias_grad,
        out_grad,
        mlp_gain_grad,
        gate_sum,
        up_sum,
        down_sum,
    )


def solution(mesh):
    groups = mesh.shape["seq"] // QUAD
    by_rows, columns, rows, vector, whole = (
        P("seq", None),
        P(None, "tp"),
        P("tp", None),
        P("tp"),
        P(),
    )
    return jax.shard_map(
        functools.partial(per_device, groups),
        mesh=mesh,
        in_specs=(
            by_rows, whole, whole, columns, vector, columns, vector, columns, vector, rows,
            whole, columns, columns, rows, by_rows,
        ),
        out_specs=(
            by_rows, by_rows, whole, columns, vector, columns, vector, columns, vector, rows,
            whole, columns, columns, rows,
        ),
        check_vma=False,
    )
```

```python
import functools

import jax
import jax.numpy as jnp
from jax import lax
from jax.experimental import pallas as pl
from jax.experimental.pallas import tpu as pltpu
from jax.sharding import PartitionSpec as P

HEAD_DIM = 64
EPSILON = 1e-06
NEGATIVE = -1e30
ROPE_BASE = 1000000.0
LANES = 128
QUAD = 4
WIDE_ROWS = 128
TALL_ROWS = 64
SHARE = (2, 2, 2, 2, 1, 1, 1, 2, 1, 1, 2, 1, 1, 1, 1)
PACE = 2
MESH = pl.DeviceIdType.MESH
VMEM_LIMIT = 62 * 1024 * 1024
BF16 = jnp.bfloat16
F32 = jnp.float32


def round_up(value, step):
    return -(-value // step) * step


def nn(left, right):
    return lax.dot_general(left, right, (((1,), (0,)), ((), ())), preferred_element_type=F32)


def nt(left, right):
    return lax.dot_general(left, right, (((1,), (1,)), ((), ())), preferred_element_type=F32)


def tn(left, right):
    return lax.dot_general(left, right, (((0,), (0,)), ((), ())), preferred_element_type=F32)


class Place:
    def __init__(self, groups):
        seq = lax.axis_index("seq").astype(jnp.int32)
        tp = lax.axis_index("tp").astype(jnp.int32)
        self.groups = groups
        self.seq = seq
        self.tp = tp
        self.group = seq // QUAD
        self.quad = seq % QUAD
        self.core = seq % 2
        self.side = (seq // 2) % 2
        self.sibling = (seq + 1 - 2 * self.core, tp)
        self.across = (seq + 2 - 4 * self.side, tp)
        self.partner = (seq, 1 - tp)

    def seq_at(self, group, side, core):
        return group * QUAD + side * 2 + core

    def in_group(self, group):
        return (group * QUAD + self.quad, self.tp)


def send(src, dst, send_sem, recv_sem, device):
    pltpu.make_async_remote_copy(
        src_ref=src,
        dst_ref=dst,
        send_sem=send_sem,
        recv_sem=recv_sem,
        device_id=device,
        device_id_type=MESH,
    ).start()


def sent(src, send_sem, device):
    pltpu.make_async_remote_copy(
        src_ref=src,
        dst_ref=src,
        send_sem=send_sem,
        recv_sem=send_sem,
        device_id=device,
        device_id_type=MESH,
    ).wait_send()


def arrived(dst, recv_sem, device):
    pltpu.make_async_remote_copy(
        src_ref=dst,
        dst_ref=dst,
        send_sem=recv_sem,
        recv_sem=recv_sem,
        device_id=device,
        device_id_type=MESH,
    ).wait_recv()


def meet(place, whole_column):
    barrier = pltpu.get_barrier_semaphore()
    for device in (place.sibling, place.across, place.partner):
        pl.semaphore_signal(barrier, inc=1, device_id=device, device_id_type=MESH)
    if whole_column:
        for step in range(1, place.groups):
            other = place.in_group((place.group + step) % place.groups)
            pl.semaphore_signal(barrier, inc=1, device_id=other, device_id_type=MESH)
        pl.semaphore_wait(barrier, 3 + place.groups - 1)
    else:
        pl.semaphore_wait(barrier, 3)


class LayerGather:
    def __init__(self, place, all_ref, half, recv, part, sems):
        self.place = place
        self.all_ref = all_ref
        self.half = half
        self.first = round_up(half // 2, 16)
        self.recv, self.part, self.sems = recv, part, sems

    def index(self, flip_side, flip_core, flip_tp):
        place = self.place
        side = 1 - place.side if flip_side else place.side
        core = 1 - place.core if flip_core else place.core
        tp = 1 - place.tp if flip_tp else place.tp
        return (side * 2 + core) * 2 + tp

    def rows(self, block, start=0, size=None):
        size = self.half if size is None else size
        return self.all_ref.at[pl.ds(pl.multiple_of(block * self.half + start, 16), size)]

    def start(self, numbers=(0, 1, 2)):
        place = self.place
        own = self.index(0, 0, 0)
        devices = (place.across, place.partner, place.sibling)
        for number in numbers:
            send(
                self.rows(own),
                self.rows(own),
                self.sems.at[number],
                self.recv.at[own],
                devices[number],
            )

    def from_across(self):
        place = self.place
        block = self.index(1, 0, 0)
        arrived(self.rows(block), self.recv.at[block], place.across)
        part = self.rows(block, 0, self.first)
        send(part, part, self.sems.at[3], self.part.at[0], place.partner)
        send(self.rows(block), self.rows(block), self.sems.at[4], self.recv.at[block], place.sibling)

    def from_partner(self):
        place = self.place
        block = self.index(0, 0, 1)
        arrived(self.rows(block), self.recv.at[block], place.partner)
        part = self.rows(block, self.first, self.half - self.first)
        send(part, part, self.sems.at[5], self.part.at[1], place.across)
        send(self.rows(block), self.rows(block), self.sems.at[6], self.recv.at[block], place.sibling)

    def diagonal(self):
        place = self.place
        block = self.index(1, 0, 1)
        arrived(self.rows(block, 0, self.first), self.part.at[0], place.partner)
        arrived(self.rows(block, self.first, self.half - self.first), self.part.at[1], place.across)
        send(self.rows(block), self.rows(block), self.sems.at[7], self.recv.at[block], place.sibling)

    def from_sibling(self, flip_side, flip_tp):
        block = self.index(flip_side, 1, flip_tp)
        arrived(self.rows(block), self.recv.at[block], self.place.sibling)

    def finish(self, waited=False):
        place = self.place
        if not waited:
            for side in (0, 1):
                for tp in (0, 1):
                    self.from_sibling(side, tp)
        own = self.index(0, 0, 0)
        for number, device in enumerate((place.across, place.partner, place.sibling)):
            sent(self.rows(own), self.sems.at[number], device)
        sent(self.rows(own, 0, self.first), self.sems.at[3], place.partner)
        sent(self.rows(own), self.sems.at[4], place.sibling)
        sent(self.rows(own, self.first, self.half - self.first), self.sems.at[5], place.across)
        sent(self.rows(own), self.sems.at[6], place.sibling)
        sent(self.rows(own), self.sems.at[7], place.sibling)


def extended_keys(kv, chip, rows, width, slots):
    count = kv.shape[0]
    lane = lax.broadcasted_iota(jnp.int32, (count, width), 1) - HEAD_DIM
    row = lax.broadcasted_iota(jnp.int32, (count, width), 0)
    block = rows // 2
    number = jnp.zeros_like(row)
    for edge in range(block, count, block):
        number = number + (row >= edge).astype(jnp.int32)
    hot = (lane == number + chip * (count // block)) | ((lane >= slots) & (lane < slots + 3))
    extra = jnp.where(hot, 1.0, 0.0).astype(BF16)
    if width == LANES:
        return jnp.where(lane < 0, kv, extra)
    first = jnp.where(lane[:, :LANES] < 0, kv, extra[:, :LANES])
    return jnp.concatenate([first, extra[:, LANES:]], axis=1)


def hide_later(scores, place, rows, half_number, first):
    count, width = scores.shape
    half = rows // 2
    key = lax.broadcasted_iota(jnp.int32, (count, 1), 0) - place.core * rows - half_number * half
    query = (lax.broadcasted_iota(jnp.int32, (1, width), 1) + first) % half
    return jnp.where((key > query) & (key < half), NEGATIVE, scores)


def split_rows(values, at, count):
    one = values.astype(BF16).astype(F32)
    two = (values - one).astype(BF16).astype(F32)
    three = values - one - two
    row = lax.broadcasted_iota(jnp.int32, (count, values.shape[1]), 0) - at
    picked = jnp.where(row == 0, one, jnp.where(row == 1, two, jnp.where(row == 2, three, 0.0)))
    return picked.astype(BF16)


def attend_kernel(
    groups,
    slots,
    kv_own,
    qt,
    x_in,
    out_weight,
    cot,
    kv_all,
    cot_all,
    resid_out,
    att_out,
    ot_out,
    lse_out,
    s_buf,
    m_buf,
    l_buf,
    part_send,
    part_recv,
    kv_recv,
    kv_z,
    kv_x,
    kv_sib,
    c_recv,
    c_part,
    c_sems,
    p_sems,
):
    place = Place(groups)
    rows = kv_own.shape[0]
    half = rows // 2
    span = 2 * rows
    width, queries = qt.shape
    block = queries // 2
    chunks = 2 * groups
    heads = out_weight.shape[0] // HEAD_DIM

    kv_all[pl.ds(place.seq * rows, rows), :] = kv_own[...]
    own_half = place.quad * 2 + place.tp
    cot_all[pl.ds(pl.multiple_of(own_half * half, 16), half), :] = cot[
        pl.ds(pl.multiple_of(place.tp * half, 16), half), :
    ]
    meet(place, True)

    def kv_rows(seq):
        return kv_all.at[pl.ds(pl.multiple_of(seq * rows, 16), rows)]

    gather_cot = LayerGather(place, cot_all, half, c_recv, c_part, c_sems)
    own = kv_rows(place.seq)
    send(own, own, kv_sib.at[0], kv_recv.at[place.seq], place.sibling)
    for step in range(1, groups):
        other = place.in_group((place.group + step) % groups)
        send(own, own, kv_z.at[step - 1], kv_recv.at[place.seq], other)
    send(own, own, kv_x.at[0], kv_recv.at[place.seq], place.across)
    gather_cot.start((1, 2))

    def chunk_place(number):
        odd = number % 2
        far = jnp.where(number < 2, odd, jnp.where(number == 2, 0, 1 - odd))
        distance = jnp.where(number < 2, 0, jnp.where(odd == 1, (number + 1) // 2, number // 2 - 1))
        distance = jnp.where(number == 2, 1, distance)
        last = number == chunks - 1
        far = jnp.where(last, 1, far)
        distance = jnp.where(last, groups - 1, distance)
        up = jnp.where(place.group < groups // 2, distance, groups - distance)
        group = (place.group + up) % groups
        side = place.side + far * (1 - 2 * place.side)
        return group, side, distance, far

    def pass_on(number):
        group, side, distance, far = chunk_place(number)
        seq = place.seq_at(group, side, place.core)
        view = kv_rows(seq)
        arrived(view, kv_recv.at[seq], place.across)
        send(view, view, kv_sib.at[number], kv_recv.at[seq], place.sibling)

        @pl.when(far == 0)
        def near():
            send(view, view, kv_x.at[distance], kv_recv.at[seq], place.across)

    def ready(number):
        group, side, _, _ = chunk_place(number)
        seq = place.seq_at(group, side, 1 - place.core)
        arrived(kv_rows(seq), kv_recv.at[seq], place.sibling)

    def kv_chunk(number):
        group, side, _, _ = chunk_place(number)
        chip = group * 2 + side
        return chip, kv_all[pl.ds(pl.multiple_of(chip * span, 16), span), :]

    def lanes_of(half_number):
        return pl.ds(pl.multiple_of(half_number * block, LANES), block)

    def scores(half_number, number, slot, own_chip=False):
        chip, kv = kv_chunk(number)
        keys = extended_keys(kv, chip, rows, width, slots)
        value = nn(keys, qt[:, lanes_of(half_number)])
        if own_chip:
            value = hide_later(value, place, rows, half_number, 0)
        s_buf[slot] = value

    def absorb(half_number, number, slot):
        chip, kv = kv_chunk(number)
        lanes = lanes_of(half_number)
        value = s_buf[slot]
        old = m_buf[:, lanes]
        top = jnp.maximum(old, jnp.max(value, axis=0, keepdims=True))
        shrink = jnp.exp(old - top)
        weights = jnp.exp(value - top)
        total = jnp.sum(weights, axis=0, keepdims=True)
        product = tn(kv[:, HEAD_DIM:], weights.astype(BF16))
        m_buf[:, lanes] = top
        l_buf[:, lanes] = total + l_buf[:, lanes] * shrink
        ot_out[:, lanes] = product + ot_out[:, lanes] * shrink

    m_buf[...] = jnp.full(m_buf.shape, NEGATIVE, F32)
    l_buf[...] = jnp.zeros_like(l_buf)
    ot_out[...] = jnp.zeros_like(ot_out)

    def comes(number):
        @pl.when(number + 2 < chunks)
        def look_ahead():
            pass_on(number + 2)

        @pl.when(number < chunks)
        def next_ready():
            ready(number)

    def sweep(half_number, waits, following):
        def two_chunks(pair, unused):
            if waits:
                comes(2 * pair + 1)
            scores(half_number, 2 * pair + 1, 1)
            absorb(half_number, 2 * pair, 0)
            if waits:
                comes(2 * pair + 2)
            scores(half_number, 2 * pair + 2, 0)
            absorb(half_number, 2 * pair + 1, 1)
            return unused

        lax.fori_loop(0, groups - 1, two_chunks, 0)
        if waits:
            comes(chunks - 1)
        scores(half_number, chunks - 1, 1)
        absorb(half_number, chunks - 2, 0)
        if following is not None:
            scores(following, 0, 0, True)
        absorb(half_number, chunks - 1, 1)

    def close_half(half_number):
        lanes = lanes_of(half_number)
        ot = ot_out[:, lanes] / l_buf[:, lanes]
        ot_out[:, lanes] = ot
        lse_out[:, lanes] = m_buf[:, lanes] + jnp.log(l_buf[:, lanes])
        natural = jnp.transpose(ot).astype(BF16)
        att = jnp.concatenate(
            [natural[head * half : (head + 1) * half, :] for head in range(heads)], axis=1
        )
        att_out[pl.ds(pl.multiple_of(half_number * half, 16), half), :] = att
        return nn(att, out_weight[...])

    theirs, mine = 1 - place.tp, place.tp
    ready(0)
    scores(theirs, 0, 0, True)
    pass_on(1)
    pass_on(2)
    sweep(theirs, True, mine)
    gather_cot.start((0,))
    part_send[...] = close_half(theirs).astype(BF16)
    send(part_send, part_recv, p_sems.at[0], p_sems.at[1], place.partner)
    gather_cot.from_partner()
    sweep(mine, False, None)
    gather_cot.from_across()
    my_rows = pl.ds(pl.multiple_of(place.tp * half, 16), half)
    resid = close_half(mine) + x_in[my_rows, :].astype(F32)
    gather_cot.diagonal()
    arrived(part_recv, p_sems.at[1], place.partner)
    resid_out[...] = resid + part_recv[...].astype(F32)
    gather_cot.finish()
    sent(part_send, p_sems.at[0], place.partner)

    def close(number, unused):
        sent(own, kv_sib.at[number], place.sibling)
        return unused

    lax.fori_loop(0, chunks, close, 0)
    for step_out in range(groups):
        sent(own, kv_x.at[step_out], place.across)
    for step_out in range(1, groups):
        sent(own, kv_z.at[step_out - 1], place.in_group((place.group + step_out) % groups))


class ChainSum:
    def __init__(self, place, own, incoming, at_root, final, sems):
        self.place = place
        self.own, self.incoming, self.at_root, self.final = own, incoming, at_root, final
        self.count = own.shape[0]
        (
            self.up_recv,
            self.up_send,
            self.fin_recv,
            self.fin_send,
            self.x_recv,
            self.x_send,
            self.c_recv,
            self.c_send,
            self.keep,
        ) = sems

    def root(self, parity):
        return self.place.groups // 2 - 1 + parity

    def lag_up(self, parity):
        groups, group, root = self.place.groups, self.place.group, self.root(parity)
        most = max(root, groups - 1 - root)
        return PACE * jnp.where(
            group < root, group, jnp.where(group > root, groups - 1 - group, most)
        )

    def lag_down(self, parity):
        groups, group, root = self.place.groups, self.place.group, self.root(parity)
        most = max(root, groups - 1 - root)
        return PACE * (most + jnp.abs(group - root))

    def total_steps(self):
        groups = self.place.groups
        most = groups // 2
        return self.count + PACE * (2 * most + 1)

    def spread(self, i, view):
        place = self.place
        final = self.final.at[place.quad, i]
        send(view, final, self.x_send.at[i], self.x_recv.at[i], place.across)
        send(view, final, self.c_send.at[0, i], self.c_recv.at[0, i], place.sibling)

    def up(self, i, parity):
        place, root = self.place, self.root(parity)
        group, last = place.group, place.groups - 1
        mine = self.own.at[i]

        here, second = self.incoming.at[i], self.at_root.at[i // 2]

        def add(way, ref):
            arrived(ref, self.up_recv.at[way, i], place.in_group(group - 1 + 2 * way))
            mine[...] = (mine[...].astype(F32) + ref[...].astype(F32)).astype(BF16)

        def onward(way, dst, send_sem, recv_sem):
            send(mine, dst, send_sem, recv_sem, place.in_group(group + 1 - 2 * way))

        @pl.when((group > 0) & (group <= root))
        def from_left():
            add(0, here)

        @pl.when((group < last) & (group > root))
        def from_right():
            add(1, here)

        @pl.when((group < last) & (group == root))
        def from_right_to_root():
            add(1, second)

        @pl.when(group < root)
        def to_right():
            onward(0, here, self.up_send.at[i], self.up_recv.at[0, i])

        @pl.when(group > root + 1)
        def to_left():
            onward(1, here, self.up_send.at[i], self.up_recv.at[1, i])

        @pl.when(group == root + 1)
        def to_root():
            onward(1, second, self.up_send.at[i], self.up_recv.at[1, i])

        @pl.when(group == root)
        def finished():
            final = self.final.at[place.quad, i]

            @pl.when(group > 0)
            def left():
                onward(1, final, self.fin_send.at[0, i], self.fin_recv.at[i])

            @pl.when(group < last)
            def right():
                onward(0, final, self.fin_send.at[1, i], self.fin_recv.at[i])

            self.spread(i, mine)
            pltpu.make_async_copy(mine, final, self.keep.at[i]).start()

    def down(self, i, parity):
        place, root = self.place, self.root(parity)
        group, last = place.group, place.groups - 1
        view = self.final.at[place.quad, i]

        @pl.when(group != root)
        def take():
            arrived(view, self.fin_recv.at[i], place.sibling)

            @pl.when((group < root) & (group > 0))
            def left():
                send(
                    view,
                    view,
                    self.fin_send.at[0, i],
                    self.fin_recv.at[i],
                    place.in_group(group - 1),
                )

            @pl.when((group > root) & (group < last))
            def right():
                send(
                    view,
                    view,
                    self.fin_send.at[1, i],
                    self.fin_recv.at[i],
                    place.in_group(group + 1),
                )

            self.spread(i, view)

    def cross(self, i):
        place = self.place
        view = self.final.at[place.across[0] % QUAD, i]
        arrived(view, self.x_recv.at[i], place.across)
        send(view, view, self.c_send.at[1, i], self.c_recv.at[1, i], place.sibling)

    def step(self, number):
        for parity in (0, 1):
            i = number - self.lag_up(parity)

            @pl.when((i >= 0) & (i < self.count) & (i % 2 == parity))
            def go_up(i=i, parity=parity):
                self.up(i, parity)

        for parity in (0, 1):
            i = number - self.lag_down(parity)

            @pl.when((i >= 0) & (i < self.count) & (i % 2 == parity))
            def go_down(i=i, parity=parity):
                self.down(i, parity)

        for parity in (0, 1):
            i = number - self.lag_down(parity) - PACE

            @pl.when((i >= 0) & (i < self.count) & (i % 2 == parity))
            def go_cross(i=i):
                self.cross(i)

    def finish(self):
        place = self.place
        group, last = place.group, place.groups - 1
        sibling_quad = place.sibling[0] % QUAD
        diagonal = 3 - place.quad

        def close(i, unused):
            root = place.groups // 2 - 1 + i % 2
            view = self.own.at[i]
            arrived(self.final.at[sibling_quad, i], self.c_recv.at[0, i], place.sibling)
            arrived(self.final.at[diagonal, i], self.c_recv.at[1, i], place.sibling)

            @pl.when(group != root)
            def up_done():
                sent(view, self.up_send.at[i], place.sibling)

            @pl.when(group == root)
            def kept():
                final = self.final.at[place.quad, i]
                pltpu.make_async_copy(view, final, self.keep.at[i]).wait()

            @pl.when((group <= root) & (group > 0))
            def left_done():
                sent(view, self.fin_send.at[0, i], place.sibling)

            @pl.when((group >= root) & (group < last))
            def right_done():
                sent(view, self.fin_send.at[1, i], place.sibling)

            sent(view, self.x_send.at[i], place.across)
            sent(view, self.c_send.at[0, i], place.sibling)
            sent(view, self.c_send.at[1, i], place.sibling)
            return unused

        lax.fori_loop(0, self.count, close, 0)


def chain_sems(count):
    dma = pltpu.SemaphoreType.DMA
    return [
        dma((2, count)),
        dma((count,)),
        dma((count,)),
        dma((2, count)),
        dma((count,)),
        dma((count,)),
        dma((2, count)),
        dma((2, count)),
        dma((count,)),
    ]


class LayerSum:
    def __init__(self, place, part, half, core_in, left, right, left_in, right_in, last_in, sems):
        self.place, self.part, self.half = place, part, half
        self.core_in, self.left, self.right = core_in, left, right
        self.left_in, self.right_in, self.last_in = left_in, right_in, last_in
        self.sems = sems
        self.cut = left.shape[2]
        self.columns = part.shape[1]

    def rows(self, side, core):
        size = 2 * self.half
        return pl.ds(pl.multiple_of((side * 2 + core) * size, 16), size)

    def start(self):
        place = self.place
        for side in (0, 1):
            view = self.part.at[self.rows(side, 1 - place.core)]
            send(
                view,
                self.core_in.at[side],
                self.sems.at[side],
                self.sems.at[2 + side],
                place.sibling,
            )

    def own_rows(self, tp):
        return pl.ds(pl.multiple_of(tp * self.half, 16), self.half)

    def after_core(self):
        place = self.place
        for side in (0, 1):
            arrived(self.core_in.at[side], self.sems.at[2 + side], place.sibling)
            total = self.part[self.rows(side, place.core), :].astype(F32) + self.core_in[
                side
            ].astype(F32)
            self.left[side] = total[:, : self.cut].astype(BF16)
            self.right[side] = total[:, self.cut :].astype(BF16)

    def cross(self):
        place = self.place
        for side in (0, 1):
            send(
                self.left.at[side, self.own_rows(1 - place.tp)],
                self.left_in.at[side],
                self.sems.at[4 + side],
                self.sems.at[6 + side],
                place.partner,
            )
        send(
            self.right.at[1 - place.side],
            self.right_in,
            self.sems.at[8],
            self.sems.at[9],
            place.across,
        )

    def after_cross(self):
        place = self.place
        mine = self.own_rows(place.tp)
        for side in (0, 1):
            arrived(self.left_in.at[side], self.sems.at[6 + side], place.partner)
            self.left_in[side] = (
                self.left[side, mine, :].astype(F32) + self.left_in[side].astype(F32)
            ).astype(BF16)
        arrived(self.right_in, self.sems.at[9], place.across)
        self.right_in[...] = (
            self.right[place.side].astype(F32) + self.right_in[...].astype(F32)
        ).astype(BF16)
        send(
            self.left_in.at[1 - place.side],
            self.last_in.at[:, : self.cut],
            self.sems.at[10],
            self.sems.at[11],
            place.across,
        )
        send(
            self.right_in.at[self.own_rows(1 - place.tp)],
            self.last_in.at[:, self.cut :],
            self.sems.at[12],
            self.sems.at[13],
            place.partner,
        )

    def result(self):
        place = self.place
        arrived(self.last_in.at[:, : self.cut], self.sems.at[11], place.across)
        arrived(self.last_in.at[:, self.cut :], self.sems.at[13], place.partner)
        mine = jnp.concatenate(
            [self.left_in[place.side], self.right_in[self.own_rows(place.tp), :]], axis=1
        )
        return mine.astype(F32) + self.last_in[...].astype(F32)

    def finish(self):
        place = self.place
        for side in (0, 1):
            sent(self.core_in.at[side], self.sems.at[side], place.sibling)
            sent(self.left_in.at[side], self.sems.at[4 + side], place.partner)
        sent(self.right_in, self.sems.at[8], place.across)
        sent(self.last_in.at[:, : self.cut], self.sems.at[10], place.across)
        sent(self.last_in.at[:, self.cut :], self.sems.at[12], place.partner)


class QuadSum:
    def __init__(self, place, part, own, core_in, x_send, x_in, sems):
        self.place, self.part, self.own = place, part, own
        self.core_in, self.x_send, self.x_in, self.sems = core_in, x_send, x_in, sems

    def start(self):
        place = self.place
        for side in (0, 1):
            send(
                self.part.at[side * 2 + 1 - place.core],
                self.core_in.at[side],
                self.sems.at[side],
                self.sems.at[2 + side],
                place.sibling,
            )

    def total(self, side):
        return self.part[side * 2 + self.place.core].astype(F32) + self.core_in[side].astype(F32)

    def middle(self):
        place = self.place
        for side in (0, 1):
            arrived(self.core_in.at[side], self.sems.at[2 + side], place.sibling)
        self.x_send[...] = self.total(1 - place.side).astype(BF16)
        send(self.x_send, self.x_in, self.sems.at[4], self.sems.at[5], place.across)

    def end(self):
        place = self.place
        arrived(self.x_in, self.sems.at[5], place.across)
        mine = (self.total(place.side) + self.x_in[...].astype(F32)).astype(BF16)
        count, step = self.own.shape[0], self.own.shape[1]
        for i in range(count):
            piece = mine[i * step : (i + 1) * step, :]
            if piece.shape[0]:
                self.own[i, : piece.shape[0], :] = piece
            if piece.shape[0] < step:
                left = step - piece.shape[0]
                self.own[i, piece.shape[0] :, :] = jnp.zeros((left, piece.shape[1]), BF16)

    def finish(self):
        place = self.place
        for side in (0, 1):
            sent(self.core_in.at[side], self.sems.at[side], place.sibling)
        sent(self.x_send, self.sems.at[4], place.across)


class ColumnSum:
    def __init__(self, place, own, incoming, final, sems):
        self.place, self.own, self.incoming, self.final = place, own, incoming, final
        self.rs_send, self.rs_recv, self.ag_send, self.ag_recv = (sems.at[i] for i in range(4))
        self.x_send, self.x_recv, self.c_send, self.c_recv = (sems.at[i] for i in range(4, 8))
        self.d_send, self.d_recv = (sems.at[i] for i in range(8, 10))

    def others(self):
        place = self.place
        for step in range(1, place.groups):
            yield step, (place.group + step) % place.groups

    def start(self):
        place = self.place
        for step, other in self.others():
            back = place.groups - step
            send(
                self.own.at[other],
                self.incoming.at[back],
                self.rs_send.at[step],
                self.rs_recv.at[back],
                place.in_group(other),
            )

    def spread(self, part, view):
        place = self.place
        final = self.final.at[place.quad, part]
        send(view, final, self.x_send.at[part], self.x_recv.at[part], place.across)
        send(view, final, self.c_send.at[part], self.c_recv.at[part], place.sibling)

    def middle(self):
        place = self.place
        mine = self.own.at[place.group]
        total = mine[...].astype(F32)
        for step, other in self.others():
            arrived(self.incoming.at[step], self.rs_recv.at[step], place.sibling)
            total = total + self.incoming[step].astype(F32)
        mine[...] = total.astype(BF16)
        final = self.final.at[place.quad, place.group]
        for step, other in self.others():
            send(
                mine,
                final,
                self.ag_send.at[step],
                self.ag_recv.at[place.group],
                place.in_group(other),
            )
        self.spread(place.group, mine)
        pltpu.make_async_copy(mine, final, self.ag_send.at[0]).start()

    def end(self):
        place = self.place
        for step, other in self.others():
            view = self.final.at[place.quad, other]
            arrived(view, self.ag_recv.at[other], place.sibling)
            self.spread(other, view)

    def cross(self):
        place = self.place
        quad = place.across[0] % QUAD
        for step in range(place.groups):
            part = (place.group + step) % place.groups
            view = self.final.at[quad, part]
            arrived(view, self.x_recv.at[part], place.across)
            send(view, view, self.d_send.at[part], self.d_recv.at[part], place.sibling)

    def finish(self):
        place = self.place
        view = self.own.at[0]
        for part in range(place.groups):
            arrived(view, self.c_recv.at[part], place.sibling)
            arrived(view, self.d_recv.at[part], place.sibling)
            sent(view, self.x_send.at[part], place.across)
            sent(view, self.c_send.at[part], place.sibling)
            sent(view, self.d_send.at[part], place.sibling)
        for step, other in self.others():
            sent(view, self.rs_send.at[step], place.sibling)
            sent(view, self.ag_send.at[step], place.sibling)
        final = self.final.at[place.quad, place.group]
        pltpu.make_async_copy(self.own.at[place.group], final, self.ag_send.at[0]).wait()


def column_parts(groups, rows, columns):
    return (groups, round_up(-(-rows // groups), 16), columns)


def column_sum_scratch(groups, rows, columns):
    parts = column_parts(groups, rows, columns)
    return [
        *quad_sum_scratch(rows, columns),
        pltpu.VMEM(parts, BF16),
        pltpu.VMEM(parts, BF16),
        pltpu.SemaphoreType.DMA((10, groups)),
    ]


def quad_sum_scratch(rows, columns):
    return [
        pltpu.VMEM((QUAD, rows, columns), BF16),
        pltpu.VMEM((2, rows, columns), BF16),
        pltpu.VMEM((rows, columns), BF16),
        pltpu.VMEM((rows, columns), BF16),
        pltpu.SemaphoreType.DMA((6,)),
    ]


def layer_sum_scratch(half, columns):
    cut = columns // LANES // 2 * LANES
    if cut * 2 < columns:
        cut += LANES
    return [
        pltpu.VMEM((2, 2 * half, columns), BF16),
        pltpu.VMEM((2, 2 * half, cut), BF16),
        pltpu.VMEM((2, 2 * half, columns - cut), BF16),
        pltpu.VMEM((2, half, cut), BF16),
        pltpu.VMEM((2 * half, columns - cut), BF16),
        pltpu.VMEM((half, columns), BF16),
        pltpu.SemaphoreType.DMA((14,)),
    ]


def backward_kernel(
    groups,
    slots,
    gate_weight,
    up_weight,
    down_weight,
    cot_all,
    resid_in,
    cot,
    gain,
    out_weight,
    att,
    ot,
    lse,
    qt_in,
    kv_all,
    x_in,
    attn_gain,
    weights_in,
    turns,
    turns_rows,
    layer_out,
    input_grad,
    wide,
    tall,
    outs,
    ins_q,
    ins_kv,
    gains,
    biases,
    *scratch,
):
    place = Place(groups)
    wide_own, tall_own, wide_up, tall_up = scratch[0:4]
    wide_root, tall_root = scratch[4:6]
    scratch = scratch[2:]
    wide_sems, tall_sems = scratch[4:13], scratch[13:22]
    sum_g, sum_m = scratch[22:29], scratch[29:36]
    branch, qt, dot_t, q_pad, do_pad, dkv = scratch[36:42]
    sib_send, sib_in, side_send, side_in, z_send, z_in = scratch[42:48]
    kv_sems, pair_sems = scratch[48:50]
    dq_out, dkv_out, resid_grad = scratch[50:53]
    turn_send, turn_in, gain_in, bias_in, gain_z, bias_z, vector_sems = scratch[53:60]
    sum_o, sum_q, sum_kv = scratch[60:68], scratch[68:76], scratch[76:84]
    rows = att.shape[0]
    half = rows // 2
    span = 2 * rows
    width, queries = qt_in.shape
    parts = 2 if groups <= 4 else 8
    block = queries // parts
    chunks = 2 * groups
    heads = out_weight.shape[0] // HEAD_DIM
    my_rows = pl.ds(pl.multiple_of(place.tp * half, 16), half)
    other_rows = pl.ds(pl.multiple_of((1 - place.tp) * half, 16), half)

    tall_sum = ChainSum(place, tall_own, tall_up, tall_root, tall, tall_sems)
    wide_sum = ChainSum(place, wide_own, wide_up, wide_root, wide, wide_sems)
    gate_piece, up_piece, down_piece, normed_all, mixed, grad_gu, grad_part, mlp_part = scratch[84:92]
    gather_sems = scratch[92:95]
    features = resid_in.shape[1]
    piece = gate_piece.shape[1]
    keep = gate_weight.shape[1] - (QUAD - 1) * piece

    def load_weights(size, quad):
        columns = pl.ds(pl.multiple_of(quad * piece, LANES), size)
        pairs = (
            (gate_weight.at[:, columns], gate_piece.at[:, pl.ds(0, size)]),
            (up_weight.at[:, columns], up_piece.at[:, pl.ds(0, size)]),
            (down_weight.at[columns], down_piece.at[pl.ds(0, size)]),
        )
        return [
            pltpu.make_async_copy(src, dst, pair_sems.at[4 + number])
            for number, (src, dst) in enumerate(pairs)
        ]

    last_quad = QUAD - 1

    @pl.when(place.quad < last_quad)
    def whole_piece():
        for copy in load_weights(piece, place.quad):
            copy.start()

    @pl.when(place.quad == last_quad)
    def last_piece():
        for copy in load_weights(keep, last_quad):
            copy.start()
        if keep < piece:
            gate_piece[:, keep:] = jnp.zeros((features, piece - keep), BF16)
            up_piece[:, keep:] = jnp.zeros((features, piece - keep), BF16)
            down_piece[keep:, :] = jnp.zeros((piece - keep, features), BF16)

    grad_sum = LayerSum(place, grad_part, half, *sum_g)
    mlp_sum = LayerSum(place, mlp_part, half, *sum_m)

    def quad_and_column(final, refs):
        quad = QuadSum(place, refs[0], refs[5], *refs[1:5])
        return quad, ColumnSum(place, refs[5], refs[6], final, refs[7])

    outs_quad, outs_sum = quad_and_column(outs, sum_o)
    q_quad, q_sum = quad_and_column(ins_q, sum_q)
    kv_quad, kv_sum = quad_and_column(ins_kv, sum_kv)
    tall_steps = tall_sum.count

    def chain_step(number):
        tall_sum.step(number)
        wide_sum.step(number - tall_steps)

    def chain_steps(first, count):
        def one(number, unused):
            chain_step(number)
            return unused

        lax.fori_loop(first, first + count, one, 0)
        return first + count

    all_steps = tall_steps + wide_sum.total_steps()

    gather = LayerGather(place, normed_all, half, *gather_sems)
    resid = resid_in[...]
    factor = lax.rsqrt(jnp.mean(resid * resid, axis=-1, keepdims=True) + EPSILON)
    own_block = place.quad * 2 + place.tp
    normed_all[pl.ds(pl.multiple_of(own_block * half, 16), half), :] = (
        resid * factor * gain[...]
    ).astype(BF16)
    meet(place, True)
    gather.start()

    @pl.when(place.quad < last_quad)
    def whole_loaded():
        for copy in load_weights(piece, place.quad):
            copy.wait()

    @pl.when(place.quad == last_quad)
    def last_loaded():
        for copy in load_weights(keep, last_quad):
            copy.wait()

    def feed(number, unused):
        @pl.when(number == 1)
        def second():
            gather.from_sibling(0, 0)

        @pl.when(number == 2)
        def third():
            gather.from_partner()
            gather.from_across()

        @pl.when(number == 4)
        def fifth():
            gather.from_sibling(0, 1)

        @pl.when(number == 5)
        def sixth():
            gather.from_sibling(1, 0)
            gather.diagonal()

        @pl.when(number == 7)
        def eighth():
            gather.from_sibling(1, 1)

        def flip(value, numbers):
            turned = functools.reduce(lambda x, y: x | y, [number == i for i in numbers])
            return jnp.where(turned, 1 - value, value)

        side = flip(place.side, (3, 5, 6, 7))
        core = flip(place.core, (1, 4, 5, 7))
        tp = flip(place.tp, (2, 4, 6, 7))
        at_rows = pl.ds(pl.multiple_of(((side * 2 + core) * 2 + tp) * half, 16), half)
        here = normed_all[at_rows, :]
        gate = nn(here, gate_piece[...])
        upward = nn(here, up_piece[...])
        sigmoid = jax.nn.sigmoid(gate)
        silu = gate * sigmoid
        mixed[at_rows, :] = (silu * upward).astype(BF16)
        grad_gu[at_rows, :piece] = (upward * sigmoid * (1.0 + gate * (1.0 - sigmoid))).astype(BF16)
        grad_gu[at_rows, piece:] = silu.astype(BF16)
        return unused

    lax.fori_loop(0, 8, feed, 0)
    tall_own[...] = tn(mixed[...], cot_all[...]).astype(BF16).reshape(tall_own.shape)
    done = chain_steps(0, SHARE[0])

    def feed_back(number, unused):
        core = jnp.where(number < 2, 1 - place.core, place.core)
        at_rows = pl.ds(pl.multiple_of((number % 2 * 2 + core) * rows, 16), rows)
        grad_mixed = nt(cot_all[at_rows, :], down_piece[...])
        grad_gate = (grad_mixed * grad_gu[at_rows, :piece].astype(F32)).astype(BF16)
        grad_upward = (grad_mixed * grad_gu[at_rows, piece:].astype(F32)).astype(BF16)
        grad_gu[at_rows, :piece] = grad_gate
        grad_gu[at_rows, piece:] = grad_upward
        grad_part[at_rows, :] = (
            nt(grad_gate, gate_piece[...]) + nt(grad_upward, up_piece[...])
        ).astype(BF16)
        mlp_part[at_rows, :] = nn(mixed[at_rows, :], down_piece[...]).astype(BF16)
        chain_step(number + SHARE[0])
        return unused

    done += 4
    lax.fori_loop(0, 2, feed_back, 0)
    grad_sum.start()
    lax.fori_loop(2, 4, feed_back, 0)
    grad_sum.after_core()
    grad_sum.cross()
    both = tn(normed_all[...], grad_gu[...])
    count = wide_own.shape[0] // 2
    for number in range(2):
        wide_own[number * count : (number + 1) * count] = (
            both[:, number * piece : (number + 1) * piece]
            .astype(BF16)
            .reshape(count, *wide_own.shape[1:])
        )
    gather.finish(True)

    qt[...] = qt_in[...]
    at = HEAD_DIM + slots
    qt[at : at + 16, :] = split_rows(-lse[...], 0, 16)
    natural_q = jnp.transpose(qt_in[0:HEAD_DIM, :].astype(F32)).astype(BF16)
    q_pad[...] = jnp.concatenate([natural_q, jnp.zeros_like(natural_q)], axis=1)

    mlp_sum.start()
    done = chain_steps(done, SHARE[1])
    grad_sum.after_cross()
    done = chain_steps(done, SHARE[2])

    normed = resid * factor
    grad_normed = grad_sum.result()
    gains[:, features:] = jnp.sum(grad_normed * normed, axis=0, keepdims=True)
    weighted = grad_normed * gain[...]
    inner = jnp.mean(weighted * normed, axis=-1, keepdims=True)
    grad_resid = cot[my_rows, :].astype(F32) + factor * (weighted - normed * inner)
    resid_grad[...] = grad_resid
    branch[my_rows, :] = grad_resid.astype(BF16)
    send(
        branch.at[my_rows],
        branch.at[my_rows],
        pair_sems.at[0],
        pair_sems.at[1],
        place.partner,
    )
    mlp_sum.after_core()
    mlp_sum.cross()
    done = chain_steps(done, SHARE[3])
    arrived(branch.at[other_rows], pair_sems.at[1], place.partner)

    grads = branch[...]
    outs_part = sum_o[0]
    outs_part[...] = tn(att[...], grads).astype(BF16).reshape(outs_part.shape)
    outs_quad.start()
    grad_att = nt(grads, out_weight[...]).astype(BF16)
    half_width = queries // 2
    filler = jnp.zeros((half_width - heads * half, HEAD_DIM), BF16)
    stacked = jnp.concatenate(
        [
            part
            for number in range(2)
            for part in (
                *(
                    grad_att[
                        number * half : (number + 1) * half,
                        head * HEAD_DIM : (head + 1) * HEAD_DIM,
                    ]
                    for head in range(heads)
                ),
                filler,
            )
        ],
        axis=0,
    )
    do_pad[...] = jnp.concatenate([jnp.zeros_like(stacked), stacked], axis=1)
    turned = jnp.transpose(stacked.astype(F32))
    delta = jnp.sum(turned * ot[...], axis=0, keepdims=True)
    dot_t[0:HEAD_DIM, :] = split_rows(-delta, 0, HEAD_DIM)
    dot_t[HEAD_DIM:, :] = turned.astype(BF16)
    done = chain_steps(done, SHARE[4])
    outs_quad.middle()

    def write_layer():
        layer_out[my_rows, :] = (resid_in[...] + mlp_sum.result()).astype(BF16)
        send(
            layer_out.at[my_rows],
            layer_out.at[my_rows],
            pair_sems.at[2],
            pair_sems.at[3],
            place.partner,
        )

    dq_out[...] = jnp.zeros_like(dq_out)

    def chunk_place(number):
        far = 1 - number % 2
        group = (place.group + 1 + number // 2) % groups
        side = place.side + far * (1 - 2 * place.side)
        return group, side

    lane = lax.broadcasted_iota(jnp.int32, (1, LANES), 1)
    ones = jnp.where(lane < 3, 1.0, 0.0).astype(BF16)

    def attend_back(number, slot, own_chip=False):
        group, side = chunk_place(number)
        chip = group * 2 + side
        at_rows = pl.ds(pl.multiple_of(chip * span, 16), span)
        kv = kv_all[at_rows, :]
        keys = extended_keys(kv, chip, rows, width, slots)
        values = jnp.where(lane >= HEAD_DIM, kv, jnp.broadcast_to(ones, kv.shape))
        for part in range(parts):
            lanes = slice(part * block, (part + 1) * block)
            score = nn(keys, qt[:, lanes])
            if own_chip:
                first = part * block
                number_of_half = first // half_width
                score = hide_later(score, place, rows, number_of_half, first % half_width)
            weights = jnp.exp(score)
            change = nn(values, dot_t[:, lanes])
            low = (weights * change).astype(BF16)
            total = nn(weights.astype(BF16), do_pad[lanes, :]) + nn(low, q_pad[lanes, :])
            if part == 0:
                dkv[slot] = total
            else:
                dkv[slot] += total
            dq_out[:, lanes] += tn(kv[:, :HEAD_DIM], low)

    def hand_over(number, slot):
        other = pl.ds(pl.multiple_of((1 - place.core) * rows, 16), rows)

        @pl.when(number >= 2)
        def free_again():
            sent(sib_send.at[slot], kv_sems.at[0, number - 2], place.sibling)

        sib_send[slot] = dkv[slot, other, :].astype(BF16)
        send(
            sib_send.at[slot],
            sib_in.at[number],
            kv_sems.at[0, number],
            kv_sems.at[1, number],
            place.sibling,
        )

    def take_over(number, near, own_group=False):
        group, side = chunk_place(number)
        step = number // 2
        arrived(sib_in.at[number], kv_sems.at[1, number], place.sibling)
        mine = pl.ds(pl.multiple_of(place.core * rows, 16), rows)
        total = dkv[1 if near else 0, mine, :] + sib_in[number].astype(F32)
        if not near:
            ring = step % 2

            @pl.when(step >= 2)
            def side_free():
                sent(side_send.at[0], kv_sems.at[2, step - 2], place.across)

            side_send[ring] = total.astype(BF16)
            send(
                side_send.at[ring],
                side_in.at[step],
                kv_sems.at[2, step],
                kv_sems.at[3, step],
                place.across,
            )
            return
        arrived(side_in.at[step], kv_sems.at[3, step], place.across)
        total = total + side_in[step].astype(F32)
        if own_group:
            dkv_out[...] = total
            return
        ring = step % 2

        @pl.when(step >= 2)
        def column_free():
            sent(z_send.at[0], kv_sems.at[4, step - 2], place.sibling)

        z_send[ring] = total.astype(BF16)
        back = groups - 2 - step
        send(
            z_send.at[ring],
            z_in.at[back],
            kv_sems.at[4, step],
            kv_sems.at[5, back],
            place.in_group(group),
        )

    each = 1

    def pair(step, unused):
        attend_back(2 * step, 0)
        hand_over(2 * step, 0)
        chain_steps(done + 2 * each * step, each)

        @pl.when(step > 0)
        def last_near():
            take_over(2 * step - 1, True)

        attend_back(2 * step + 1, 1)
        hand_over(2 * step + 1, 1)
        take_over(2 * step, False)
        chain_steps(done + 2 * each * step + each, each)

        @pl.when(step == 0)
        def outs_ready():
            mlp_sum.after_cross()
            outs_quad.end()
            outs_sum.start()

        @pl.when(step == 1)
        def layer_ready():
            write_layer()
            outs_sum.middle()

        return unused

    lax.fori_loop(0, groups - 1, pair, 0)
    outs_sum.end()
    done += 2 * each * (groups - 1)
    attend_back(chunks - 2, 0)
    hand_over(chunks - 2, 0)
    done = chain_steps(done, each)
    if groups > 1:
        take_over(chunks - 3, True)
    attend_back(chunks - 1, 1, True)
    hand_over(chunks - 1, 1)
    take_over(chunks - 2, False)
    done = chain_steps(done, SHARE[5])

    quarter = HEAD_DIM // 2
    raw = dq_out[...] * HEAD_DIM**-0.5
    one, two = raw[:quarter, :], raw[quarter:, :]
    cos, sin = turns[:quarter, :], turns[quarter:, :]
    turned = jnp.concatenate([one * cos + two * sin, two * cos - one * sin], axis=0)
    natural = jnp.transpose(turned).astype(BF16)
    grad_query = jnp.concatenate(
        [
            jnp.concatenate(
                [
                    natural[start + head * half : start + (head + 1) * half, :]
                    for head in range(heads)
                ],
                axis=1,
            )
            for start in (0, half_width)
        ],
        axis=0,
    )
    x_all = x_in[...].astype(F32)
    factor_all = lax.rsqrt(jnp.mean(x_all * x_all, axis=-1, keepdims=True) + EPSILON)
    normed_attn = (x_all * factor_all * attn_gain[...]).astype(BF16)
    wide_q = grad_query.shape[1]
    q_part = sum_q[0]
    q_part[...] = tn(grad_query, normed_attn).astype(BF16).reshape(q_part.shape)
    q_quad.start()
    turn_send[...] = nn(grad_query, weights_in[:wide_q, :])
    biases[...] = jnp.zeros_like(biases)
    biases[:, :wide_q] = jnp.sum(grad_query.astype(F32), axis=0, keepdims=True)
    done = chain_steps(done, SHARE[11])
    take_over(chunks - 1, True, True)
    q_quad.middle()
    outs_sum.cross()
    done = chain_steps(done, SHARE[6])
    for step in range(groups - 1):
        arrived(z_in.at[step], kv_sems.at[5, step], place.sibling)
        dkv_out[...] += z_in[step].astype(F32)
    turned = jnp.transpose(dkv_out[...])
    one, two = turned[:quarter, :], turned[quarter:HEAD_DIM, :]
    cos, sin = turns_rows[:quarter, :], turns_rows[quarter:, :]
    turned = jnp.concatenate(
        [one * cos + two * sin, two * cos - one * sin, turned[HEAD_DIM:, :]], axis=0
    )
    grad_kv = jnp.transpose(turned).astype(BF16)
    kv_part = sum_kv[0]
    kv_part[...] = tn(grad_kv, normed_attn).astype(BF16).reshape(kv_part.shape)
    kv_quad.start()
    turn_send[...] += nn(grad_kv, weights_in[wide_q:, :])
    turn_in[0] = turn_send[other_rows, :].astype(BF16)
    send(turn_in.at[0], turn_in.at[1], vector_sems.at[0], vector_sems.at[1], place.partner)
    biases[:, wide_q : wide_q + LANES] = jnp.sum(grad_kv.astype(F32), axis=0, keepdims=True)
    done = chain_steps(done, SHARE[12])
    kv_quad.middle()
    q_quad.end()
    q_sum.start()
    done = chain_steps(done, SHARE[7])
    kv_quad.end()
    kv_sum.start()
    x_half = x_in[my_rows, :].astype(F32)
    factor = lax.rsqrt(jnp.mean(x_half * x_half, axis=-1, keepdims=True) + EPSILON)
    normed = x_half * factor
    done = chain_steps(done, SHARE[13])
    arrived(turn_in.at[1], vector_sems.at[1], place.partner)
    grad_normed = turn_send[my_rows, :] + turn_in[1].astype(F32)
    gains[:, :features] = jnp.sum(grad_normed * normed, axis=0, keepdims=True)
    weighted = grad_normed * attn_gain[...]
    mean = jnp.mean(weighted * normed, axis=-1, keepdims=True)
    input_grad[my_rows, :] = (
        resid_grad[...] + factor * (weighted - normed * mean)
    ).astype(BF16)

    def vectors(hop, device, with_biases):
        send(gains, gain_in.at[hop], vector_sems.at[4 + 4 * hop], vector_sems.at[5 + 4 * hop], device)
        if with_biases:
            send(
                biases,
                bias_in.at[hop],
                vector_sems.at[6 + 4 * hop],
                vector_sems.at[7 + 4 * hop],
                device,
            )

    def vectors_done(hop, device, with_biases):
        arrived(gain_in.at[hop], vector_sems.at[5 + 4 * hop], device)
        sent(gains, vector_sems.at[4 + 4 * hop], device)
        gains[...] += gain_in[hop]
        if with_biases:
            arrived(bias_in.at[hop], vector_sems.at[7 + 4 * hop], device)
            sent(biases, vector_sems.at[6 + 4 * hop], device)
            biases[...] += bias_in[hop]

    hops = ((place.partner, False), (place.sibling, True), (place.across, True))
    vectors(0, *hops[0])
    send(
        input_grad.at[my_rows],
        input_grad.at[my_rows],
        vector_sems.at[2],
        vector_sems.at[3],
        place.partner,
    )
    done = chain_steps(done, SHARE[14])
    q_sum.middle()
    vectors_done(0, *hops[0])
    vectors(1, *hops[1])
    kv_sum.middle()
    done = chain_steps(done, SHARE[8])
    vectors_done(1, *hops[1])
    vectors(2, *hops[2])
    done = chain_steps(done, SHARE[9])
    vectors_done(2, *hops[2])
    gain_z[place.group] = gains[...]
    bias_z[place.group] = biases[...]
    base = 16
    for step in range(1, groups):
        other = place.in_group((place.group + step) % groups)
        for number, ref in enumerate((gain_z, bias_z)):
            send(
                ref.at[place.group],
                ref.at[place.group],
                vector_sems.at[base + 4 * step + 2 * number],
                vector_sems.at[base + 4 * (groups - step) + 2 * number + 1],
                other,
            )
    q_sum.end()
    kv_sum.end()
    done = chain_steps(done, SHARE[10])
    q_sum.cross()
    kv_sum.cross()
    for step in range(1, groups):
        other = (place.group + groups - step) % groups
        for number, ref in enumerate((gain_z, bias_z)):
            arrived(
                ref.at[other],
                vector_sems.at[base + 4 * (groups - step) + 2 * number + 1],
                place.sibling,
            )
            sent(
                ref.at[place.group],
                vector_sems.at[base + 4 * step + 2 * number],
                place.sibling,
            )
    gains[...] = jnp.sum(gain_z[...], axis=0)
    biases[...] = jnp.sum(bias_z[...], axis=0)

    def last(number, unused):
        chain_step(number)
        return unused

    lax.fori_loop(done, all_steps, last, 0)

    arrived(input_grad.at[other_rows], vector_sems.at[3], place.partner)
    sent(input_grad.at[my_rows], vector_sems.at[2], place.partner)
    sent(turn_in.at[0], vector_sems.at[0], place.partner)
    for part in (outs_quad, q_quad, kv_quad, outs_sum, q_sum, kv_sum):
        part.finish()
    arrived(layer_out.at[other_rows], pair_sems.at[3], place.partner)
    sent(branch.at[my_rows], pair_sems.at[0], place.partner)
    sent(branch.at[my_rows], pair_sems.at[2], place.partner)
    grad_sum.finish()
    mlp_sum.finish()
    tall_sum.finish()
    wide_sum.finish()
    for number in range(chunks - 2, chunks):
        sent(sib_send.at[0], kv_sems.at[0, number], place.sibling)
    for step in range(groups - 2, groups):
        sent(side_send.at[0], kv_sems.at[2, step], place.across)
    for step in range(groups - 3, groups - 1):
        sent(z_send.at[0], kv_sems.at[4, step], place.sibling)


def vmem_specs(count):
    return [pl.BlockSpec(memory_space=pltpu.VMEM)] * count


def params(collective):
    return pltpu.CompilerParams(
        collective_id=collective, has_side_effects=True, vmem_limit_bytes=VMEM_LIMIT
    )


def attend(groups, slots, kv_own, qt, x_in, out_weight, cot):
    rows, features = x_in.shape
    half = rows // 2
    total = groups * QUAD * rows
    width, queries = qt.shape
    dma = pltpu.SemaphoreType.DMA
    shape = jax.ShapeDtypeStruct
    return pl.pallas_call(
        functools.partial(attend_kernel, groups, slots),
        out_shape=[
            shape((total, LANES), BF16),
            shape((QUAD * rows, features), BF16),
            shape((half, features), F32),
            shape((rows, out_weight.shape[0]), BF16),
            shape((HEAD_DIM, queries), F32),
            shape((1, queries), F32),
        ],
        in_specs=vmem_specs(5),
        out_specs=vmem_specs(6),
        scratch_shapes=[
            pltpu.VMEM((2, 2 * rows, queries // 2), F32),
            pltpu.VMEM((1, queries), F32),
            pltpu.VMEM((1, queries), F32),
            pltpu.VMEM((half, features), BF16),
            pltpu.VMEM((half, features), BF16),
            dma((groups * QUAD,)),
            dma((groups,)),
            dma((groups,)),
            dma((2 * groups,)),
            dma((8,)),
            dma((2,)),
            dma((8,)),
            dma((2,)),
        ],
        compiler_params=params(1),
        name="attend",
    )(kv_own, qt, x_in, out_weight, cot)


def backward(groups, slots, operands):
    (gate_weight, _, _, cot_all, resid, cot, gain, out_weight, att, ot, lse, qt, kv_all) = operands[
        :13
    ]
    weights_in = operands[15]
    rows, inner = att.shape
    half = rows // 2
    features, hidden = gate_weight.shape
    piece = piece_width(hidden)
    layer_rows = QUAD * rows
    width, queries = qt.shape
    chunks = 2 * groups
    both = round_up(weights_in.shape[0], LANES)
    dma = pltpu.SemaphoreType.DMA
    shape = jax.ShapeDtypeStruct
    pass_shape = (rows, LANES)
    wide = jax.ShapeDtypeStruct((2 * features // WIDE_ROWS, WIDE_ROWS, piece), BF16)
    tall = jax.ShapeDtypeStruct((piece // TALL_ROWS, TALL_ROWS, features), BF16)
    outs = (inner // QUAD, features)
    ins_q = (inner // QUAD, features)
    ins_kv = (LANES // QUAD, features)
    return pl.pallas_call(
        functools.partial(backward_kernel, groups, slots),
        out_shape=[
            shape((rows, features), BF16),
            shape((rows, features), BF16),
            shape((QUAD, *wide.shape), BF16),
            shape((QUAD, *tall.shape), BF16),
            *(shape((QUAD, *column_parts(groups, *dims)), BF16) for dims in (outs, ins_q, ins_kv)),
            shape((1, 2 * features), F32),
            shape((1, both), F32),
        ],
        in_specs=[pl.BlockSpec(memory_space=pl.ANY)] * 3 + vmem_specs(15),
        out_specs=vmem_specs(2) + [pl.BlockSpec(memory_space=pl.ANY)] * 5 + vmem_specs(2),
        scratch_shapes=[
            pltpu.VMEM(wide.shape, BF16),
            pltpu.VMEM(tall.shape, BF16),
            pltpu.VMEM(wide.shape, BF16),
            pltpu.VMEM(tall.shape, BF16),
            pltpu.VMEM((round_up(wide.shape[0], 2) // 2, *wide.shape[1:]), BF16),
            pltpu.VMEM((round_up(tall.shape[0], 2) // 2, *tall.shape[1:]), BF16),
            *chain_sems(wide.shape[0]),
            *chain_sems(tall.shape[0]),
            *layer_sum_scratch(half, features),
            *layer_sum_scratch(half, features),
            pltpu.VMEM((rows, features), BF16),
            pltpu.VMEM((width, queries), BF16),
            pltpu.VMEM((LANES, queries), BF16),
            pltpu.VMEM((queries, LANES), BF16),
            pltpu.VMEM((queries, LANES), BF16),
            pltpu.VMEM((2, 2 * rows, LANES), F32),
            pltpu.VMEM((2, *pass_shape), BF16),
            pltpu.VMEM((chunks, *pass_shape), BF16),
            pltpu.VMEM((2, *pass_shape), BF16),
            pltpu.VMEM((groups, *pass_shape), BF16),
            pltpu.VMEM((2, *pass_shape), BF16),
            pltpu.VMEM((groups, *pass_shape), BF16),
            dma((6, chunks)),
            dma((7,)),
            pltpu.VMEM((HEAD_DIM, queries), F32),
            pltpu.VMEM((rows, LANES), F32),
            pltpu.VMEM((half, features), F32),
            pltpu.VMEM((rows, features), F32),
            pltpu.VMEM((2, half, features), BF16),
            pltpu.VMEM((3, 1, 2 * features), F32),
            pltpu.VMEM((3, 1, both), F32),
            pltpu.VMEM((groups, 1, 2 * features), F32),
            pltpu.VMEM((groups, 1, both), F32),
            dma((16 + 4 * groups + 4,)),
            *column_sum_scratch(groups, *outs),
            *column_sum_scratch(groups, *ins_q),
            *column_sum_scratch(groups, *ins_kv),
            pltpu.VMEM((features, piece), BF16),
            pltpu.VMEM((features, piece), BF16),
            pltpu.VMEM((piece, features), BF16),
            pltpu.VMEM((layer_rows, features), BF16),
            pltpu.VMEM((layer_rows, piece), BF16),
            pltpu.VMEM((layer_rows, 2 * piece), BF16),
            pltpu.VMEM((layer_rows, features), BF16),
            pltpu.VMEM((layer_rows, features), BF16),
            dma((8,)),
            dma((2,)),
            dma((8,)),
        ],
        compiler_params=params(2),
        name="backward",
    )(*operands)


def rope_tables(positions, head_size):
    half_size = head_size // 2
    exponent = jnp.arange(half_size, dtype=F32) * (2.0 / head_size)
    frequency = jnp.power(ROPE_BASE, -exponent)
    angle = positions.astype(F32)[:, None] * frequency[None, :]
    return (jnp.cos(angle)[:, None, :], jnp.sin(angle)[:, None, :])


def rotate(values, cosine, sine):
    half_size = values.shape[-1] // 2
    first = values[..., :half_size]
    second = values[..., half_size:]
    return jnp.concatenate(
        [first * cosine - second * sine, second * cosine + first * sine], axis=-1
    )


def piece_width(hidden):
    return round_up(hidden // LANES, QUAD) // QUAD * LANES


def per_device(
    groups,
    layer_input,
    block_order,
    attn_gain,
    query_weight,
    query_bias,
    key_weight,
    key_bias,
    value_weight,
    value_bias,
    out_weight,
    mlp_gain,
    gate_weight,
    up_weight,
    down_weight,
    out_cotangent,
):
    rows, features = layer_input.shape
    block_rows = rows // 2
    slots = block_order.shape[0]
    hidden = gate_weight.shape[1]
    heads = query_weight.shape[1] // HEAD_DIM
    piece = piece_width(hidden)
    half_width = round_up(heads * block_rows, 2 * LANES)
    queries = 2 * half_width
    width = round_up(HEAD_DIM + slots + 16, LANES)
    scale = HEAD_DIM ** (-0.5)
    seq_index = lax.axis_index("seq")
    own_slots = lax.dynamic_slice_in_dim(block_order, 2 * seq_index, 2)
    steps_in = jnp.arange(block_rows, dtype=jnp.int32)
    own_places = (own_slots[:, None] * block_rows + steps_in[None, :]).reshape(-1)
    cosine, sine = rope_tables(own_places, HEAD_DIM)
    inputs = layer_input.astype(F32)
    factor_first = lax.rsqrt(jnp.mean(inputs * inputs, axis=-1, keepdims=True) + EPSILON)
    normed_first = inputs * factor_first
    normed_attn = (normed_first * attn_gain).astype(BF16)
    query_rows = (
        jnp.dot(normed_attn, query_weight, preferred_element_type=F32) + query_bias
    ).reshape(rows, heads, HEAD_DIM)
    key_rows = (jnp.dot(normed_attn, key_weight, preferred_element_type=F32) + key_bias).reshape(
        rows, 1, HEAD_DIM
    )
    value_rows = (
        jnp.dot(normed_attn, value_weight, preferred_element_type=F32) + value_bias
    ).astype(BF16)
    query_rot = rotate(query_rows, cosine, sine).astype(BF16)
    key_rot = rotate(key_rows, cosine, sine).astype(BF16).reshape(rows, HEAD_DIM)
    kv_own = jnp.concatenate([key_rot, value_rows], axis=1)
    padding = ((0, 0), (0, 0), (0, half_width - heads * block_rows))

    def by_columns(values):
        count = values.shape[-1]
        values = values.reshape(2, block_rows, heads, count)
        values = jnp.transpose(values, (3, 0, 2, 1)).reshape(count, 2, heads * block_rows)
        return jnp.pad(values, padding).reshape(count, queries)

    query_t = by_columns(query_rot * jnp.asarray(scale, BF16))
    later = block_order[:, None] > own_slots[None, :]
    bias = jnp.where(later, NEGATIVE, 0.0).astype(BF16)
    bias = jnp.broadcast_to(bias[:, :, None], (slots, 2, half_width)).reshape(slots, queries)
    qt = jnp.concatenate(
        [query_t, bias, jnp.zeros((width - HEAD_DIM - slots, queries), BF16)], axis=0
    )
    gain_row = mlp_gain[None, :]

    kv_all, cot_all, resid, att, ot, lse = attend(
        groups, slots, kv_own, qt, layer_input, out_weight, out_cotangent
    )

    weights_in = jnp.concatenate(
        [jnp.transpose(w) for w in (query_weight, key_weight, value_weight)], axis=0
    )
    turns_rows = jnp.concatenate([cosine[:, 0, :], sine[:, 0, :]], axis=1)
    tables = (
        by_columns(jnp.broadcast_to(turns_rows[:, None, :], (rows, heads, HEAD_DIM))),
        jnp.transpose(turns_rows),
    )
    layer_output, input_grad, wide_sum, tall_sum, outs, ins_q, ins_kv, gains, biases = backward(
        groups,
        slots,
        (
            gate_weight, up_weight, down_weight, cot_all, resid, out_cotangent, gain_row, out_weight,
            att, ot, lse, qt, kv_all, layer_input, attn_gain[None, :], weights_in, *tables,
        ),
    )

    keep = hidden - (QUAD - 1) * piece
    wide_sum = wide_sum.reshape(QUAD, 2, features, piece)
    tall_sum = tall_sum.reshape(QUAD, piece, features)

    def side_by_side(number):
        parts = [wide_sum[i, number] for i in range(QUAD - 1)] + [
            wide_sum[QUAD - 1, number][:, :keep]
        ]
        return jnp.concatenate(parts, axis=1).astype(F32)

    gate_sum, up_sum = side_by_side(0), side_by_side(1)
    down_sum = tall_sum.reshape(QUAD * piece, features)[:hidden].astype(F32)

    query_width = heads * HEAD_DIM

    def quarters(parts, row_count):
        parts = parts.reshape(QUAD, -1, parts.shape[-1])[:, : row_count // QUAD]
        return parts.reshape(row_count, -1).astype(F32)

    out_grad = quarters(outs, query_width)
    query_grad = jnp.transpose(quarters(ins_q, query_width))
    key_value = quarters(ins_kv, 2 * HEAD_DIM)
    key_grad = jnp.transpose(key_value[:HEAD_DIM])
    value_grad = jnp.transpose(key_value[HEAD_DIM:])
    attn_gain_grad, mlp_gain_grad = gains[0, :features], gains[0, features:]
    query_bias_grad = biases[0, :query_width]
    key_bias_grad = biases[0, query_width : query_width + HEAD_DIM]
    value_bias_grad = biases[0, query_width + HEAD_DIM : query_width + 2 * HEAD_DIM]
    return (
        layer_output,
        input_grad,
        attn_gain_grad,
        query_grad,
        query_bias_grad,
        key_grad,
        key_bias_grad,
        value_grad,
        value_bias_grad,
        out_grad,
        mlp_gain_grad,
        gate_sum,
        up_sum,
        down_sum,
    )


def solution(mesh):
    groups = mesh.shape["seq"] // QUAD
    by_rows, columns, rows, vector, whole = (
        P("seq", None),
        P(None, "tp"),
        P("tp", None),
        P("tp"),
        P(),
    )
    return jax.shard_map(
        functools.partial(per_device, groups),
        mesh=mesh,
        in_specs=(
            by_rows, whole, whole, columns, vector, columns, vector, columns, vector, rows,
            whole, columns, columns, rows, by_rows,
        ),
        out_specs=(
            by_rows, by_rows, whole, columns, vector, columns, vector, columns, vector, rows,
            whole, columns, columns, rows,
        ),
        check_vma=False,
    )
```

```python
import functools

import jax
import jax.numpy as jnp
from jax import lax
from jax.experimental import pallas as pl
from jax.experimental.pallas import tpu as pltpu
from jax.sharding import PartitionSpec as P

HEAD_DIM = 64
EPSILON = 1e-06
NEGATIVE = -1e30
ROPE_BASE = 1000000.0
LANES = 128
QUAD = 4
WIDE_ROWS = 128
TALL_ROWS = 64
SHARE = (2, 2, 2, 2, 1, 1, 1, 2, 1, 1, 2, 1, 1, 1, 1)
PACE = 2
MESH = pl.DeviceIdType.MESH
VMEM_LIMIT = 62 * 1024 * 1024
BF16 = jnp.bfloat16
F32 = jnp.float32


def round_up(value, step):
    return -(-value // step) * step


def nn(left, right):
    return lax.dot_general(left, right, (((1,), (0,)), ((), ())), preferred_element_type=F32)


def nt(left, right):
    return lax.dot_general(left, right, (((1,), (1,)), ((), ())), preferred_element_type=F32)


def tn(left, right):
    return lax.dot_general(left, right, (((0,), (0,)), ((), ())), preferred_element_type=F32)


class Place:
    def __init__(self, groups):
        seq = lax.axis_index("seq").astype(jnp.int32)
        tp = lax.axis_index("tp").astype(jnp.int32)
        self.groups = groups
        self.seq = seq
        self.tp = tp
        self.group = seq // QUAD
        self.quad = seq % QUAD
        self.core = seq % 2
        self.side = (seq // 2) % 2
        self.sibling = (seq + 1 - 2 * self.core, tp)
        self.across = (seq + 2 - 4 * self.side, tp)
        self.partner = (seq, 1 - tp)

    def seq_at(self, group, side, core):
        return group * QUAD + side * 2 + core

    def in_group(self, group):
        return (group * QUAD + self.quad, self.tp)


def send(src, dst, send_sem, recv_sem, device):
    pltpu.make_async_remote_copy(
        src_ref=src,
        dst_ref=dst,
        send_sem=send_sem,
        recv_sem=recv_sem,
        device_id=device,
        device_id_type=MESH,
    ).start()


def sent(src, send_sem, device):
    pltpu.make_async_remote_copy(
        src_ref=src,
        dst_ref=src,
        send_sem=send_sem,
        recv_sem=send_sem,
        device_id=device,
        device_id_type=MESH,
    ).wait_send()


def arrived(dst, recv_sem, device):
    pltpu.make_async_remote_copy(
        src_ref=dst,
        dst_ref=dst,
        send_sem=recv_sem,
        recv_sem=recv_sem,
        device_id=device,
        device_id_type=MESH,
    ).wait_recv()


def meet(place, whole_column):
    barrier = pltpu.get_barrier_semaphore()
    for device in (place.sibling, place.across, place.partner):
        pl.semaphore_signal(barrier, inc=1, device_id=device, device_id_type=MESH)
    if whole_column:
        for step in range(1, place.groups):
            other = place.in_group((place.group + step) % place.groups)
            pl.semaphore_signal(barrier, inc=1, device_id=other, device_id_type=MESH)
        pl.semaphore_wait(barrier, 3 + place.groups - 1)
    else:
        pl.semaphore_wait(barrier, 3)


class LayerGather:
    def __init__(self, place, all_ref, half, recv, part, sems):
        self.place = place
        self.all_ref = all_ref
        self.half = half
        self.first = round_up(half // 2, 16)
        self.recv, self.part, self.sems = recv, part, sems

    def index(self, flip_side, flip_core, flip_tp):
        place = self.place
        side = 1 - place.side if flip_side else place.side
        core = 1 - place.core if flip_core else place.core
        tp = 1 - place.tp if flip_tp else place.tp
        return (side * 2 + core) * 2 + tp

    def rows(self, block, start=0, size=None):
        size = self.half if size is None else size
        return self.all_ref.at[pl.ds(pl.multiple_of(block * self.half + start, 16), size)]

    def start(self, numbers=(0, 1, 2)):
        place = self.place
        own = self.index(0, 0, 0)
        devices = (place.across, place.partner, place.sibling)
        for number in numbers:
            send(
                self.rows(own),
                self.rows(own),
                self.sems.at[number],
                self.recv.at[own],
                devices[number],
            )

    def from_across(self):
        place = self.place
        block = self.index(1, 0, 0)
        arrived(self.rows(block), self.recv.at[block], place.across)
        part = self.rows(block, 0, self.first)
        send(part, part, self.sems.at[3], self.part.at[0], place.partner)
        send(self.rows(block), self.rows(block), self.sems.at[4], self.recv.at[block], place.sibling)

    def from_partner(self):
        place = self.place
        block = self.index(0, 0, 1)
        arrived(self.rows(block), self.recv.at[block], place.partner)
        part = self.rows(block, self.first, self.half - self.first)
        send(part, part, self.sems.at[5], self.part.at[1], place.across)
        send(self.rows(block), self.rows(block), self.sems.at[6], self.recv.at[block], place.sibling)

    def diagonal(self):
        place = self.place
        block = self.index(1, 0, 1)
        arrived(self.rows(block, 0, self.first), self.part.at[0], place.partner)
        arrived(self.rows(block, self.first, self.half - self.first), self.part.at[1], place.across)
        send(self.rows(block), self.rows(block), self.sems.at[7], self.recv.at[block], place.sibling)

    def from_sibling(self, flip_side, flip_tp):
        block = self.index(flip_side, 1, flip_tp)
        arrived(self.rows(block), self.recv.at[block], self.place.sibling)

    def finish(self, waited=False):
        place = self.place
        if not waited:
            for side in (0, 1):
                for tp in (0, 1):
                    self.from_sibling(side, tp)
        own = self.index(0, 0, 0)
        for number, device in enumerate((place.across, place.partner, place.sibling)):
            sent(self.rows(own), self.sems.at[number], device)
        sent(self.rows(own, 0, self.first), self.sems.at[3], place.partner)
        sent(self.rows(own), self.sems.at[4], place.sibling)
        sent(self.rows(own, self.first, self.half - self.first), self.sems.at[5], place.across)
        sent(self.rows(own), self.sems.at[6], place.sibling)
        sent(self.rows(own), self.sems.at[7], place.sibling)


def extended_keys(kv, chip, rows, width, slots):
    count = kv.shape[0]
    lane = lax.broadcasted_iota(jnp.int32, (count, width), 1) - HEAD_DIM
    row = lax.broadcasted_iota(jnp.int32, (count, width), 0)
    block = rows // 2
    number = jnp.zeros_like(row)
    for edge in range(block, count, block):
        number = number + (row >= edge).astype(jnp.int32)
    hot = (lane == number + chip * (count // block)) | ((lane >= slots) & (lane < slots + 3))
    extra = jnp.where(hot, 1.0, 0.0).astype(BF16)
    if width == LANES:
        return jnp.where(lane < 0, kv, extra)
    first = jnp.where(lane[:, :LANES] < 0, kv, extra[:, :LANES])
    return jnp.concatenate([first, extra[:, LANES:]], axis=1)


def hide_later(scores, place, rows, half_number, first):
    count, width = scores.shape
    half = rows // 2
    key = lax.broadcasted_iota(jnp.int32, (count, 1), 0) - place.core * rows - half_number * half
    query = (lax.broadcasted_iota(jnp.int32, (1, width), 1) + first) % half
    return jnp.where((key > query) & (key < half), NEGATIVE, scores)


def split_rows(values, at, count):
    one = values.astype(BF16).astype(F32)
    two = (values - one).astype(BF16).astype(F32)
    three = values - one - two
    row = lax.broadcasted_iota(jnp.int32, (count, values.shape[1]), 0) - at
    picked = jnp.where(row == 0, one, jnp.where(row == 1, two, jnp.where(row == 2, three, 0.0)))
    return picked.astype(BF16)


def attend_kernel(
    groups,
    slots,
    kv_own,
    qt,
    x_in,
    out_weight,
    cot,
    kv_all,
    cot_all,
    resid_out,
    att_out,
    ot_out,
    lse_out,
    s_buf,
    m_buf,
    l_buf,
    part_send,
    part_recv,
    kv_recv,
    kv_z,
    kv_x,
    kv_sib,
    c_recv,
    c_part,
    c_sems,
    p_sems,
):
    place = Place(groups)
    rows = kv_own.shape[0]
    half = rows // 2
    span = 2 * rows
    width, queries = qt.shape
    block = queries // 2
    chunks = 2 * groups
    heads = out_weight.shape[0] // HEAD_DIM

    kv_all[pl.ds(place.seq * rows, rows), :] = kv_own[...]
    own_half = place.quad * 2 + place.tp
    cot_all[pl.ds(pl.multiple_of(own_half * half, 16), half), :] = cot[
        pl.ds(pl.multiple_of(place.tp * half, 16), half), :
    ]
    meet(place, True)

    def kv_rows(seq):
        return kv_all.at[pl.ds(pl.multiple_of(seq * rows, 16), rows)]

    gather_cot = LayerGather(place, cot_all, half, c_recv, c_part, c_sems)
    own = kv_rows(place.seq)
    send(own, own, kv_sib.at[0], kv_recv.at[place.seq], place.sibling)
    for step in range(1, groups):
        other = place.in_group((place.group + step) % groups)
        send(own, own, kv_z.at[step - 1], kv_recv.at[place.seq], other)
    send(own, own, kv_x.at[0], kv_recv.at[place.seq], place.across)
    gather_cot.start((1, 2))

    def chunk_place(number):
        odd = number % 2
        far = jnp.where(number < 2, odd, jnp.where(number == 2, 0, 1 - odd))
        distance = jnp.where(number < 2, 0, jnp.where(odd == 1, (number + 1) // 2, number // 2 - 1))
        distance = jnp.where(number == 2, 1, distance)
        last = number == chunks - 1
        far = jnp.where(last, 1, far)
        distance = jnp.where(last, groups - 1, distance)
        up = jnp.where(place.group < groups // 2, distance, groups - distance)
        group = (place.group + up) % groups
        side = place.side + far * (1 - 2 * place.side)
        return group, side, distance, far

    def pass_on(number):
        group, side, distance, far = chunk_place(number)
        seq = place.seq_at(group, side, place.core)
        view = kv_rows(seq)
        arrived(view, kv_recv.at[seq], place.across)
        send(view, view, kv_sib.at[number], kv_recv.at[seq], place.sibling)

        @pl.when(far == 0)
        def near():
            send(view, view, kv_x.at[distance], kv_recv.at[seq], place.across)

    def ready(number):
        group, side, _, _ = chunk_place(number)
        seq = place.seq_at(group, side, 1 - place.core)
        arrived(kv_rows(seq), kv_recv.at[seq], place.sibling)

    def kv_chunk(number):
        group, side, _, _ = chunk_place(number)
        chip = group * 2 + side
        return chip, kv_all[pl.ds(pl.multiple_of(chip * span, 16), span), :]

    def lanes_of(half_number):
        return pl.ds(pl.multiple_of(half_number * block, LANES), block)

    def scores(half_number, number, slot, own_chip=False):
        chip, kv = kv_chunk(number)
        keys = extended_keys(kv, chip, rows, width, slots)
        value = nn(keys, qt[:, lanes_of(half_number)])
        if own_chip:
            value = hide_later(value, place, rows, half_number, 0)
        s_buf[slot] = value

    def absorb(half_number, number, slot):
        chip, kv = kv_chunk(number)
        lanes = lanes_of(half_number)
        value = s_buf[slot]
        old = m_buf[:, lanes]
        top = jnp.maximum(old, jnp.max(value, axis=0, keepdims=True))
        shrink = jnp.exp(old - top)
        weights = jnp.exp(value - top)
        total = jnp.sum(weights, axis=0, keepdims=True)
        product = tn(kv[:, HEAD_DIM:], weights.astype(BF16))
        m_buf[:, lanes] = top
        l_buf[:, lanes] = total + l_buf[:, lanes] * shrink
        ot_out[:, lanes] = product + ot_out[:, lanes] * shrink

    m_buf[...] = jnp.full(m_buf.shape, NEGATIVE, F32)
    l_buf[...] = jnp.zeros_like(l_buf)
    ot_out[...] = jnp.zeros_like(ot_out)

    def comes(number):
        @pl.when(number + 2 < chunks)
        def look_ahead():
            pass_on(number + 2)

        @pl.when(number < chunks)
        def next_ready():
            ready(number)

    def sweep(half_number, waits, following):
        def two_chunks(pair, unused):
            if waits:
                comes(2 * pair + 1)
            scores(half_number, 2 * pair + 1, 1)
            absorb(half_number, 2 * pair, 0)
            if waits:
                comes(2 * pair + 2)
            scores(half_number, 2 * pair + 2, 0)
            absorb(half_number, 2 * pair + 1, 1)
            return unused

        lax.fori_loop(0, groups - 1, two_chunks, 0)
        if waits:
            comes(chunks - 1)
        scores(half_number, chunks - 1, 1)
        absorb(half_number, chunks - 2, 0)
        if following is not None:
            scores(following, 0, 0, True)
        absorb(half_number, chunks - 1, 1)

    def close_half(half_number):
        lanes = lanes_of(half_number)
        ot = ot_out[:, lanes] / l_buf[:, lanes]
        ot_out[:, lanes] = ot
        lse_out[:, lanes] = m_buf[:, lanes] + jnp.log(l_buf[:, lanes])
        natural = jnp.transpose(ot).astype(BF16)
        att = jnp.concatenate(
            [natural[head * half : (head + 1) * half, :] for head in range(heads)], axis=1
        )
        att_out[pl.ds(pl.multiple_of(half_number * half, 16), half), :] = att
        return nn(att, out_weight[...])

    theirs, mine = 1 - place.tp, place.tp
    ready(0)
    scores(theirs, 0, 0, True)
    pass_on(1)
    pass_on(2)
    sweep(theirs, True, mine)
    gather_cot.start((0,))
    part_send[...] = close_half(theirs).astype(BF16)
    send(part_send, part_recv, p_sems.at[0], p_sems.at[1], place.partner)
    gather_cot.from_partner()
    sweep(mine, False, None)
    gather_cot.from_across()
    my_rows = pl.ds(pl.multiple_of(place.tp * half, 16), half)
    resid = close_half(mine) + x_in[my_rows, :].astype(F32)
    gather_cot.diagonal()
    arrived(part_recv, p_sems.at[1], place.partner)
    resid_out[...] = resid + part_recv[...].astype(F32)
    gather_cot.finish()
    sent(part_send, p_sems.at[0], place.partner)

    def close(number, unused):
        sent(own, kv_sib.at[number], place.sibling)
        return unused

    lax.fori_loop(0, chunks, close, 0)
    for step_out in range(groups):
        sent(own, kv_x.at[step_out], place.across)
    for step_out in range(1, groups):
        sent(own, kv_z.at[step_out - 1], place.in_group((place.group + step_out) % groups))


class ChainSum:
    def __init__(self, place, own, incoming, at_root, final, sems):
        self.place = place
        self.own, self.incoming, self.at_root, self.final = own, incoming, at_root, final
        self.count = own.shape[0]
        (
            self.up_recv,
            self.up_send,
            self.fin_recv,
            self.fin_send,
            self.x_recv,
            self.x_send,
            self.c_recv,
            self.c_send,
            self.keep,
        ) = sems

    def root(self, parity):
        return self.place.groups // 2 - 1 + parity

    def lag_up(self, parity):
        groups, group, root = self.place.groups, self.place.group, self.root(parity)
        most = max(root, groups - 1 - root)
        return PACE * jnp.where(
            group < root, group, jnp.where(group > root, groups - 1 - group, most)
        )

    def lag_down(self, parity):
        groups, group, root = self.place.groups, self.place.group, self.root(parity)
        most = max(root, groups - 1 - root)
        return PACE * (most + jnp.abs(group - root))

    def total_steps(self):
        groups = self.place.groups
        most = groups // 2
        return self.count + PACE * (2 * most + 1)

    def spread(self, i, view):
        place = self.place
        final = self.final.at[place.quad, i]
        send(view, final, self.x_send.at[i], self.x_recv.at[i], place.across)
        send(view, final, self.c_send.at[0, i], self.c_recv.at[0, i], place.sibling)

    def up(self, i, parity):
        place, root = self.place, self.root(parity)
        group, last = place.group, place.groups - 1
        mine = self.own.at[i]

        here, second = self.incoming.at[i], self.at_root.at[i // 2]

        def add(way, ref):
            arrived(ref, self.up_recv.at[way, i], place.in_group(group - 1 + 2 * way))
            mine[...] = (mine[...].astype(F32) + ref[...].astype(F32)).astype(BF16)

        def onward(way, dst, send_sem, recv_sem):
            send(mine, dst, send_sem, recv_sem, place.in_group(group + 1 - 2 * way))

        @pl.when((group > 0) & (group <= root))
        def from_left():
            add(0, here)

        @pl.when((group < last) & (group > root))
        def from_right():
            add(1, here)

        @pl.when((group < last) & (group == root))
        def from_right_to_root():
            add(1, second)

        @pl.when(group < root)
        def to_right():
            onward(0, here, self.up_send.at[i], self.up_recv.at[0, i])

        @pl.when(group > root + 1)
        def to_left():
            onward(1, here, self.up_send.at[i], self.up_recv.at[1, i])

        @pl.when(group == root + 1)
        def to_root():
            onward(1, second, self.up_send.at[i], self.up_recv.at[1, i])

        @pl.when(group == root)
        def finished():
            final = self.final.at[place.quad, i]

            @pl.when(group > 0)
            def left():
                onward(1, final, self.fin_send.at[0, i], self.fin_recv.at[i])

            @pl.when(group < last)
            def right():
                onward(0, final, self.fin_send.at[1, i], self.fin_recv.at[i])

            self.spread(i, mine)
            pltpu.make_async_copy(mine, final, self.keep.at[i]).start()

    def down(self, i, parity):
        place, root = self.place, self.root(parity)
        group, last = place.group, place.groups - 1
        view = self.final.at[place.quad, i]

        @pl.when(group != root)
        def take():
            arrived(view, self.fin_recv.at[i], place.sibling)

            @pl.when((group < root) & (group > 0))
            def left():
                send(
                    view,
                    view,
                    self.fin_send.at[0, i],
                    self.fin_recv.at[i],
                    place.in_group(group - 1),
                )

            @pl.when((group > root) & (group < last))
            def right():
                send(
                    view,
                    view,
                    self.fin_send.at[1, i],
                    self.fin_recv.at[i],
                    place.in_group(group + 1),
                )

            self.spread(i, view)

    def cross(self, i):
        place = self.place
        view = self.final.at[place.across[0] % QUAD, i]
        arrived(view, self.x_recv.at[i], place.across)
        send(view, view, self.c_send.at[1, i], self.c_recv.at[1, i], place.sibling)

    def step(self, number):
        for parity in (0, 1):
            i = number - self.lag_up(parity)

            @pl.when((i >= 0) & (i < self.count) & (i % 2 == parity))
            def go_up(i=i, parity=parity):
                self.up(i, parity)

        for parity in (0, 1):
            i = number - self.lag_down(parity)

            @pl.when((i >= 0) & (i < self.count) & (i % 2 == parity))
            def go_down(i=i, parity=parity):
                self.down(i, parity)

        for parity in (0, 1):
            i = number - self.lag_down(parity) - PACE

            @pl.when((i >= 0) & (i < self.count) & (i % 2 == parity))
            def go_cross(i=i):
                self.cross(i)

    def finish(self):
        place = self.place
        group, last = place.group, place.groups - 1
        sibling_quad = place.sibling[0] % QUAD
        diagonal = 3 - place.quad

        def close(i, unused):
            root = place.groups // 2 - 1 + i % 2
            view = self.own.at[i]
            arrived(self.final.at[sibling_quad, i], self.c_recv.at[0, i], place.sibling)
            arrived(self.final.at[diagonal, i], self.c_recv.at[1, i], place.sibling)

            @pl.when(group != root)
            def up_done():
                sent(view, self.up_send.at[i], place.sibling)

            @pl.when(group == root)
            def kept():
                final = self.final.at[place.quad, i]
                pltpu.make_async_copy(view, final, self.keep.at[i]).wait()

            @pl.when((group <= root) & (group > 0))
            def left_done():
                sent(view, self.fin_send.at[0, i], place.sibling)

            @pl.when((group >= root) & (group < last))
            def right_done():
                sent(view, self.fin_send.at[1, i], place.sibling)

            sent(view, self.x_send.at[i], place.across)
            sent(view, self.c_send.at[0, i], place.sibling)
            sent(view, self.c_send.at[1, i], place.sibling)
            return unused

        lax.fori_loop(0, self.count, close, 0)


def chain_sems(count):
    dma = pltpu.SemaphoreType.DMA
    return [
        dma((2, count)),
        dma((count,)),
        dma((count,)),
        dma((2, count)),
        dma((count,)),
        dma((count,)),
        dma((2, count)),
        dma((2, count)),
        dma((count,)),
    ]


class LayerSum:
    def __init__(self, place, part, half, core_in, left, right, left_in, right_in, last_in, sems):
        self.place, self.part, self.half = place, part, half
        self.core_in, self.left, self.right = core_in, left, right
        self.left_in, self.right_in, self.last_in = left_in, right_in, last_in
        self.sems = sems
        self.cut = left.shape[2]
        self.columns = part.shape[1]

    def rows(self, side, core):
        size = 2 * self.half
        return pl.ds(pl.multiple_of((side * 2 + core) * size, 16), size)

    def start(self):
        place = self.place
        for side in (0, 1):
            view = self.part.at[self.rows(side, 1 - place.core)]
            send(
                view,
                self.core_in.at[side],
                self.sems.at[side],
                self.sems.at[2 + side],
                place.sibling,
            )

    def own_rows(self, tp):
        return pl.ds(pl.multiple_of(tp * self.half, 16), self.half)

    def after_core(self):
        place = self.place
        for side in (0, 1):
            arrived(self.core_in.at[side], self.sems.at[2 + side], place.sibling)
            total = self.part[self.rows(side, place.core), :].astype(F32) + self.core_in[
                side
            ].astype(F32)
            self.left[side] = total[:, : self.cut].astype(BF16)
            self.right[side] = total[:, self.cut :].astype(BF16)

    def cross(self):
        place = self.place
        for side in (0, 1):
            send(
                self.left.at[side, self.own_rows(1 - place.tp)],
                self.left_in.at[side],
                self.sems.at[4 + side],
                self.sems.at[6 + side],
                place.partner,
            )
        send(
            self.right.at[1 - place.side],
            self.right_in,
            self.sems.at[8],
            self.sems.at[9],
            place.across,
        )

    def after_cross(self):
        place = self.place
        mine = self.own_rows(place.tp)
        for side in (0, 1):
            arrived(self.left_in.at[side], self.sems.at[6 + side], place.partner)
            self.left_in[side] = (
                self.left[side, mine, :].astype(F32) + self.left_in[side].astype(F32)
            ).astype(BF16)
        arrived(self.right_in, self.sems.at[9], place.across)
        self.right_in[...] = (
            self.right[place.side].astype(F32) + self.right_in[...].astype(F32)
        ).astype(BF16)
        send(
            self.left_in.at[1 - place.side],
            self.last_in.at[:, : self.cut],
            self.sems.at[10],
            self.sems.at[11],
            place.across,
        )
        send(
            self.right_in.at[self.own_rows(1 - place.tp)],
            self.last_in.at[:, self.cut :],
            self.sems.at[12],
            self.sems.at[13],
            place.partner,
        )

    def result(self):
        place = self.place
        arrived(self.last_in.at[:, : self.cut], self.sems.at[11], place.across)
        arrived(self.last_in.at[:, self.cut :], self.sems.at[13], place.partner)
        mine = jnp.concatenate(
            [self.left_in[place.side], self.right_in[self.own_rows(place.tp), :]], axis=1
        )
        return mine.astype(F32) + self.last_in[...].astype(F32)

    def finish(self):
        place = self.place
        for side in (0, 1):
            sent(self.core_in.at[side], self.sems.at[side], place.sibling)
            sent(self.left_in.at[side], self.sems.at[4 + side], place.partner)
        sent(self.right_in, self.sems.at[8], place.across)
        sent(self.last_in.at[:, : self.cut], self.sems.at[10], place.across)
        sent(self.last_in.at[:, self.cut :], self.sems.at[12], place.partner)


class QuadSum:
    def __init__(self, place, part, own, core_in, x_send, x_in, sems):
        self.place, self.part, self.own = place, part, own
        self.core_in, self.x_send, self.x_in, self.sems = core_in, x_send, x_in, sems

    def start(self):
        place = self.place
        for side in (0, 1):
            send(
                self.part.at[side * 2 + 1 - place.core],
                self.core_in.at[side],
                self.sems.at[side],
                self.sems.at[2 + side],
                place.sibling,
            )

    def total(self, side):
        return self.part[side * 2 + self.place.core].astype(F32) + self.core_in[side].astype(F32)

    def middle(self):
        place = self.place
        for side in (0, 1):
            arrived(self.core_in.at[side], self.sems.at[2 + side], place.sibling)
        self.x_send[...] = self.total(1 - place.side).astype(BF16)
        send(self.x_send, self.x_in, self.sems.at[4], self.sems.at[5], place.across)

    def end(self):
        place = self.place
        arrived(self.x_in, self.sems.at[5], place.across)
        mine = (self.total(place.side) + self.x_in[...].astype(F32)).astype(BF16)
        count, step = self.own.shape[0], self.own.shape[1]
        for i in range(count):
            piece = mine[i * step : (i + 1) * step, :]
            if piece.shape[0]:
                self.own[i, : piece.shape[0], :] = piece
            if piece.shape[0] < step:
                left = step - piece.shape[0]
                self.own[i, piece.shape[0] :, :] = jnp.zeros((left, piece.shape[1]), BF16)

    def finish(self):
        place = self.place
        for side in (0, 1):
            sent(self.core_in.at[side], self.sems.at[side], place.sibling)
        sent(self.x_send, self.sems.at[4], place.across)


class ColumnSum:
    def __init__(self, place, own, incoming, final, sems):
        self.place, self.own, self.incoming, self.final = place, own, incoming, final
        self.rs_send, self.rs_recv, self.ag_send, self.ag_recv = (sems.at[i] for i in range(4))
        self.x_send, self.x_recv, self.c_send, self.c_recv = (sems.at[i] for i in range(4, 8))
        self.d_send, self.d_recv = (sems.at[i] for i in range(8, 10))

    def others(self):
        place = self.place
        for step in range(1, place.groups):
            yield step, (place.group + step) % place.groups

    def start(self):
        place = self.place
        for step, other in self.others():
            back = place.groups - step
            send(
                self.own.at[other],
                self.incoming.at[back],
                self.rs_send.at[step],
                self.rs_recv.at[back],
                place.in_group(other),
            )

    def spread(self, part, view):
        place = self.place
        final = self.final.at[place.quad, part]
        send(view, final, self.x_send.at[part], self.x_recv.at[part], place.across)
        send(view, final, self.c_send.at[part], self.c_recv.at[part], place.sibling)

    def middle(self):
        place = self.place
        mine = self.own.at[place.group]
        total = mine[...].astype(F32)
        for step, other in self.others():
            arrived(self.incoming.at[step], self.rs_recv.at[step], place.sibling)
            total = total + self.incoming[step].astype(F32)
        mine[...] = total.astype(BF16)
        final = self.final.at[place.quad, place.group]
        for step, other in self.others():
            send(
                mine,
                final,
                self.ag_send.at[step],
                self.ag_recv.at[place.group],
                place.in_group(other),
            )
        self.spread(place.group, mine)
        pltpu.make_async_copy(mine, final, self.ag_send.at[0]).start()

    def end(self):
        place = self.place
        for step, other in self.others():
            view = self.final.at[place.quad, other]
            arrived(view, self.ag_recv.at[other], place.sibling)
            self.spread(other, view)

    def cross(self):
        place = self.place
        quad = place.across[0] % QUAD
        for step in range(place.groups):
            part = (place.group + step) % place.groups
            view = self.final.at[quad, part]
            arrived(view, self.x_recv.at[part], place.across)
            send(view, view, self.d_send.at[part], self.d_recv.at[part], place.sibling)

    def finish(self):
        place = self.place
        view = self.own.at[0]
        for part in range(place.groups):
            arrived(view, self.c_recv.at[part], place.sibling)
            arrived(view, self.d_recv.at[part], place.sibling)
            sent(view, self.x_send.at[part], place.across)
            sent(view, self.c_send.at[part], place.sibling)
            sent(view, self.d_send.at[part], place.sibling)
        for step, other in self.others():
            sent(view, self.rs_send.at[step], place.sibling)
            sent(view, self.ag_send.at[step], place.sibling)
        final = self.final.at[place.quad, place.group]
        pltpu.make_async_copy(self.own.at[place.group], final, self.ag_send.at[0]).wait()


def column_parts(groups, rows, columns):
    return (groups, round_up(-(-rows // groups), 16), columns)


def column_sum_scratch(groups, rows, columns):
    parts = column_parts(groups, rows, columns)
    return [
        *quad_sum_scratch(rows, columns),
        pltpu.VMEM(parts, BF16),
        pltpu.VMEM(parts, BF16),
        pltpu.SemaphoreType.DMA((10, groups)),
    ]


def quad_sum_scratch(rows, columns):
    return [
        pltpu.VMEM((QUAD, rows, columns), BF16),
        pltpu.VMEM((2, rows, columns), BF16),
        pltpu.VMEM((rows, columns), BF16),
        pltpu.VMEM((rows, columns), BF16),
        pltpu.SemaphoreType.DMA((6,)),
    ]


def layer_sum_scratch(half, columns):
    cut = columns // LANES // 2 * LANES
    if cut * 2 < columns:
        cut += LANES
    return [
        pltpu.VMEM((2, 2 * half, columns), BF16),
        pltpu.VMEM((2, 2 * half, cut), BF16),
        pltpu.VMEM((2, 2 * half, columns - cut), BF16),
        pltpu.VMEM((2, half, cut), BF16),
        pltpu.VMEM((2 * half, columns - cut), BF16),
        pltpu.VMEM((half, columns), BF16),
        pltpu.SemaphoreType.DMA((14,)),
    ]


def backward_kernel(
    groups,
    slots,
    gate_weight,
    up_weight,
    down_weight,
    cot_all,
    resid_in,
    cot,
    gain,
    out_weight,
    att,
    ot,
    lse,
    qt_in,
    kv_all,
    x_in,
    attn_gain,
    weights_in,
    turns,
    turns_rows,
    layer_out,
    input_grad,
    wide,
    tall,
    outs,
    ins_q,
    ins_kv,
    gains,
    biases,
    *scratch,
):
    place = Place(groups)
    wide_own, tall_own, wide_up, tall_up = scratch[0:4]
    wide_root, tall_root = scratch[4:6]
    scratch = scratch[2:]
    wide_sems, tall_sems = scratch[4:13], scratch[13:22]
    sum_g, sum_m = scratch[22:29], scratch[29:36]
    branch, qt, dot_t, q_pad, do_pad, dkv = scratch[36:42]
    sib_send, sib_in, side_send, side_in, z_send, z_in = scratch[42:48]
    kv_sems, pair_sems = scratch[48:50]
    dq_out, dkv_out, resid_grad = scratch[50:53]
    turn_send, turn_in, gain_in, bias_in, gain_z, bias_z, vector_sems = scratch[53:60]
    sum_o, sum_q, sum_kv = scratch[60:68], scratch[68:76], scratch[76:84]
    rows = att.shape[0]
    half = rows // 2
    span = 2 * rows
    width, queries = qt_in.shape
    parts = 2 if groups <= 4 else 8
    block = queries // parts
    chunks = 2 * groups
    heads = out_weight.shape[0] // HEAD_DIM
    my_rows = pl.ds(pl.multiple_of(place.tp * half, 16), half)
    other_rows = pl.ds(pl.multiple_of((1 - place.tp) * half, 16), half)

    tall_sum = ChainSum(place, tall_own, tall_up, tall_root, tall, tall_sems)
    wide_sum = ChainSum(place, wide_own, wide_up, wide_root, wide, wide_sems)
    gate_piece, up_piece, down_piece, normed_all, mixed, grad_gu, grad_part, mlp_part = scratch[84:92]
    gather_sems = scratch[92:95]
    features = resid_in.shape[1]
    piece = gate_piece.shape[1]
    keep = gate_weight.shape[1] - (QUAD - 1) * piece

    def load_weights(size, quad):
        columns = pl.ds(pl.multiple_of(quad * piece, LANES), size)
        pairs = (
            (gate_weight.at[:, columns], gate_piece.at[:, pl.ds(0, size)]),
            (up_weight.at[:, columns], up_piece.at[:, pl.ds(0, size)]),
            (down_weight.at[columns], down_piece.at[pl.ds(0, size)]),
        )
        return [
            pltpu.make_async_copy(src, dst, pair_sems.at[4 + number])
            for number, (src, dst) in enumerate(pairs)
        ]

    last_quad = QUAD - 1

    @pl.when(place.quad < last_quad)
    def whole_piece():
        for copy in load_weights(piece, place.quad):
            copy.start()

    @pl.when(place.quad == last_quad)
    def last_piece():
        for copy in load_weights(keep, last_quad):
            copy.start()
        if keep < piece:
            gate_piece[:, keep:] = jnp.zeros((features, piece - keep), BF16)
            up_piece[:, keep:] = jnp.zeros((features, piece - keep), BF16)
            down_piece[keep:, :] = jnp.zeros((piece - keep, features), BF16)

    grad_sum = LayerSum(place, grad_part, half, *sum_g)
    mlp_sum = LayerSum(place, mlp_part, half, *sum_m)

    def quad_and_column(final, refs):
        quad = QuadSum(place, refs[0], refs[5], *refs[1:5])
        return quad, ColumnSum(place, refs[5], refs[6], final, refs[7])

    outs_quad, outs_sum = quad_and_column(outs, sum_o)
    q_quad, q_sum = quad_and_column(ins_q, sum_q)
    kv_quad, kv_sum = quad_and_column(ins_kv, sum_kv)
    tall_steps = tall_sum.count

    def chain_step(number):
        tall_sum.step(number)
        wide_sum.step(number - tall_steps)

    def chain_steps(first, count):
        def one(number, unused):
            chain_step(number)
            return unused

        lax.fori_loop(first, first + count, one, 0)
        return first + count

    all_steps = tall_steps + wide_sum.total_steps()

    gather = LayerGather(place, normed_all, half, *gather_sems)
    resid = resid_in[...]
    factor = lax.rsqrt(jnp.mean(resid * resid, axis=-1, keepdims=True) + EPSILON)
    own_block = place.quad * 2 + place.tp
    normed_all[pl.ds(pl.multiple_of(own_block * half, 16), half), :] = (
        resid * factor * gain[...]
    ).astype(BF16)
    meet(place, True)
    gather.start()

    @pl.when(place.quad < last_quad)
    def whole_loaded():
        for copy in load_weights(piece, place.quad):
            copy.wait()

    @pl.when(place.quad == last_quad)
    def last_loaded():
        for copy in load_weights(keep, last_quad):
            copy.wait()

    def feed(number, unused):
        @pl.when(number == 1)
        def second():
            gather.from_sibling(0, 0)

        @pl.when(number == 2)
        def third():
            gather.from_partner()
            gather.from_across()

        @pl.when(number == 4)
        def fifth():
            gather.from_sibling(0, 1)

        @pl.when(number == 5)
        def sixth():
            gather.from_sibling(1, 0)
            gather.diagonal()

        @pl.when(number == 7)
        def eighth():
            gather.from_sibling(1, 1)

        def flip(value, numbers):
            turned = functools.reduce(lambda x, y: x | y, [number == i for i in numbers])
            return jnp.where(turned, 1 - value, value)

        side = flip(place.side, (3, 5, 6, 7))
        core = flip(place.core, (1, 4, 5, 7))
        tp = flip(place.tp, (2, 4, 6, 7))
        at_rows = pl.ds(pl.multiple_of(((side * 2 + core) * 2 + tp) * half, 16), half)
        here = normed_all[at_rows, :]
        gate = nn(here, gate_piece[...])
        upward = nn(here, up_piece[...])
        sigmoid = jax.nn.sigmoid(gate)
        silu = gate * sigmoid
        mixed[at_rows, :] = (silu * upward).astype(BF16)
        grad_gu[at_rows, :piece] = (upward * sigmoid * (1.0 + gate * (1.0 - sigmoid))).astype(BF16)
        grad_gu[at_rows, piece:] = silu.astype(BF16)
        return unused

    lax.fori_loop(0, 8, feed, 0)
    tall_own[...] = tn(mixed[...], cot_all[...]).astype(BF16).reshape(tall_own.shape)
    done = chain_steps(0, SHARE[0])

    def feed_back(number, unused):
        core = jnp.where(number < 2, 1 - place.core, place.core)
        at_rows = pl.ds(pl.multiple_of((number % 2 * 2 + core) * rows, 16), rows)
        grad_mixed = nt(cot_all[at_rows, :], down_piece[...])
        grad_gate = (grad_mixed * grad_gu[at_rows, :piece].astype(F32)).astype(BF16)
        grad_upward = (grad_mixed * grad_gu[at_rows, piece:].astype(F32)).astype(BF16)
        grad_gu[at_rows, :piece] = grad_gate
        grad_gu[at_rows, piece:] = grad_upward
        grad_part[at_rows, :] = (
            nt(grad_gate, gate_piece[...]) + nt(grad_upward, up_piece[...])
        ).astype(BF16)
        mlp_part[at_rows, :] = nn(mixed[at_rows, :], down_piece[...]).astype(BF16)
        chain_step(number + SHARE[0])
        return unused

    done += 4
    lax.fori_loop(0, 2, feed_back, 0)
    grad_sum.start()
    lax.fori_loop(2, 4, feed_back, 0)
    grad_sum.after_core()
    grad_sum.cross()
    both = tn(normed_all[...], grad_gu[...])
    count = wide_own.shape[0] // 2
    for number in range(2):
        wide_own[number * count : (number + 1) * count] = (
            both[:, number * piece : (number + 1) * piece]
            .astype(BF16)
            .reshape(count, *wide_own.shape[1:])
        )
    gather.finish(True)

    qt[...] = qt_in[...]
    at = HEAD_DIM + slots
    qt[at : at + 16, :] = split_rows(-lse[...], 0, 16)
    natural_q = jnp.transpose(qt_in[0:HEAD_DIM, :].astype(F32)).astype(BF16)
    q_pad[...] = jnp.concatenate([natural_q, jnp.zeros_like(natural_q)], axis=1)

    mlp_sum.start()
    done = chain_steps(done, SHARE[1])
    grad_sum.after_cross()
    done = chain_steps(done, SHARE[2])

    normed = resid * factor
    grad_normed = grad_sum.result()
    gains[:, features:] = jnp.sum(grad_normed * normed, axis=0, keepdims=True)
    weighted = grad_normed * gain[...]
    inner = jnp.mean(weighted * normed, axis=-1, keepdims=True)
    grad_resid = cot[my_rows, :].astype(F32) + factor * (weighted - normed * inner)
    resid_grad[...] = grad_resid
    branch[my_rows, :] = grad_resid.astype(BF16)
    send(
        branch.at[my_rows],
        branch.at[my_rows],
        pair_sems.at[0],
        pair_sems.at[1],
        place.partner,
    )
    mlp_sum.after_core()
    mlp_sum.cross()
    done = chain_steps(done, SHARE[3])
    arrived(branch.at[other_rows], pair_sems.at[1], place.partner)

    grads = branch[...]
    outs_part = sum_o[0]
    outs_part[...] = tn(att[...], grads).astype(BF16).reshape(outs_part.shape)
    outs_quad.start()
    grad_att = nt(grads, out_weight[...]).astype(BF16)
    half_width = queries // 2
    filler = jnp.zeros((half_width - heads * half, HEAD_DIM), BF16)
    stacked = jnp.concatenate(
        [
            part
            for number in range(2)
            for part in (
                *(
                    grad_att[
                        number * half : (number + 1) * half,
                        head * HEAD_DIM : (head + 1) * HEAD_DIM,
                    ]
                    for head in range(heads)
                ),
                filler,
            )
        ],
        axis=0,
    )
    do_pad[...] = jnp.concatenate([jnp.zeros_like(stacked), stacked], axis=1)
    turned = jnp.transpose(stacked.astype(F32))
    delta = jnp.sum(turned * ot[...], axis=0, keepdims=True)
    dot_t[0:HEAD_DIM, :] = split_rows(-delta, 0, HEAD_DIM)
    dot_t[HEAD_DIM:, :] = turned.astype(BF16)
    done = chain_steps(done, SHARE[4])
    outs_quad.middle()

    def write_layer():
        layer_out[my_rows, :] = (resid_in[...] + mlp_sum.result()).astype(BF16)
        send(
            layer_out.at[my_rows],
            layer_out.at[my_rows],
            pair_sems.at[2],
            pair_sems.at[3],
            place.partner,
        )

    dq_out[...] = jnp.zeros_like(dq_out)

    def chunk_place(number):
        far = 1 - number % 2
        group = (place.group + 1 + number // 2) % groups
        side = place.side + far * (1 - 2 * place.side)
        return group, side

    lane = lax.broadcasted_iota(jnp.int32, (1, LANES), 1)
    ones = jnp.where(lane < 3, 1.0, 0.0).astype(BF16)

    def attend_back(number, slot, own_chip=False):
        group, side = chunk_place(number)
        chip = group * 2 + side
        at_rows = pl.ds(pl.multiple_of(chip * span, 16), span)
        kv = kv_all[at_rows, :]
        keys = extended_keys(kv, chip, rows, width, slots)
        values = jnp.where(lane >= HEAD_DIM, kv, jnp.broadcast_to(ones, kv.shape))
        for part in range(parts):
            lanes = slice(part * block, (part + 1) * block)
            score = nn(keys, qt[:, lanes])
            if own_chip:
                first = part * block
                number_of_half = first // half_width
                score = hide_later(score, place, rows, number_of_half, first % half_width)
            weights = jnp.exp(score)
            change = nn(values, dot_t[:, lanes])
            low = (weights * change).astype(BF16)
            total = nn(weights.astype(BF16), do_pad[lanes, :]) + nn(low, q_pad[lanes, :])
            if part == 0:
                dkv[slot] = total
            else:
                dkv[slot] += total
            dq_out[:, lanes] += tn(kv[:, :HEAD_DIM], low)

    def hand_over(number, slot):
        other = pl.ds(pl.multiple_of((1 - place.core) * rows, 16), rows)

        @pl.when(number >= 2)
        def free_again():
            sent(sib_send.at[slot], kv_sems.at[0, number - 2], place.sibling)

        sib_send[slot] = dkv[slot, other, :].astype(BF16)
        send(
            sib_send.at[slot],
            sib_in.at[number],
            kv_sems.at[0, number],
            kv_sems.at[1, number],
            place.sibling,
        )

    def take_over(number, near, own_group=False):
        group, side = chunk_place(number)
        step = number // 2
        arrived(sib_in.at[number], kv_sems.at[1, number], place.sibling)
        mine = pl.ds(pl.multiple_of(place.core * rows, 16), rows)
        total = dkv[1 if near else 0, mine, :] + sib_in[number].astype(F32)
        if not near:
            ring = step % 2

            @pl.when(step >= 2)
            def side_free():
                sent(side_send.at[0], kv_sems.at[2, step - 2], place.across)

            side_send[ring] = total.astype(BF16)
            send(
                side_send.at[ring],
                side_in.at[step],
                kv_sems.at[2, step],
                kv_sems.at[3, step],
                place.across,
            )
            return
        arrived(side_in.at[step], kv_sems.at[3, step], place.across)
        total = total + side_in[step].astype(F32)
        if own_group:
            dkv_out[...] = total
            return
        ring = step % 2

        @pl.when(step >= 2)
        def column_free():
            sent(z_send.at[0], kv_sems.at[4, step - 2], place.sibling)

        z_send[ring] = total.astype(BF16)
        back = groups - 2 - step
        send(
            z_send.at[ring],
            z_in.at[back],
            kv_sems.at[4, step],
            kv_sems.at[5, back],
            place.in_group(group),
        )

    each = 1

    def pair(step, unused):
        attend_back(2 * step, 0)
        hand_over(2 * step, 0)
        chain_steps(done + 2 * each * step, each)

        @pl.when(step > 0)
        def last_near():
            take_over(2 * step - 1, True)

        attend_back(2 * step + 1, 1)
        hand_over(2 * step + 1, 1)
        take_over(2 * step, False)
        chain_steps(done + 2 * each * step + each, each)

        @pl.when(step == 0)
        def outs_ready():
            mlp_sum.after_cross()
            outs_quad.end()
            outs_sum.start()

        @pl.when(step == 1)
        def layer_ready():
            write_layer()
            outs_sum.middle()

        return unused

    lax.fori_loop(0, groups - 1, pair, 0)
    outs_sum.end()
    done += 2 * each * (groups - 1)
    attend_back(chunks - 2, 0)
    hand_over(chunks - 2, 0)
    done = chain_steps(done, each)
    if groups > 1:
        take_over(chunks - 3, True)
    attend_back(chunks - 1, 1, True)
    hand_over(chunks - 1, 1)
    take_over(chunks - 2, False)
    done = chain_steps(done, SHARE[5])

    quarter = HEAD_DIM // 2
    raw = dq_out[...] * HEAD_DIM**-0.5
    one, two = raw[:quarter, :], raw[quarter:, :]
    cos, sin = turns[:quarter, :], turns[quarter:, :]
    turned = jnp.concatenate([one * cos + two * sin, two * cos - one * sin], axis=0)
    natural = jnp.transpose(turned).astype(BF16)
    grad_query = jnp.concatenate(
        [
            jnp.concatenate(
                [
                    natural[start + head * half : start + (head + 1) * half, :]
                    for head in range(heads)
                ],
                axis=1,
            )
            for start in (0, half_width)
        ],
        axis=0,
    )
    x_all = x_in[...].astype(F32)
    factor_all = lax.rsqrt(jnp.mean(x_all * x_all, axis=-1, keepdims=True) + EPSILON)
    normed_attn = (x_all * factor_all * attn_gain[...]).astype(BF16)
    wide_q = grad_query.shape[1]
    q_part = sum_q[0]
    q_part[...] = tn(grad_query, normed_attn).astype(BF16).reshape(q_part.shape)
    q_quad.start()
    turn_send[...] = nn(grad_query, weights_in[:wide_q, :])
    biases[...] = jnp.zeros_like(biases)
    biases[:, :wide_q] = jnp.sum(grad_query.astype(F32), axis=0, keepdims=True)
    done = chain_steps(done, SHARE[11])
    take_over(chunks - 1, True, True)
    q_quad.middle()
    outs_sum.cross()
    done = chain_steps(done, SHARE[6])
    for step in range(groups - 1):
        arrived(z_in.at[step], kv_sems.at[5, step], place.sibling)
        dkv_out[...] += z_in[step].astype(F32)
    turned = jnp.transpose(dkv_out[...])
    one, two = turned[:quarter, :], turned[quarter:HEAD_DIM, :]
    cos, sin = turns_rows[:quarter, :], turns_rows[quarter:, :]
    turned = jnp.concatenate(
        [one * cos + two * sin, two * cos - one * sin, turned[HEAD_DIM:, :]], axis=0
    )
    grad_kv = jnp.transpose(turned).astype(BF16)
    kv_part = sum_kv[0]
    kv_part[...] = tn(grad_kv, normed_attn).astype(BF16).reshape(kv_part.shape)
    kv_quad.start()
    turn_send[...] += nn(grad_kv, weights_in[wide_q:, :])
    turn_in[0] = turn_send[other_rows, :].astype(BF16)
    send(turn_in.at[0], turn_in.at[1], vector_sems.at[0], vector_sems.at[1], place.partner)
    biases[:, wide_q : wide_q + LANES] = jnp.sum(grad_kv.astype(F32), axis=0, keepdims=True)
    done = chain_steps(done, SHARE[12])
    kv_quad.middle()
    q_quad.end()
    q_sum.start()
    done = chain_steps(done, SHARE[7])
    kv_quad.end()
    kv_sum.start()
    x_half = x_in[my_rows, :].astype(F32)
    factor = lax.rsqrt(jnp.mean(x_half * x_half, axis=-1, keepdims=True) + EPSILON)
    normed = x_half * factor
    done = chain_steps(done, SHARE[13])
    arrived(turn_in.at[1], vector_sems.at[1], place.partner)
    grad_normed = turn_send[my_rows, :] + turn_in[1].astype(F32)
    gains[:, :features] = jnp.sum(grad_normed * normed, axis=0, keepdims=True)
    weighted = grad_normed * attn_gain[...]
    mean = jnp.mean(weighted * normed, axis=-1, keepdims=True)
    input_grad[my_rows, :] = (
        resid_grad[...] + factor * (weighted - normed * mean)
    ).astype(BF16)

    def vectors(hop, device, with_biases):
        send(gains, gain_in.at[hop], vector_sems.at[4 + 4 * hop], vector_sems.at[5 + 4 * hop], device)
        if with_biases:
            send(
                biases,
                bias_in.at[hop],
                vector_sems.at[6 + 4 * hop],
                vector_sems.at[7 + 4 * hop],
                device,
            )

    def vectors_done(hop, device, with_biases):
        arrived(gain_in.at[hop], vector_sems.at[5 + 4 * hop], device)
        sent(gains, vector_sems.at[4 + 4 * hop], device)
        gains[...] += gain_in[hop]
        if with_biases:
            arrived(bias_in.at[hop], vector_sems.at[7 + 4 * hop], device)
            sent(biases, vector_sems.at[6 + 4 * hop], device)
            biases[...] += bias_in[hop]

    hops = ((place.partner, False), (place.sibling, True), (place.across, True))
    vectors(0, *hops[0])
    send(
        input_grad.at[my_rows],
        input_grad.at[my_rows],
        vector_sems.at[2],
        vector_sems.at[3],
        place.partner,
    )
    done = chain_steps(done, SHARE[14])
    q_sum.middle()
    vectors_done(0, *hops[0])
    vectors(1, *hops[1])
    kv_sum.middle()
    done = chain_steps(done, SHARE[8])
    vectors_done(1, *hops[1])
    vectors(2, *hops[2])
    done = chain_steps(done, SHARE[9])
    vectors_done(2, *hops[2])
    gain_z[place.group] = gains[...]
    bias_z[place.group] = biases[...]
    base = 16
    for step in range(1, groups):
        other = place.in_group((place.group + step) % groups)
        for number, ref in enumerate((gain_z, bias_z)):
            send(
                ref.at[place.group],
                ref.at[place.group],
                vector_sems.at[base + 4 * step + 2 * number],
                vector_sems.at[base + 4 * (groups - step) + 2 * number + 1],
                other,
            )
    q_sum.end()
    kv_sum.end()
    done = chain_steps(done, SHARE[10])
    q_sum.cross()
    kv_sum.cross()
    for step in range(1, groups):
        other = (place.group + groups - step) % groups
        for number, ref in enumerate((gain_z, bias_z)):
            arrived(
                ref.at[other],
                vector_sems.at[base + 4 * (groups - step) + 2 * number + 1],
                place.sibling,
            )
            sent(
                ref.at[place.group],
                vector_sems.at[base + 4 * step + 2 * number],
                place.sibling,
            )
    gains[...] = jnp.sum(gain_z[...], axis=0)
    biases[...] = jnp.sum(bias_z[...], axis=0)

    def last(number, unused):
        chain_step(number)
        return unused

    lax.fori_loop(done, all_steps, last, 0)

    arrived(input_grad.at[other_rows], vector_sems.at[3], place.partner)
    sent(input_grad.at[my_rows], vector_sems.at[2], place.partner)
    sent(turn_in.at[0], vector_sems.at[0], place.partner)
    for part in (outs_quad, q_quad, kv_quad, outs_sum, q_sum, kv_sum):
        part.finish()
    arrived(layer_out.at[other_rows], pair_sems.at[3], place.partner)
    sent(branch.at[my_rows], pair_sems.at[0], place.partner)
    sent(branch.at[my_rows], pair_sems.at[2], place.partner)
    grad_sum.finish()
    mlp_sum.finish()
    tall_sum.finish()
    wide_sum.finish()
    for number in range(chunks - 2, chunks):
        sent(sib_send.at[0], kv_sems.at[0, number], place.sibling)
    for step in range(groups - 2, groups):
        sent(side_send.at[0], kv_sems.at[2, step], place.across)
    for step in range(groups - 3, groups - 1):
        sent(z_send.at[0], kv_sems.at[4, step], place.sibling)


def vmem_specs(count):
    return [pl.BlockSpec(memory_space=pltpu.VMEM)] * count


def params(collective):
    return pltpu.CompilerParams(
        collective_id=collective, has_side_effects=True, vmem_limit_bytes=VMEM_LIMIT
    )


def attend(groups, slots, kv_own, qt, x_in, out_weight, cot):
    rows, features = x_in.shape
    half = rows // 2
    total = groups * QUAD * rows
    width, queries = qt.shape
    dma = pltpu.SemaphoreType.DMA
    shape = jax.ShapeDtypeStruct
    return pl.pallas_call(
        functools.partial(attend_kernel, groups, slots),
        out_shape=[
            shape((total, LANES), BF16),
            shape((QUAD * rows, features), BF16),
            shape((half, features), F32),
            shape((rows, out_weight.shape[0]), BF16),
            shape((HEAD_DIM, queries), F32),
            shape((1, queries), F32),
        ],
        in_specs=vmem_specs(5),
        out_specs=vmem_specs(6),
        scratch_shapes=[
            pltpu.VMEM((2, 2 * rows, queries // 2), F32),
            pltpu.VMEM((1, queries), F32),
            pltpu.VMEM((1, queries), F32),
            pltpu.VMEM((half, features), BF16),
            pltpu.VMEM((half, features), BF16),
            dma((groups * QUAD,)),
            dma((groups,)),
            dma((groups,)),
            dma((2 * groups,)),
            dma((8,)),
            dma((2,)),
            dma((8,)),
            dma((2,)),
        ],
        compiler_params=params(1),
        name="attend",
    )(kv_own, qt, x_in, out_weight, cot)


def backward(groups, slots, operands):
    (gate_weight, _, _, cot_all, resid, cot, gain, out_weight, att, ot, lse, qt, kv_all) = operands[
        :13
    ]
    weights_in = operands[15]
    rows, inner = att.shape
    half = rows // 2
    features, hidden = gate_weight.shape
    piece = piece_width(hidden)
    layer_rows = QUAD * rows
    width, queries = qt.shape
    chunks = 2 * groups
    both = round_up(weights_in.shape[0], LANES)
    dma = pltpu.SemaphoreType.DMA
    shape = jax.ShapeDtypeStruct
    pass_shape = (rows, LANES)
    wide = jax.ShapeDtypeStruct((2 * features // WIDE_ROWS, WIDE_ROWS, piece), BF16)
    tall = jax.ShapeDtypeStruct((piece // TALL_ROWS, TALL_ROWS, features), BF16)
    outs = (inner // QUAD, features)
    ins_q = (inner // QUAD, features)
    ins_kv = (LANES // QUAD, features)
    return pl.pallas_call(
        functools.partial(backward_kernel, groups, slots),
        out_shape=[
            shape((rows, features), BF16),
            shape((rows, features), BF16),
            shape((QUAD, *wide.shape), BF16),
            shape((QUAD, *tall.shape), BF16),
            *(shape((QUAD, *column_parts(groups, *dims)), BF16) for dims in (outs, ins_q, ins_kv)),
            shape((1, 2 * features), F32),
            shape((1, both), F32),
        ],
        in_specs=[pl.BlockSpec(memory_space=pl.ANY)] * 3 + vmem_specs(15),
        out_specs=vmem_specs(2) + [pl.BlockSpec(memory_space=pl.ANY)] * 5 + vmem_specs(2),
        scratch_shapes=[
            pltpu.VMEM(wide.shape, BF16),
            pltpu.VMEM(tall.shape, BF16),
            pltpu.VMEM(wide.shape, BF16),
            pltpu.VMEM(tall.shape, BF16),
            pltpu.VMEM((round_up(wide.shape[0], 2) // 2, *wide.shape[1:]), BF16),
            pltpu.VMEM((round_up(tall.shape[0], 2) // 2, *tall.shape[1:]), BF16),
            *chain_sems(wide.shape[0]),
            *chain_sems(tall.shape[0]),
            *layer_sum_scratch(half, features),
            *layer_sum_scratch(half, features),
            pltpu.VMEM((rows, features), BF16),
            pltpu.VMEM((width, queries), BF16),
            pltpu.VMEM((LANES, queries), BF16),
            pltpu.VMEM((queries, LANES), BF16),
            pltpu.VMEM((queries, LANES), BF16),
            pltpu.VMEM((2, 2 * rows, LANES), F32),
            pltpu.VMEM((2, *pass_shape), BF16),
            pltpu.VMEM((chunks, *pass_shape), BF16),
            pltpu.VMEM((2, *pass_shape), BF16),
            pltpu.VMEM((groups, *pass_shape), BF16),
            pltpu.VMEM((2, *pass_shape), BF16),
            pltpu.VMEM((groups, *pass_shape), BF16),
            dma((6, chunks)),
            dma((7,)),
            pltpu.VMEM((HEAD_DIM, queries), F32),
            pltpu.VMEM((rows, LANES), F32),
            pltpu.VMEM((half, features), F32),
            pltpu.VMEM((rows, features), F32),
            pltpu.VMEM((2, half, features), BF16),
            pltpu.VMEM((3, 1, 2 * features), F32),
            pltpu.VMEM((3, 1, both), F32),
            pltpu.VMEM((groups, 1, 2 * features), F32),
            pltpu.VMEM((groups, 1, both), F32),
            dma((16 + 4 * groups + 4,)),
            *column_sum_scratch(groups, *outs),
            *column_sum_scratch(groups, *ins_q),
            *column_sum_scratch(groups, *ins_kv),
            pltpu.VMEM((features, piece), BF16),
            pltpu.VMEM((features, piece), BF16),
            pltpu.VMEM((piece, features), BF16),
            pltpu.VMEM((layer_rows, features), BF16),
            pltpu.VMEM((layer_rows, piece), BF16),
            pltpu.VMEM((layer_rows, 2 * piece), BF16),
            pltpu.VMEM((layer_rows, features), BF16),
            pltpu.VMEM((layer_rows, features), BF16),
            dma((8,)),
            dma((2,)),
            dma((8,)),
        ],
        compiler_params=params(2),
        name="backward",
    )(*operands)


def unfold_kernel(keep, gate_in, up_in, gate, up):
    for src, dst in ((gate_in, gate), (up_in, up)):
        size = src.shape[2]
        for number in range(QUAD):
            count = size if number < QUAD - 1 else keep
            dst[:, number * size : number * size + count] = src[number, :, :count].astype(F32)


def unfold(parts, features, hidden):
    piece = parts.shape[2]
    blocks = features // WIDE_ROWS
    block = (QUAD, WIDE_ROWS, piece)
    out = pl.BlockSpec((WIDE_ROWS, hidden), lambda i: (i, 0))
    return pl.pallas_call(
        functools.partial(unfold_kernel, hidden - (QUAD - 1) * piece),
        grid=(blocks,),
        out_shape=[jax.ShapeDtypeStruct((features, hidden), F32)] * 2,
        in_specs=[
            pl.BlockSpec(block, lambda i: (0, i, 0)),
            pl.BlockSpec(block, lambda i: (0, i + blocks, 0)),
        ],
        out_specs=[out, out],
        compiler_params=pltpu.CompilerParams(vmem_limit_bytes=VMEM_LIMIT),
        name="unfold",
    )(parts, parts)


def rope_tables(positions, head_size):
    half_size = head_size // 2
    exponent = jnp.arange(half_size, dtype=F32) * (2.0 / head_size)
    frequency = jnp.power(ROPE_BASE, -exponent)
    angle = positions.astype(F32)[:, None] * frequency[None, :]
    return (jnp.cos(angle)[:, None, :], jnp.sin(angle)[:, None, :])


def rotate(values, cosine, sine):
    half_size = values.shape[-1] // 2
    first = values[..., :half_size]
    second = values[..., half_size:]
    return jnp.concatenate(
        [first * cosine - second * sine, second * cosine + first * sine], axis=-1
    )


def piece_width(hidden):
    return round_up(hidden // LANES, QUAD) // QUAD * LANES


def per_device(
    groups,
    layer_input,
    block_order,
    attn_gain,
    query_weight,
    query_bias,
    key_weight,
    key_bias,
    value_weight,
    value_bias,
    out_weight,
    mlp_gain,
    gate_weight,
    up_weight,
    down_weight,
    out_cotangent,
):
    rows, features = layer_input.shape
    block_rows = rows // 2
    slots = block_order.shape[0]
    hidden = gate_weight.shape[1]
    heads = query_weight.shape[1] // HEAD_DIM
    piece = piece_width(hidden)
    half_width = round_up(heads * block_rows, 2 * LANES)
    queries = 2 * half_width
    width = round_up(HEAD_DIM + slots + 16, LANES)
    scale = HEAD_DIM ** (-0.5)
    seq_index = lax.axis_index("seq")
    own_slots = lax.dynamic_slice_in_dim(block_order, 2 * seq_index, 2)
    steps_in = jnp.arange(block_rows, dtype=jnp.int32)
    own_places = (own_slots[:, None] * block_rows + steps_in[None, :]).reshape(-1)
    cosine, sine = rope_tables(own_places, HEAD_DIM)
    inputs = layer_input.astype(F32)
    factor_first = lax.rsqrt(jnp.mean(inputs * inputs, axis=-1, keepdims=True) + EPSILON)
    normed_first = inputs * factor_first
    normed_attn = (normed_first * attn_gain).astype(BF16)
    query_rows = (
        jnp.dot(normed_attn, query_weight, preferred_element_type=F32) + query_bias
    ).reshape(rows, heads, HEAD_DIM)
    key_rows = (jnp.dot(normed_attn, key_weight, preferred_element_type=F32) + key_bias).reshape(
        rows, 1, HEAD_DIM
    )
    value_rows = (
        jnp.dot(normed_attn, value_weight, preferred_element_type=F32) + value_bias
    ).astype(BF16)
    query_rot = rotate(query_rows, cosine, sine).astype(BF16)
    key_rot = rotate(key_rows, cosine, sine).astype(BF16).reshape(rows, HEAD_DIM)
    kv_own = jnp.concatenate([key_rot, value_rows], axis=1)
    padding = ((0, 0), (0, 0), (0, half_width - heads * block_rows))

    def by_columns(values):
        count = values.shape[-1]
        values = values.reshape(2, block_rows, heads, count)
        values = jnp.transpose(values, (3, 0, 2, 1)).reshape(count, 2, heads * block_rows)
        return jnp.pad(values, padding).reshape(count, queries)

    query_t = by_columns(query_rot * jnp.asarray(scale, BF16))
    later = block_order[:, None] > own_slots[None, :]
    bias = jnp.where(later, NEGATIVE, 0.0).astype(BF16)
    bias = jnp.broadcast_to(bias[:, :, None], (slots, 2, half_width)).reshape(slots, queries)
    qt = jnp.concatenate(
        [query_t, bias, jnp.zeros((width - HEAD_DIM - slots, queries), BF16)], axis=0
    )
    gain_row = mlp_gain[None, :]

    kv_all, cot_all, resid, att, ot, lse = attend(
        groups, slots, kv_own, qt, layer_input, out_weight, out_cotangent
    )

    weights_in = jnp.concatenate(
        [jnp.transpose(w) for w in (query_weight, key_weight, value_weight)], axis=0
    )
    turns_rows = jnp.concatenate([cosine[:, 0, :], sine[:, 0, :]], axis=1)
    tables = (
        by_columns(jnp.broadcast_to(turns_rows[:, None, :], (rows, heads, HEAD_DIM))),
        jnp.transpose(turns_rows),
    )
    layer_output, input_grad, wide_sum, tall_sum, outs, ins_q, ins_kv, gains, biases = backward(
        groups,
        slots,
        (
            gate_weight, up_weight, down_weight, cot_all, resid, out_cotangent, gain_row, out_weight,
            att, ot, lse, qt, kv_all, layer_input, attn_gain[None, :], weights_in, *tables,
        ),
    )

    gate_sum, up_sum = unfold(wide_sum.reshape(QUAD, 2 * features, piece), features, hidden)
    tall_sum = tall_sum.reshape(QUAD, piece, features)
    down_sum = tall_sum.reshape(QUAD * piece, features)[:hidden].astype(F32)

    query_width = heads * HEAD_DIM

    def quarters(parts, row_count):
        parts = parts.reshape(QUAD, -1, parts.shape[-1])[:, : row_count // QUAD]
        return parts.reshape(row_count, -1).astype(F32)

    out_grad = quarters(outs, query_width)
    query_grad = jnp.transpose(quarters(ins_q, query_width))
    key_value = quarters(ins_kv, 2 * HEAD_DIM)
    key_grad = jnp.transpose(key_value[:HEAD_DIM])
    value_grad = jnp.transpose(key_value[HEAD_DIM:])
    attn_gain_grad, mlp_gain_grad = gains[0, :features], gains[0, features:]
    query_bias_grad = biases[0, :query_width]
    key_bias_grad = biases[0, query_width : query_width + HEAD_DIM]
    value_bias_grad = biases[0, query_width + HEAD_DIM : query_width + 2 * HEAD_DIM]
    return (
        layer_output,
        input_grad,
        attn_gain_grad,
        query_grad,
        query_bias_grad,
        key_grad,
        key_bias_grad,
        value_grad,
        value_bias_grad,
        out_grad,
        mlp_gain_grad,
        gate_sum,
        up_sum,
        down_sum,
    )


def solution(mesh):
    groups = mesh.shape["seq"] // QUAD
    by_rows, columns, rows, vector, whole = (
        P("seq", None),
        P(None, "tp"),
        P("tp", None),
        P("tp"),
        P(),
    )
    return jax.shard_map(
        functools.partial(per_device, groups),
        mesh=mesh,
        in_specs=(
            by_rows, whole, whole, columns, vector, columns, vector, columns, vector, rows,
            whole, columns, columns, rows, by_rows,
        ),
        out_specs=(
            by_rows, by_rows, whole, columns, vector, columns, vector, columns, vector, rows,
            whole, columns, columns, rows,
        ),
        check_vma=False,
    )
```
